32 devices in a mesh: dp: 8 (over z, x), tensor: 4 (over y, core).
Axes of the slice: x: 2, y: 2, z: 4, core: 2. Of those that a mesh axis runs over, the one named last changes fastest.
Arguments:
- tokens: bfloat16 [4096, 768], P(('dp', 'tensor')), may hold values from -6 to 6
- cotangent: bfloat16 [4096, 768], P(('dp', 'tensor')), may hold values from -6 to 6
- w_qkv: bfloat16 [768, 3, 768], P('dp', None, 'tensor'), may hold values from -0.21875 to 0.21875
- w_out_attn: bfloat16 [768, 768], P('dp', 'tensor'), may hold values from -3 to 3
- w_router: bfloat16 [768, 4], P('dp'), may hold values from -0.109375 to 0.109375
- w_in: bfloat16 [768, 4, 3072], P('dp', None, 'tensor'), may hold values from -0.21875 to 0.21875
- w_out: bfloat16 [768, 4, 3072], P('dp', None, 'tensor'), may hold values from -0.875 to 0.875
- norm1_gain: bfloat16 [768], P('dp'), may hold values from 0.099609375 to 1.8984375
- norm2_gain: bfloat16 [768], P('dp'), may hold values from 0.099609375 to 1.8984375
- bias_table: bfloat16 [384], P('dp'), may hold values from -4 to 4
- seq_length: int32 [8], P('dp'), may hold values from 385 to 512, as said below
- expert_ids: int32 [4096], P('dp'), may hold values from 0 to 3
- expert_slots: int32 [4096], P('dp'), may hold values from -1 to 127, as said below
- buckets: int32 [1023], replicated, may hold values from 0 to 31
Outputs:
- layer_out: bfloat16 [4096, 768], P(('dp', 'tensor'))
- grad_tokens: float32 [4096, 768], P(('dp', 'tensor'))
- grad_w_qkv: float32 [768, 3, 768], P('dp', None, 'tensor')
- grad_w_out_attn: float32 [768, 768], P('dp', 'tensor')
- grad_w_router: float32 [768, 4], P('dp')
- grad_w_in: float32 [768, 4, 3072], P('dp', None, 'tensor')
- grad_w_out: float32 [768, 4, 3072], P('dp', None, 'tensor')
- grad_norm1_gain: float32 [768], P('dp')
- grad_norm2_gain: float32 [768], P('dp')
- grad_bias_table: float32 [384], P('dp')
The draws below stay inside these ranges and needn't reach their ends.
Inputs may be any that keep to these rules, and one draw needn't show every extreme that they name: Positions at or past a group's seq_length are padding; some group is full. `expert_slots`: within one group no two tokens share an expert and a slot; -1 marks a token that is not sent (padding, or over the capacity of 128); in every group some expert's 128 slots are all used.
All inputs are finite; a program needn't handle non-finite values.
Results may differ from the reference program's by a relative error of at most 0.017.
Values may be sent and summed in bfloat16 or wider, within the bound.
No kernel may reach another device: no remote copies, remote signals or barrier semaphores. Data moves between devices by JAX's collectives and lax.ppermute only.
A program may use at most 192 MiB of HBM per device.

```python
import jax
import jax.numpy as jnp
from jax import lax

D = 768
H = 12
HD = 64
FF = 3072
NB = 32
E = 4
SEQ = 512
CAP = 128
GROUPS = 8
TOKENS = 4096


def routing_tables(key):
    split_keys = jax.random.split(key, 5)
    shorter = jax.random.randint(split_keys[0], (GROUPS,), 0, SEQ // 4)
    full_group = jax.random.randint(split_keys[1], (), 0, GROUPS)
    lengths = jnp.where(jnp.arange(GROUPS) == full_group, SEQ, SEQ - shorter).astype(jnp.int32)
    favored = jax.random.randint(split_keys[2], (GROUPS, 1), 0, E)
    phases = jax.random.randint(split_keys[3], (GROUPS, 1), 0, 3)
    others = jax.random.randint(split_keys[4], (GROUPS, SEQ), 0, E)
    position = jnp.arange(SEQ, dtype=jnp.int32)[None, :]
    chosen = jnp.where((position + phases) % 3 == 0, favored, others).astype(jnp.int32)
    live_rows = position < lengths[:, None]
    onehot = ((chosen[:, :, None] == jnp.arange(E, dtype=jnp.int32)[None, None, :]) & live_rows[:, :, None]).astype(jnp.int32)
    ranking = jnp.sum((jnp.cumsum(onehot, axis=1) - 1) * onehot, axis=2)
    slot_ids = jnp.where(live_rows & (ranking < CAP), ranking, -1).astype(jnp.int32)
    return (lengths, chosen.reshape(-1), slot_ids.reshape(-1))


def draw_seq_length(key, part):
    lengths, chosen, slot_ids = routing_tables(key)
    return lengths


def draw_expert_ids(key, part):
    lengths, chosen, slot_ids = routing_tables(key)
    return chosen


def draw_expert_slots(key, part):
    lengths, chosen, slot_ids = routing_tables(key)
    return slot_ids


def touch_ends(values, rng, smallest, largest):
    longest = values.shape.index(max(values.shape))
    spots = []
    for shift in (0, 1):
        where = [jax.random.randint(jax.random.fold_in(rng, axis), (), 0, length) for axis, length in enumerate(values.shape)]
        where[longest] = (where[longest] + shift) % values.shape[longest]
        spots.append(tuple(where))
    return values.at[spots[0]].set(smallest).at[spots[1]].set(largest)


def strengthened(values, key, source, target, blocks, factor):
    def block_of(axis_at):
        return (jnp.arange(values.shape[axis_at]) // (values.shape[axis_at] // blocks)).reshape((-1,) + (1,) * (values.ndim - 1 - axis_at))

    near = jax.random.permutation(key, blocks)[block_of(target)]
    other_side = (block_of(target) + blocks // 2) % blocks
    return jnp.where((block_of(source) == near) | (block_of(source) == other_side), factor * values, values)


def shard_levels(own_key, extent, cuts, smallest, largest):
    def one(dim, shards_of):
        heights = jax.random.uniform(jax.random.fold_in(jax.random.fold_in(own_key, 6), dim), (shards_of,), jnp.float32, smallest / len(cuts), largest / len(cuts))
        return jnp.repeat(jnp.exp(heights), extent[dim] // shards_of).reshape((-1,) + (1,) * (len(extent) - dim - 1))

    gain = one(*cuts[0])
    for cut in cuts[1:]:
        gain = gain * one(*cut)
    return gain


def normal_values(key, shape, deviation, bound, cuts=(), held_as=jnp.bfloat16):
    values = deviation * jax.random.normal(key, shape, jnp.float32)
    if cuts:
        values = values * shard_levels(key, shape, cuts, -0.22, 0.18)
    return jnp.clip(values, -bound, bound).astype(held_as)


def bell_draw_with(key, dims, width, reach, pieces, heavy, kind=jnp.bfloat16):
    values = width * jax.random.normal(key, dims, jnp.float32)
    if pieces:
        values = values * shard_levels(key, dims, pieces, -0.22, 0.18)
    return jnp.clip(strengthened(values, jax.random.fold_in(key, 3), *heavy), -reach, reach).astype(kind)


def setup_inputs(seed: int = 0) -> dict:
    splits = jax.random.split(jax.random.key(seed), 15)
    tokens = normal_values(splits[0], (TOKENS, D), 1.0, 6.0, ((0, 32),))
    cotangent = bell_draw_with(splits[1], (TOKENS, D), 1.0, 6.0, ((0, 32),), (0, 1, 32, 2.75))
    w_qkv = normal_values(splits[2], (D, 3, D), D ** -0.5, 0.21875, ((0, 8), (2, 4)))
    w_out_attn = normal_values(splits[3], (D, D), 4 ** -0.5, 3.0, ((0, 8), (1, 4)))
    w_router = normal_values(splits[4], (D, E), (4 * D) ** -0.5, 0.109375, ((0, 8),))
    w_in = normal_values(splits[5], (D, E, FF), D ** -0.5, 0.21875, ((0, 8), (2, 4)))
    w_out = normal_values(splits[6], (D, E, FF), (max(1, FF // 64)) ** -0.5, 0.875, ((0, 8), (2, 4)))
    norm1_gain = jnp.clip(1.0 + 0.18 * jax.random.normal(splits[7], (D,), jnp.float32), 0.099609375, 1.8984375).astype(jnp.bfloat16)
    norm2_gain = jnp.clip(1.0 + 0.18 * jax.random.normal(splits[8], (D,), jnp.float32), 0.099609375, 1.8984375).astype(jnp.bfloat16)
    bias_table = normal_values(splits[9], (H * NB,), 1.0, 4.0, ((0, 8),))
    seq_length = draw_seq_length(jax.random.fold_in(splits[14], 71), 0)
    expert_ids = draw_expert_ids(jax.random.fold_in(splits[14], 71), 0)
    expert_slots = draw_expert_slots(jax.random.fold_in(splits[14], 71), 0)
    buckets = touch_ends(jax.random.randint(splits[13], (2 * SEQ - 1,), 0, NB), jax.random.fold_in(splits[13], 1), 0, NB - 1).astype(jnp.int32)
    return dict(tokens=tokens, cotangent=cotangent, w_qkv=w_qkv, w_out_attn=w_out_attn, w_router=w_router, w_in=w_in, w_out=w_out, norm1_gain=norm1_gain, norm2_gain=norm2_gain, bias_table=bias_table, seq_length=seq_length, expert_ids=expert_ids, expert_slots=expert_slots, buckets=buckets)


EPSILON = 1e-06
HIGHEST_PRECISION = lax.Precision.HIGHEST

@jax.custom_vjp
def low(v):
    return lax.optimization_barrier(v.astype(jnp.bfloat16)).astype(jnp.float32)

@jax.custom_vjp
def low_back(v):
    return v

def low_keep(v):
    return (low(v), None)

def low_pass(kept, grad):
    return (grad,)

def back_keep(v):
    return (v, None)

def back_low(kept, grad):
    return (low(grad),)
low.defvjp(low_keep, low_pass)
low_back.defvjp(back_keep, back_low)

def normalize(values, scale_gain):
    return values * lax.rsqrt(lax.optimization_barrier(jnp.mean(values * values, axis=-1, keepdims=True)) + EPSILON) * scale_gain

def attention(queries, keys_all, values_all, bias_rows, buckets, key_live):
    block_rows = min(512, SEQ)

    def one_block(offset):
        query_block = lax.dynamic_slice_in_dim(queries, offset, block_rows, 0)
        distance = (offset + jnp.arange(block_rows, dtype=jnp.int32))[:, None] - jnp.arange(SEQ, dtype=jnp.int32)[None, :] + (SEQ - 1)
        rel_bias = bias_rows[:, buckets[distance]]
        scores = jnp.einsum('qhe,khe->hqk', query_block, keys_all, precision=HIGHEST_PRECISION) * 0.125 + rel_bias
        scores = low_back(scores)
        scores = jnp.where(key_live[None, None, :], scores, -1e+30)
        attn_probs = low(jax.nn.softmax(scores, axis=-1))
        return jnp.einsum('hqk,khe->qhe', attn_probs, values_all, precision=HIGHEST_PRECISION)
    block_starts = jnp.arange(SEQ // block_rows, dtype=jnp.int32) * block_rows
    blocks_out = lax.map(jax.checkpoint(one_block), block_starts)
    return blocks_out.reshape(SEQ, H * HD)

def encoder_layer(inputs, length, chosen, slot_ids, w_qkv, w_out_attn, w_router, w_in, w_out, gain_one, gain_two, bias_table, buckets):
    normed_one = low(normalize(inputs, gain_one))
    qkv_all = low_back(low(jnp.einsum('td,dcf->tcf', normed_one, w_qkv, precision=HIGHEST_PRECISION)))
    queries = qkv_all[:, 0].reshape(SEQ, H, HD)
    keys_all = qkv_all[:, 1].reshape(SEQ, H, HD)
    values_all = qkv_all[:, 2].reshape(SEQ, H, HD)
    key_live = jnp.arange(SEQ, dtype=jnp.int32) < length
    heads_all = low_back(low(attention(queries, keys_all, values_all, bias_table.reshape(H, NB), buckets, key_live)))
    attended = low_back(jnp.dot(heads_all, w_out_attn.T, precision=HIGHEST_PRECISION))
    middle = inputs + attended
    normed_two = low(normalize(middle, gain_two))
    logits = jnp.dot(normed_two, w_router, precision=HIGHEST_PRECISION)
    route = jax.nn.softmax(logits, axis=-1)
    chosen_mask = chosen[:, None] == jnp.arange(E, dtype=jnp.int32)[None, :]
    gate_value = lax.optimization_barrier(jnp.sum(jnp.where(chosen_mask, route, 0.0), axis=-1))
    dispatched = slot_ids >= 0
    flat_slot = jnp.where(dispatched, chosen * CAP + slot_ids, E * CAP).astype(jnp.int32)
    owners = jnp.zeros((E * CAP + 1,), jnp.int32).at[flat_slot].set(jnp.arange(SEQ, dtype=jnp.int32))[:E * CAP]
    filled = jnp.zeros((E * CAP + 1,), jnp.float32).at[flat_slot].set(1.0)[:E * CAP]
    buffer = (normed_two[owners] * filled[:, None]).reshape(E, CAP, D)
    pre_act = low_back(jnp.einsum('ecd,def->ecf', buffer, w_in, precision=HIGHEST_PRECISION))
    activation = low(jax.nn.gelu(pre_act))
    expert_out = jnp.einsum('ecf,def->ecd', activation, w_out, precision=HIGHEST_PRECISION).reshape(E * CAP, D)
    picked = expert_out[jnp.minimum(flat_slot, E * CAP - 1)] * dispatched[:, None].astype(jnp.float32)
    combined = low_back(picked)
    return middle + gate_value[:, None] * combined

def reference(tokens, cotangent, w_qkv, w_out_attn, w_router, w_in, w_out, norm1_gain, norm2_gain, bias_table, seq_length, expert_ids, expert_slots, buckets):
    floats = tuple((array.astype(jnp.float32) for array in (tokens, w_qkv, w_out_attn, w_router, w_in, w_out, norm1_gain, norm2_gain, bias_table)))

    def forward(inputs, qkv_weight, attn_weight, router_weight, in_weight, out_weight, gain_one, gain_two, table_flat):

        def group_layer(group_item):
            group_rows, length, chosen, slot_ids = group_item
            return encoder_layer(group_rows, length, chosen, slot_ids, qkv_weight, attn_weight, router_weight, in_weight, out_weight, gain_one, gain_two, table_flat, buckets)
        checked = jax.checkpoint(group_layer)

        def scan_step(carried, group_item):
            return (carried, checked(group_item))
        group_items = (inputs.reshape(GROUPS, SEQ, D), seq_length, expert_ids.reshape(GROUPS, SEQ), expert_slots.reshape(GROUPS, SEQ))
        _, outputs = lax.scan(scan_step, jnp.zeros((), jnp.float32), group_items)
        return outputs.reshape(TOKENS, D)
    result, pullback = jax.vjp(forward, *floats)
    gradients = pullback(cotangent.astype(jnp.float32))
    return (result.astype(jnp.bfloat16), gradients[0], gradients[1], gradients[2], gradients[3], gradients[4], gradients[5], gradients[6], gradients[7], gradients[8])
```

```python
import functools

import jax
import jax.numpy as jnp
from jax import lax
from jax.experimental import pallas as pl
from jax.experimental.pallas import tpu as pltpu
from jax.sharding import PartitionSpec as P

D = 768
H = 12
HD = 64
NB = 32
E = 4
SEQ = 512
CAP = 128
T = 4
LH = H // T
LW = LH * HD
ROWS = SEQ // T
SUB = CAP // T
SPAN = 2 * SEQ
TILE = 128
TILES = SEQ // TILE

EPSILON = 1e-06
HIGHEST_PRECISION = lax.Precision.HIGHEST
BF = jnp.bfloat16
F32 = jnp.float32


def mm(a, b, ca, cb):
    return lax.dot_general(a, b, (((ca,), (cb,)), ((), ())), preferred_element_type=F32)


def over_t(x, k):
    return lax.ppermute(x, "tensor", [(i, i ^ k) for i in range(T)])


def over_z(x, d):
    n = lax.axis_size("dp")
    r = n // E
    return lax.ppermute(x, "dp", [(i, ((i // r) ^ d) * r + i % r) for i in range(n)])


def over_r(x, c):
    n = lax.axis_size("dp")
    r = n // E
    return lax.ppermute(x, "dp", [(i, (i // r) * r + ((i % r) ^ c)) for i in range(n)])


def natural(parts, index):
    bit = 1
    while bit < len(parts):
        flip = (index & bit) != 0
        parts = [jnp.where(flip, parts[j ^ bit], parts[j]) for j in range(len(parts))]
        bit *= 2
    return parts


def gather_t(x):
    far = over_t(x, 2)
    near, diagonal = over_t(x, 1), over_t(far, 1)
    return [x, near, far, diagonal]


def scatter_t(blocks):
    first = over_t(blocks[3], 1)
    second = over_t(blocks[1], 1)
    away = (blocks[2].astype(F32) + first.astype(F32)).astype(BF)
    home = blocks[0].astype(F32) + second.astype(F32)
    return home + over_t(away, 2).astype(F32)


def pick(x, index, axis):
    return lax.dynamic_index_in_dim(x, index, axis, keepdims=False)


def scatter_dp(x, z, r):
    n = x.shape[0]
    R = n // E
    x = x.reshape(E, R, *x.shape[1:])
    total = pick(x, r, 1).astype(F32)
    for c in range(1, R):
        total = total + over_r(pick(x, r ^ c, 1).astype(BF), c).astype(F32)
    low = total.astype(BF)
    out = pick(total, z, 0)
    for d in range(1, E):
        out = out + over_z(pick(low, z ^ d, 0), d).astype(F32)
    return out


def attention_forward(length, qkv_ref, rel_ref, probs_ref, heads_ref):
    live = lax.broadcasted_iota(jnp.int32, (TILE, SEQ), 1) < length[0]
    for h in range(LH):
        key = qkv_ref[:, LW + h * HD : LW + (h + 1) * HD]
        value = qkv_ref[:, 2 * LW + h * HD : 2 * LW + (h + 1) * HD]
        bias = jnp.broadcast_to(rel_ref[h : h + 1, :], (TILE, SPAN))
        for i in range(TILES):
            rows = slice(i * TILE, (i + 1) * TILE)
            query = qkv_ref[rows, h * HD : (h + 1) * HD]
            rolled = pltpu.roll(bias, SEQ + 1 + i * TILE, 1, stride=1, stride_axis=0)[:, :SEQ]
            scores = mm(query, key, 1, 1) * 0.125 + rolled
            scores = jnp.where(live, scores, -1e30)
            exponent = jnp.exp(scores - jnp.max(scores, axis=1, keepdims=True))
            probs = exponent / jnp.sum(exponent, axis=1, keepdims=True)
            probs_ref[h, rows, :] = probs
            heads_ref[rows, h * HD : (h + 1) * HD] = mm(probs.astype(BF), value, 1, 0).astype(BF)


def attention_backward(qkv_ref, probs_ref, grad_ref, out_ref, rel_ref):
    flip = (
        lax.broadcasted_iota(jnp.int32, (TILE, TILE), 0)
        + lax.broadcasted_iota(jnp.int32, (TILE, TILE), 1)
        == TILE - 1
    ).astype(BF)
    rel_ref[...] = jnp.zeros_like(rel_ref)
    for h in range(LH):
        key = qkv_ref[:, LW + h * HD : LW + (h + 1) * HD]
        value = qkv_ref[:, 2 * LW + h * HD : 2 * LW + (h + 1) * HD]
        grad_key = jnp.zeros((SEQ, HD), F32)
        grad_value = jnp.zeros((SEQ, HD), F32)
        diagonal = [None] * (2 * TILES - 1)
        for i in range(TILES):
            rows = slice(i * TILE, (i + 1) * TILE)
            query = qkv_ref[rows, h * HD : (h + 1) * HD]
            grad = grad_ref[rows, h * HD : (h + 1) * HD]
            probs = probs_ref[h, rows, :]
            grad_probs = mm(grad, value, 1, 1)
            inner = jnp.sum(probs * grad_probs, axis=1, keepdims=True)
            low = (probs * (grad_probs - inner)).astype(BF)
            out_ref[rows, h * HD : (h + 1) * HD] = (mm(low, key, 1, 0) * 0.125).astype(BF)
            grad_key = grad_key + mm(low, query, 0, 0)
            grad_value = grad_value + mm(probs.astype(BF), grad, 0, 0)
            for j in range(TILES):
                turned = mm(low[:, j * TILE : (j + 1) * TILE], flip, 1, 0)
                at = i - j + TILES - 1
                diagonal[at] = turned if diagonal[at] is None else diagonal[at] + turned
        out_ref[:, LW + h * HD : LW + (h + 1) * HD] = (grad_key * 0.125).astype(BF)
        out_ref[:, 2 * LW + h * HD : 2 * LW + (h + 1) * HD] = grad_value.astype(BF)
        for at, block in enumerate(diagonal):
            wide = jnp.concatenate([block, jnp.zeros((TILE, TILE), F32)], axis=1)
            line = jnp.sum(
                pltpu.roll(wide, 0, 1, stride=1, stride_axis=0), axis=0, keepdims=True
            )
            rel_ref[h : h + 1, at * TILE : (at + 2) * TILE] += line


VMEM = pl.BlockSpec(memory_space=pltpu.VMEM)
BIG = pltpu.CompilerParams(vmem_limit_bytes=40 * 2**20)


def attend(qkv, reversed_rel, length):
    return pl.pallas_call(
        attention_forward,
        out_shape=(
            jax.ShapeDtypeStruct((LH, SEQ, SEQ), F32),
            jax.ShapeDtypeStruct((SEQ, LW), BF),
        ),
        in_specs=[pl.BlockSpec(memory_space=pltpu.SMEM), VMEM, VMEM],
        out_specs=(VMEM, VMEM),
        compiler_params=BIG,
        cost_estimate=pl.CostEstimate(
            flops=4 * LH * SEQ * SEQ * HD,
            bytes_accessed=4 * LH * SEQ * SEQ,
            transcendentals=LH * SEQ * SEQ,
        ),
        name="attention_forward",
    )(length, qkv, reversed_rel)


def attend_back(qkv, probs, grad_heads):
    return pl.pallas_call(
        attention_backward,
        out_shape=(
            jax.ShapeDtypeStruct((SEQ, 3 * LW), BF),
            jax.ShapeDtypeStruct((LH, SPAN), F32),
        ),
        in_specs=[VMEM, VMEM, VMEM],
        out_specs=(VMEM, VMEM),
        compiler_params=BIG,
        cost_estimate=pl.CostEstimate(
            flops=12 * LH * SEQ * SEQ * HD, bytes_accessed=4 * LH * SEQ * SEQ, transcendentals=0
        ),
        name="attention_backward",
    )(qkv, probs, grad_heads)


def norm_scale(values):
    return lax.rsqrt(jnp.mean(values * values, axis=-1, keepdims=True) + EPSILON)


def norm_back(grad, values, scale, gain):
    u = grad * gain
    inner = jnp.mean(u * values, axis=-1, keepdims=True)
    return scale * u - scale * scale * scale * values * inner


def gather_weight(weight, z, r):
    parts = [pick(weight, z, 1)] + [over_z(pick(weight, z ^ d, 1), d) for d in range(1, E)]
    column = jnp.stack(natural(parts, z))
    n = lax.axis_size("dp")
    R = n // E
    every = [column] + [over_r(column, c) for c in range(1, R)]
    return jnp.stack(natural(every, r), axis=1).reshape(-1, weight.shape[2])


def scatter_weight(grad, z, r):
    n = lax.axis_size("dp")
    R = n // E
    x = grad.reshape(E, R, D // n, -1)
    total = pick(x, r, 1).astype(F32)
    for c in range(1, R):
        total = total + over_r(pick(x, r ^ c, 1).astype(BF), c).astype(F32)
    low = total.astype(BF)
    parts = [pick(low, z, 0)] + [over_z(pick(low, z ^ d, 0), d) for d in range(1, E)]
    return jnp.stack(natural(parts, z), axis=1).astype(F32)


def body(
    tokens,
    cotangent,
    w_qkv,
    w_out_attn,
    w_router,
    w_in,
    w_out,
    norm1_gain,
    norm2_gain,
    bias_table,
    seq_length,
    expert_ids,
    expert_slots,
    buckets,
):
    n = lax.axis_size("dp")
    R = n // E
    at_dp = lax.axis_index("dp")
    z, r = at_dp // R, at_dp % R
    t = lax.axis_index("tensor")
    local = D // n

    table_column = jnp.pad(bias_table, (0, local - bias_table.shape[0]))
    packed = jnp.concatenate(
        [
            w_qkv.reshape(local, 3 * LW),
            w_out_attn,
            w_router,
            norm1_gain[:, None],
            norm2_gain[:, None],
            table_column[:, None],
        ],
        axis=1,
    )
    packed = lax.all_gather(packed, "dp", axis=0, tiled=True)
    qkv_weight = packed[:, : 3 * LW]
    attn_weight = packed[:, 3 * LW : 4 * LW]
    router_weight = packed[:, 4 * LW : 4 * LW + E]
    gain_one = packed[:, 4 * LW + E].astype(F32)
    gain_two = packed[:, 4 * LW + E + 1].astype(F32)
    table_flat = packed[:, 4 * LW + E + 2].reshape(n, local)[:, : H * NB // n].reshape(-1)

    token_parts = gather_t(tokens)
    tokens_all = jnp.concatenate(natural(token_parts, t), axis=0)
    cotangent_all = jnp.concatenate(natural(gather_t(cotangent), t), axis=0)

    sent = expert_slots >= 0
    absolute = jnp.where(sent, expert_ids * CAP + expert_slots, -1)
    position = jnp.arange(SEQ, dtype=jnp.int32)
    empty = ~jnp.any(absolute[None, :] == position[:, None], axis=1)
    before = position[None, :] <= position[:, None]
    empty_rank = jnp.sum((before & empty[None, :]).astype(jnp.int32), axis=1)
    unsent_rank = jnp.sum((before & ~sent[None, :]).astype(jnp.int32), axis=1)
    match = empty[None, :] & (empty_rank[None, :] == unsent_rank[:, None])
    spare = jnp.sum(jnp.where(match, position[None, :], 0), axis=1)
    slot = jnp.where(sent, absolute, spare)
    in_expert = slot % CAP
    place = ((in_expert // SUB) ^ t) * ROWS + ((slot // CAP) ^ z) * SUB + in_expert % SUB
    to_slots_mask = place[None, :] == position[:, None]
    to_slots = to_slots_mask.astype(BF)
    own_mask = to_slots_mask[:ROWS]
    sent_own = jnp.any(own_mask & sent[None, :], axis=1)
    chosen_own = jnp.sum(jnp.where(own_mask, expert_ids[None, :], 0), axis=1)
    own_tokens = lax.dynamic_slice_in_dim(place, t * ROWS, ROWS, 0)
    from_slots_own = (own_tokens[:, None] == position[None, :]).astype(BF)

    def dispatch(rows):
        rows = jnp.where(sent_own[:, None], rows, 0).astype(BF)
        blocks = [rows[d * SUB : (d + 1) * SUB] for d in range(E)]
        arrived = [blocks[0]] + [over_z(blocks[d], d) for d in range(1, E)]
        return jnp.concatenate(gather_t(jnp.concatenate(arrived, axis=0)), axis=0)

    grad_output = mm(to_slots[:ROWS], cotangent_all, 1, 0)
    expert_cotangent = dispatch(grad_output)
    in_weight = gather_weight(w_in, z, r)
    out_weight = gather_weight(w_out, z, r)

    inputs_all = tokens_all.astype(F32)
    scale_all = norm_scale(inputs_all)
    normed_all = (inputs_all * scale_all * gain_one).astype(BF)
    qkv = mm(normed_all, qkv_weight, 1, 0).astype(BF)
    table_rows = lax.dynamic_slice_in_dim(table_flat.astype(F32).reshape(H, NB), t * LH, LH, 0)
    bucket_table = (buckets[None, :] == jnp.arange(NB, dtype=jnp.int32)[:, None]).astype(F32)
    reversed_rel = jnp.dot(
        table_rows,
        jnp.pad(bucket_table[:, ::-1], ((0, 0), (0, 1))),
        precision=HIGHEST_PRECISION,
    )
    probs, heads_all = attend(qkv, reversed_rel, seq_length)
    heads_slots = mm(to_slots, heads_all, 1, 0).astype(BF)
    part = mm(heads_slots, attn_weight, 1, 1).astype(BF).reshape(T, ROWS, D)
    attended = scatter_t([part[k] for k in range(T)])
    inputs = mm(to_slots[:ROWS], tokens_all, 1, 0)
    middle = inputs + attended
    scale_two = norm_scale(middle)
    normed_two = (middle * scale_two * gain_two).astype(BF)

    buffer = dispatch(normed_two)

    def route_of(rows):
        return jax.nn.softmax(mm(rows, router_weight, 1, 0), axis=-1)

    experts = jnp.arange(E, dtype=jnp.int32)[None, :]
    expert_gate = jnp.sum(jnp.where(experts == z, route_of(buffer), 0.0), axis=-1)
    grad_expert = (expert_gate[:, None] * expert_cotangent.astype(F32)).astype(BF)
    pre_act = mm(buffer, in_weight, 1, 0)
    activation, gelu_pull = jax.vjp(jax.nn.gelu, pre_act)
    activation = activation.astype(BF)
    grad_act = mm(grad_expert, out_weight, 1, 0)
    grad_pre = gelu_pull(grad_act)[0].astype(BF)
    expert_out = mm(activation, out_weight, 1, 1).astype(BF)
    grad_buffer = mm(grad_pre, in_weight, 1, 1).astype(BF)
    both = jnp.concatenate([expert_out, grad_buffer], axis=1).reshape(T, ROWS, 2 * D)
    mine = scatter_t([both[k] for k in range(T)]).astype(BF)
    blocks = [mine[d * SUB : (d + 1) * SUB] for d in range(E)]
    returned = jnp.concatenate(
        [blocks[0]] + [over_z(blocks[d], d) for d in range(1, E)], axis=0
    ).astype(F32)
    combined, grad_normed_two = returned[:, :D], returned[:, D:]

    summed_out_grad = scatter_weight(mm(grad_expert, activation, 0, 0), z, r)
    summed_in_grad = scatter_weight(mm(buffer, grad_pre, 0, 0), z, r)

    route = route_of(normed_two)
    chosen = experts == chosen_own[:, None]
    gate = jnp.sum(jnp.where(chosen, route, 0.0), axis=-1)
    layer_rows = (middle + gate[:, None] * combined).astype(BF)
    grad_gate = jnp.sum(grad_output * combined, axis=-1)
    grad_logits = gate[:, None] * (chosen.astype(F32) - route) * grad_gate[:, None]
    grad_router = jnp.dot(normed_two.astype(F32).T, grad_logits, precision=HIGHEST_PRECISION)
    grad_normed_two = grad_normed_two + jnp.dot(
        grad_logits, router_weight.astype(F32).T, precision=HIGHEST_PRECISION
    )
    grad_gain_two = jnp.sum(grad_normed_two * middle * scale_two, axis=0)
    grad_middle = (grad_output + norm_back(grad_normed_two, middle, scale_two, gain_two)).astype(BF)
    grad_slots = jnp.concatenate(gather_t(grad_middle), axis=0)
    layer_slots = jnp.concatenate(gather_t(layer_rows), axis=0)
    layer_out = mm(from_slots_own, layer_slots, 1, 0).astype(BF)

    grad_attended = mm(to_slots, grad_slots, 0, 0).astype(BF)
    grad_heads = mm(grad_attended, attn_weight, 1, 0).astype(BF)
    grad_attn_weight = mm(grad_attended, heads_all, 0, 0)
    grad_qkv, grad_rel = attend_back(qkv, probs, grad_heads)
    grad_normed_part = mm(grad_qkv, qkv_weight, 1, 1)
    grad_qkv_weight = mm(normed_all, grad_qkv, 0, 0)
    grad_gain_one = jnp.sum(grad_normed_part * inputs_all * scale_all, axis=0)
    part = natural(list(grad_normed_part.astype(BF).reshape(T, ROWS, D)), t)
    grad_normed_one = scatter_t(part)
    own_inputs = tokens.astype(F32)
    grad_tokens = mm(from_slots_own, grad_slots, 1, 0) + norm_back(
        grad_normed_one, own_inputs, norm_scale(own_inputs), gain_one
    )
    grad_table_rows = jnp.dot(
        grad_rel,
        jnp.pad(bucket_table, ((0, 0), (0, 1))).T,
        precision=HIGHEST_PRECISION,
    )
    grad_table = lax.dynamic_update_slice_in_dim(
        jnp.zeros((H, NB), F32), grad_table_rows, t * LH, 0
    ).reshape(n, H * NB // n)

    def with_tail(matrix, columns):
        tail = jnp.concatenate(columns, axis=1)
        width = matrix.shape[2]
        tail = jnp.pad(tail, ((0, 0), (0, -tail.shape[1] % width)))
        return jnp.concatenate([matrix, tail.reshape(n, -1, width)], axis=1)

    early = scatter_dp(
        with_tail(
            grad_attn_weight.reshape(n, local, LW),
            [grad_router.reshape(n, local * E), grad_gain_two.reshape(n, local)],
        ),
        z,
        r,
    )
    late = scatter_dp(
        with_tail(
            grad_qkv_weight.reshape(n, local, 3 * LW),
            [grad_gain_one.reshape(n, local), grad_table],
        ),
        z,
        r,
    )
    early_tail = early[local:].reshape(-1)[: local * (E + 1)]
    late_tail = late[local:].reshape(-1)[: local + H * NB // n]
    small = jnp.concatenate([early_tail, late_tail]).reshape(1, -1)
    small = small + over_t(small, 1)
    small = (small + over_t(small, 2))[0]
    return (
        layer_out,
        grad_tokens,
        late[:local].reshape(local, 3, LW),
        early[:local],
        small[: local * E].reshape(local, E),
        summed_in_grad,
        summed_out_grad,
        small[local * (E + 1) : local * (E + 2)],
        small[local * E : local * (E + 1)],
        small[local * (E + 2) :],
    )


def solution(mesh):
    in_specs = (
        P(("dp", "tensor"), None),
        P(("dp", "tensor"), None),
        P("dp", None, "tensor"),
        P("dp", "tensor"),
        P("dp", None),
        P("dp", None, "tensor"),
        P("dp", None, "tensor"),
        P("dp"),
        P("dp"),
        P("dp"),
        P("dp"),
        P("dp"),
        P("dp"),
        P(),
    )
    out_specs = (
        P(("dp", "tensor"), None),
        P(("dp", "tensor"), None),
        P("dp", None, "tensor"),
        P("dp", "tensor"),
        P("dp", None),
        P("dp", None, "tensor"),
        P("dp", None, "tensor"),
        P("dp"),
        P("dp"),
        P("dp"),
    )
    return jax.shard_map(body, mesh=mesh, in_specs=in_specs, out_specs=out_specs, check_vma=False)
```

```python
import functools

import jax
import jax.numpy as jnp
from jax import lax
from jax.experimental import pallas as pl
from jax.experimental.pallas import tpu as pltpu
from jax.sharding import PartitionSpec as P

D = 768
H = 12
HD = 64
NB = 32
E = 4
SEQ = 512
CAP = 128
T = 4
LH = H // T
LW = LH * HD
ROWS = SEQ // T
SUB = CAP // T
SPAN = 2 * SEQ
TILE = 128
TILES = SEQ // TILE

EPSILON = 1e-06
HIGHEST_PRECISION = lax.Precision.HIGHEST
BF = jnp.bfloat16
F32 = jnp.float32


def mm(a, b, ca, cb):
    return lax.dot_general(a, b, (((ca,), (cb,)), ((), ())), preferred_element_type=F32)


def over_t(x, k):
    return lax.ppermute(x, "tensor", [(i, i ^ k) for i in range(T)])


def over_z(x, d):
    n = lax.axis_size("dp")
    r = n // E
    return lax.ppermute(x, "dp", [(i, ((i // r) ^ d) * r + i % r) for i in range(n)])


def over_r(x, c):
    n = lax.axis_size("dp")
    r = n // E
    return lax.ppermute(x, "dp", [(i, (i // r) * r + ((i % r) ^ c)) for i in range(n)])


def natural(parts, index):
    bit = 1
    while bit < len(parts):
        flip = (index & bit) != 0
        parts = [jnp.where(flip, parts[j ^ bit], parts[j]) for j in range(len(parts))]
        bit *= 2
    return parts


def gather_t(x):
    far = over_t(x, 2)
    near = over_t(jnp.stack([x, far]), 1)
    return [x, near[0], far, near[1]]


def scatter_t(blocks, *earlier):
    first = over_t(jnp.stack([blocks[3], blocks[1]]), 1).astype(F32)
    away = after((blocks[2].astype(F32) + first[0]).astype(BF), *earlier)
    home = blocks[0].astype(F32) + first[1]
    return home + over_t(away, 2).astype(F32)


def pick(x, index, axis):
    return lax.dynamic_index_in_dim(x, index, axis, keepdims=False)


def attention_forward(length, qkv_ref, rel_ref, probs_ref, heads_ref):
    live = lax.broadcasted_iota(jnp.int32, (TILE, SEQ), 1) < length[0]
    for h in range(LH):
        key = qkv_ref[:, LW + h * HD : LW + (h + 1) * HD]
        value = qkv_ref[:, 2 * LW + h * HD : 2 * LW + (h + 1) * HD]
        bias = jnp.broadcast_to(rel_ref[h : h + 1, :], (TILE, SPAN))
        for i in range(TILES):
            rows = slice(i * TILE, (i + 1) * TILE)
            query = qkv_ref[rows, h * HD : (h + 1) * HD]
            rolled = pltpu.roll(bias, SEQ + 1 + i * TILE, 1, stride=1, stride_axis=0)[:, :SEQ]
            scores = mm(query, key, 1, 1) * 0.125 + rolled
            scores = jnp.where(live, scores, -1e30)
            exponent = jnp.exp(scores - jnp.max(scores, axis=1, keepdims=True))
            probs = exponent / jnp.sum(exponent, axis=1, keepdims=True)
            probs_ref[h, rows, :] = probs
            heads_ref[rows, h * HD : (h + 1) * HD] = mm(probs.astype(BF), value, 1, 0).astype(BF)


def attention_backward(qkv_ref, probs_ref, grad_ref, out_ref, rel_ref):
    flip = (
        lax.broadcasted_iota(jnp.int32, (TILE, TILE), 0)
        + lax.broadcasted_iota(jnp.int32, (TILE, TILE), 1)
        == TILE - 1
    ).astype(BF)
    rel_ref[...] = jnp.zeros_like(rel_ref)
    for h in range(LH):
        key = qkv_ref[:, LW + h * HD : LW + (h + 1) * HD]
        value = qkv_ref[:, 2 * LW + h * HD : 2 * LW + (h + 1) * HD]
        grad_key = jnp.zeros((SEQ, HD), F32)
        grad_value = jnp.zeros((SEQ, HD), F32)
        diagonal = [None] * (2 * TILES - 1)
        for i in range(TILES):
            rows = slice(i * TILE, (i + 1) * TILE)
            query = qkv_ref[rows, h * HD : (h + 1) * HD]
            grad = grad_ref[rows, h * HD : (h + 1) * HD]
            probs = probs_ref[h, rows, :]
            grad_probs = mm(grad, value, 1, 1)
            inner = jnp.sum(probs * grad_probs, axis=1, keepdims=True)
            low = (probs * (grad_probs - inner)).astype(BF)
            out_ref[rows, h * HD : (h + 1) * HD] = (mm(low, key, 1, 0) * 0.125).astype(BF)
            grad_key = grad_key + mm(low, query, 0, 0)
            grad_value = grad_value + mm(probs.astype(BF), grad, 0, 0)
            for j in range(TILES):
                turned = mm(low[:, j * TILE : (j + 1) * TILE], flip, 1, 0)
                at = i - j + TILES - 1
                diagonal[at] = turned if diagonal[at] is None else diagonal[at] + turned
        out_ref[:, LW + h * HD : LW + (h + 1) * HD] = (grad_key * 0.125).astype(BF)
        out_ref[:, 2 * LW + h * HD : 2 * LW + (h + 1) * HD] = grad_value.astype(BF)
        for at, block in enumerate(diagonal):
            wide = jnp.concatenate([block, jnp.zeros((TILE, TILE), F32)], axis=1)
            line = jnp.sum(
                pltpu.roll(wide, 0, 1, stride=1, stride_axis=0), axis=0, keepdims=True
            )
            rel_ref[h : h + 1, at * TILE : (at + 2) * TILE] += line


VMEM = pl.BlockSpec(memory_space=pltpu.VMEM)
BIG = pltpu.CompilerParams(vmem_limit_bytes=40 * 2**20)


def attend(qkv, reversed_rel, length):
    return pl.pallas_call(
        attention_forward,
        out_shape=(
            jax.ShapeDtypeStruct((LH, SEQ, SEQ), F32),
            jax.ShapeDtypeStruct((SEQ, LW), BF),
        ),
        in_specs=[pl.BlockSpec(memory_space=pltpu.SMEM), VMEM, VMEM],
        out_specs=(VMEM, VMEM),
        compiler_params=BIG,
        cost_estimate=pl.CostEstimate(
            flops=4 * LH * SEQ * SEQ * HD,
            bytes_accessed=4 * LH * SEQ * SEQ,
            transcendentals=LH * SEQ * SEQ,
        ),
        name="attention_forward",
    )(length, qkv, reversed_rel)


def attend_back(qkv, probs, grad_heads):
    return pl.pallas_call(
        attention_backward,
        out_shape=(
            jax.ShapeDtypeStruct((SEQ, 3 * LW), BF),
            jax.ShapeDtypeStruct((LH, SPAN), F32),
        ),
        in_specs=[VMEM, VMEM, VMEM],
        out_specs=(VMEM, VMEM),
        compiler_params=BIG,
        cost_estimate=pl.CostEstimate(
            flops=12 * LH * SEQ * SEQ * HD, bytes_accessed=4 * LH * SEQ * SEQ, transcendentals=0
        ),
        name="attention_backward",
    )(qkv, probs, grad_heads)


def norm_scale(values):
    return lax.rsqrt(jnp.mean(values * values, axis=-1, keepdims=True) + EPSILON)


def norm_back(grad, values, scale, gain):
    u = grad * gain
    inner = jnp.mean(u * values, axis=-1, keepdims=True)
    return scale * u - scale * scale * scale * values * inner


def exchange_weight(weight, z):
    parts = [pick(weight, z, 1)] + [over_z(pick(weight, z ^ d, 1), d) for d in range(1, E)]
    return jnp.stack(natural(parts, z))


def join_weight(column, r):
    R = lax.axis_size("dp") // E
    every = [column] + [over_r(column, c) for c in range(1, R)]
    return jnp.stack(natural(every, r), axis=1).reshape(-1, column.shape[2])


def swap_terms(x, r):
    n = x.shape[0]
    R = n // E
    x = x.reshape(E, R, *x.shape[1:])
    total = pick(x, r, 1).astype(F32)
    for c in range(1, R):
        total = total + over_r(pick(x, r ^ c, 1).astype(BF), c).astype(F32)
    return total


def deliver(low, z):
    return [pick(low, z, 0)] + [over_z(pick(low, z ^ d, 0), d) for d in range(1, E)]


def sum_everywhere(x):
    R = lax.axis_size("dp") // E
    for k in (1, 2):
        x = x + over_t(x, k)
    c = 1
    while c < R:
        x = x + over_r(x, c)
        c *= 2
    for d in (1, 2):
        x = x + over_z(x, d)
    return x


def after(x, *others):
    return lax.optimization_barrier((x, others))[0]


def body(
    tokens,
    cotangent,
    w_qkv,
    w_out_attn,
    w_router,
    w_in,
    w_out,
    norm1_gain,
    norm2_gain,
    bias_table,
    seq_length,
    expert_ids,
    expert_slots,
    buckets,
):
    n = lax.axis_size("dp")
    R = n // E
    at_dp = lax.axis_index("dp")
    z, r = at_dp // R, at_dp % R
    t = lax.axis_index("tensor")
    local = D // n

    tail_row = jnp.concatenate([w_router.reshape(-1), norm1_gain, norm2_gain, bias_table])
    tail_row = jnp.pad(tail_row, (0, -tail_row.shape[0] % (4 * LW))).reshape(-1, 4 * LW)
    packed = jnp.concatenate(
        [jnp.concatenate([w_qkv.reshape(local, 3 * LW), w_out_attn], axis=1), tail_row], axis=0
    )
    columns = [packed] + [over_z(packed, d) for d in range(1, E)]
    pieces = []
    for column in columns:
        pieces += [column] + [over_r(column, c) for c in range(1, R)]
    packed = jnp.stack(natural(pieces, at_dp))
    attention_weights = packed[:, :local].reshape(D, 4 * LW)
    qkv_weight = attention_weights[:, : 3 * LW]
    attn_weight = attention_weights[:, 3 * LW :]
    tails = packed[:, local:].reshape(n, -1)
    router_weight = tails[:, : local * E].reshape(D, E)
    gain_one = tails[:, local * E : local * (E + 1)].reshape(D).astype(F32)
    gain_two = tails[:, local * (E + 1) : local * (E + 2)].reshape(D).astype(F32)
    table_flat = tails[:, local * (E + 2) : local * (E + 2) + H * NB // n].reshape(-1)

    token_parts = gather_t(tokens)
    tokens_all = jnp.concatenate(natural(token_parts, t), axis=0)
    cotangent_parts = gather_t(after(cotangent, token_parts[3]))
    cotangent_all = jnp.concatenate(natural(cotangent_parts, t), axis=0)

    sent = expert_slots >= 0
    absolute = jnp.where(sent, expert_ids * CAP + expert_slots, -1)
    position = jnp.arange(SEQ, dtype=jnp.int32)
    empty = ~jnp.any(absolute[None, :] == position[:, None], axis=1)
    before = position[None, :] <= position[:, None]
    empty_rank = jnp.sum((before & empty[None, :]).astype(jnp.int32), axis=1)
    unsent_rank = jnp.sum((before & ~sent[None, :]).astype(jnp.int32), axis=1)
    match = empty[None, :] & (empty_rank[None, :] == unsent_rank[:, None])
    spare = jnp.sum(jnp.where(match, position[None, :], 0), axis=1)
    slot = jnp.where(sent, absolute, spare)
    in_expert = slot % CAP
    place = ((in_expert // SUB) ^ t) * ROWS + ((slot // CAP) ^ z) * SUB + in_expert % SUB
    to_slots_mask = place[None, :] == position[:, None]
    to_slots = to_slots_mask.astype(BF)
    own_mask = to_slots_mask[:ROWS]
    sent_own = jnp.any(own_mask & sent[None, :], axis=1)
    chosen_own = jnp.sum(jnp.where(own_mask, expert_ids[None, :], 0), axis=1)
    own_tokens = lax.dynamic_slice_in_dim(place, t * ROWS, ROWS, 0)
    from_slots_own = (own_tokens[:, None] == position[None, :]).astype(BF)

    def dispatch_z(rows):
        rows = jnp.where(sent_own[:, None], rows, 0).astype(BF)
        blocks = [rows[d * SUB : (d + 1) * SUB] for d in range(E)]
        arrived = [blocks[0]] + [over_z(blocks[d], d) for d in range(1, E)]
        return jnp.concatenate(arrived, axis=0)

    def dispatch_t(rows):
        return jnp.concatenate(gather_t(rows), axis=0)

    grad_output = mm(to_slots[:ROWS], cotangent_all, 1, 0)
    cotangent_z = dispatch_z(after(grad_output, columns))
    in_columns = exchange_weight(after(w_in, cotangent_z), z)
    out_columns = exchange_weight(after(w_out, in_columns), z)
    expert_cotangent = dispatch_t(cotangent_z)
    in_weight = join_weight(in_columns, r)
    out_weight = join_weight(out_columns, r)

    inputs_all = tokens_all.astype(F32)
    scale_all = norm_scale(inputs_all)
    normed_all = (inputs_all * scale_all * gain_one).astype(BF)
    qkv = mm(after(normed_all, cotangent_z), qkv_weight, 1, 0).astype(BF)
    table_rows = lax.dynamic_slice_in_dim(table_flat.astype(F32).reshape(H, NB), t * LH, LH, 0)
    bucket_table = (buckets[None, :] == jnp.arange(NB, dtype=jnp.int32)[:, None]).astype(F32)
    reversed_rel = jnp.dot(
        table_rows,
        jnp.pad(bucket_table[:, ::-1], ((0, 0), (0, 1))),
        precision=HIGHEST_PRECISION,
    )
    probs, heads_all = attend(qkv, reversed_rel, seq_length)
    heads_slots = mm(to_slots, heads_all, 1, 0).astype(BF)
    part = mm(heads_slots, attn_weight, 1, 1).astype(BF).reshape(T, ROWS, D)
    attended = scatter_t([part[k] for k in range(T)], in_columns)
    inputs = mm(to_slots[:ROWS], tokens_all, 1, 0)
    middle = inputs + attended
    scale_two = norm_scale(middle)
    normed_two = (middle * scale_two * gain_two).astype(BF)

    buffer = dispatch_t(dispatch_z(after(normed_two, out_columns)))

    def route_of(rows):
        return jax.nn.softmax(mm(rows, router_weight, 1, 0), axis=-1)

    experts = jnp.arange(E, dtype=jnp.int32)[None, :]
    expert_gate = jnp.sum(jnp.where(experts == z, route_of(buffer), 0.0), axis=-1)
    grad_expert = (expert_gate[:, None] * expert_cotangent.astype(F32)).astype(BF)
    pre_act = mm(buffer, in_weight, 1, 0)
    activation, gelu_pull = jax.vjp(jax.nn.gelu, pre_act)
    activation = activation.astype(BF)
    grad_act = mm(grad_expert, out_weight, 1, 0)
    grad_pre = gelu_pull(grad_act)[0].astype(BF)
    expert_out = mm(activation, out_weight, 1, 1).astype(BF)
    grad_buffer = mm(grad_pre, in_weight, 1, 1).astype(BF)
    both = jnp.concatenate([expert_out, grad_buffer], axis=1).reshape(T, ROWS, 2 * D)
    mine = scatter_t([both[k] for k in range(T)]).astype(BF)
    blocks = [mine[d * SUB : (d + 1) * SUB] for d in range(E)]
    returned = jnp.concatenate(
        [blocks[0]] + [over_z(blocks[d], d) for d in range(1, E)], axis=0
    ).astype(F32)
    combined, grad_normed_two = returned[:, :D], returned[:, D:]

    grad_out_terms = mm(grad_expert, activation, 0, 0).reshape(n, local, -1)
    grad_in_terms = mm(buffer, grad_pre, 0, 0).reshape(n, local, -1)
    out_sums = swap_terms(after(grad_out_terms, mine), r).astype(BF)
    in_sums = swap_terms(after(grad_in_terms, returned), r).astype(BF)

    route = route_of(normed_two)
    chosen = experts == chosen_own[:, None]
    gate = jnp.sum(jnp.where(chosen, route, 0.0), axis=-1)
    layer_rows = (middle + gate[:, None] * combined).astype(BF)
    grad_gate = jnp.sum(grad_output * combined, axis=-1)
    grad_logits = gate[:, None] * (chosen.astype(F32) - route) * grad_gate[:, None]
    grad_router = lax.dot_general(
        grad_logits,
        normed_two.astype(F32),
        (((0,), (0,)), ((), ())),
        precision=HIGHEST_PRECISION,
    )
    grad_normed_two = grad_normed_two + jnp.dot(
        grad_logits, router_weight.astype(F32).T, precision=HIGHEST_PRECISION
    )
    grad_gain_two = jnp.sum(grad_normed_two * middle * scale_two, axis=0)
    grad_middle = (grad_output + norm_back(grad_normed_two, middle, scale_two, gain_two)).astype(BF)
    grad_slots = jnp.concatenate(gather_t(grad_middle), axis=0)
    out_parts = deliver(after(out_sums, returned), z)
    layer_slots = jnp.concatenate(gather_t(after(layer_rows, grad_slots)), axis=0)
    layer_out = mm(from_slots_own, layer_slots, 1, 0).astype(BF)

    grad_attended = mm(to_slots, grad_slots, 0, 0).astype(BF)
    grad_heads = mm(grad_attended, attn_weight, 1, 0).astype(BF)
    grad_attn_weight = mm(grad_attended, heads_all, 0, 0)
    in_parts = deliver(after(in_sums, out_parts, grad_slots), z)
    early_sums = swap_terms(after(grad_attn_weight, in_sums).reshape(n, local, LW), r)
    grad_qkv, grad_rel = attend_back(qkv, probs, after(grad_heads, out_parts, in_sums))
    grad_normed_part = mm(grad_qkv, qkv_weight, 1, 1)
    grad_qkv_weight = mm(normed_all, grad_qkv, 0, 0)
    grad_gain_one = jnp.sum(grad_normed_part * inputs_all * scale_all, axis=0)
    part = natural(list(grad_normed_part.astype(BF).reshape(T, ROWS, D)), t)
    grad_normed_one = scatter_t(part, layer_slots)
    own_inputs = tokens.astype(F32)
    grad_tokens = mm(from_slots_own, grad_slots, 1, 0) + norm_back(
        grad_normed_one, own_inputs, norm_scale(own_inputs), gain_one
    )
    grad_table_rows = jnp.dot(
        grad_rel,
        jnp.pad(bucket_table, ((0, 0), (0, 1))).T,
        precision=HIGHEST_PRECISION,
    )
    grad_table = lax.dynamic_update_slice_in_dim(
        jnp.zeros((H, NB), F32), grad_table_rows, t * LH, 0
    ).reshape(-1)

    def sum_dp(sums):
        parts = deliver(sums.astype(BF), z)
        return pick(sums, z, 0) + sum(part.astype(F32) for part in parts[1:])

    late_sums = swap_terms(after(grad_qkv_weight, early_sums).reshape(n, local, 3 * LW), r)
    small = jnp.concatenate(
        [
            grad_router,
            grad_gain_two[None],
            grad_gain_one[None],
            jnp.pad(grad_table, (0, D - H * NB))[None],
            jnp.zeros((1, D), F32),
        ],
        axis=0,
    )
    small = sum_everywhere(small)
    early = sum_dp(after(early_sums, in_parts))
    late = sum_dp(after(late_sums, early))

    small_own = lax.dynamic_slice_in_dim(small[: E + 2], at_dp * local, local, 1)
    table_own = lax.dynamic_slice_in_dim(small[E + 2], at_dp * (H * NB // n), H * NB // n, 0)
    return (
        layer_out,
        grad_tokens,
        late.reshape(local, 3, LW),
        early,
        small_own[:E].T,
        jnp.stack(natural(in_parts, z), axis=1).astype(F32),
        jnp.stack(natural(out_parts, z), axis=1).astype(F32),
        small_own[E + 1],
        small_own[E],
        table_own,
    )


def solution(mesh):
    in_specs = (
        P(("dp", "tensor"), None),
        P(("dp", "tensor"), None),
        P("dp", None, "tensor"),
        P("dp", "tensor"),
        P("dp", None),
        P("dp", None, "tensor"),
        P("dp", None, "tensor"),
        P("dp"),
        P("dp"),
        P("dp"),
        P("dp"),
        P("dp"),
        P("dp"),
        P(),
    )
    out_specs = (
        P(("dp", "tensor"), None),
        P(("dp", "tensor"), None),
        P("dp", None, "tensor"),
        P("dp", "tensor"),
        P("dp", None),
        P("dp", None, "tensor"),
        P("dp", None, "tensor"),
        P("dp"),
        P("dp"),
        P("dp"),
    )
    return jax.shard_map(body, mesh=mesh, in_specs=in_specs, out_specs=out_specs, check_vma=False)
```

```python
import functools

import jax
import jax.numpy as jnp
from jax import lax
from jax.experimental import pallas as pl
from jax.experimental.pallas import tpu as pltpu
from jax.sharding import PartitionSpec as P

D = 768
H = 12
HD = 64
NB = 32
E = 4
SEQ = 512
CAP = 128
T = 4
LH = H // T
LW = LH * HD
ROWS = SEQ // T
SUB = CAP // T
SPAN = 2 * SEQ
TILE = 128
TILES = SEQ // TILE

EPSILON = 1e-06
HIGHEST_PRECISION = lax.Precision.HIGHEST
BF = jnp.bfloat16
F32 = jnp.float32


def mm(a, b, ca, cb):
    return lax.dot_general(a, b, (((ca,), (cb,)), ((), ())), preferred_element_type=F32)


def over_t(x, k):
    return lax.ppermute(x, "tensor", [(i, i ^ k) for i in range(T)])


def over_z(x, d):
    n = lax.axis_size("dp")
    r = n // E
    return lax.ppermute(x, "dp", [(i, ((i // r) ^ d) * r + i % r) for i in range(n)])


def over_r(x, c):
    n = lax.axis_size("dp")
    r = n // E
    return lax.ppermute(x, "dp", [(i, (i // r) * r + ((i % r) ^ c)) for i in range(n)])


def natural(parts, index):
    bit = 1
    while bit < len(parts):
        flip = (index & bit) != 0
        parts = [jnp.where(flip, parts[j ^ bit], parts[j]) for j in range(len(parts))]
        bit *= 2
    return parts


def gather_t(x):
    far = over_t(x, 2)
    return x, far, over_t(jnp.stack([x, far]), 1)


def in_order(gathered):
    own, far, near = gathered
    return [own, near[0], far, near[1]]


def scatter_t(kept, sent, *earlier):
    first = over_t(sent, 1).astype(F32)
    away = after((kept[1].astype(F32) + first[1]).astype(BF), *earlier)
    return kept[0].astype(F32) + first[0] + over_t(away, 2).astype(F32)


def pick(x, index, axis):
    return lax.dynamic_index_in_dim(x, index, axis, keepdims=False)


def after(x, *others):
    return lax.optimization_barrier((x, others))[0]


def swap_r(x):
    total = x[0].astype(F32)
    for c in range(1, x.shape[0]):
        total = total + over_r(x[c], c).astype(F32)
    return total


def deliver_z(x):
    return [x[0]] + [over_z(x[d], d) for d in range(1, E)]


def sum_everywhere(x, *earlier):
    R = lax.axis_size("dp") // E
    for k in (1, 2):
        x = x + over_t(x, k)
    x = after(x, *earlier)
    c = 1
    while c < R:
        x = x + over_r(x, c)
        c *= 2
    for d in (1, 2):
        x = x + over_z(x, d)
    return x


VMEM = pl.BlockSpec(memory_space=pltpu.VMEM)
SMEM = pl.BlockSpec(memory_space=pltpu.SMEM)
PARAMS = pltpu.CompilerParams(vmem_limit_bytes=48 * 2**20)


def call(kernel, name, micros, outs, scratch, at, *operands):
    moved = sum(a.size * a.dtype.itemsize for a in operands)
    return pl.pallas_call(
        kernel,
        out_shape=[jax.ShapeDtypeStruct(shape, kind) for shape, kind in outs],
        in_specs=[SMEM] + [VMEM] * len(operands),
        out_specs=[VMEM] * len(outs),
        scratch_shapes=[pltpu.VMEM(shape, kind) for shape, kind in scratch],
        compiler_params=PARAMS,
        cost_estimate=pl.CostEstimate(
            flops=micros * 10**9, bytes_accessed=moved, transcendentals=0
        ),
        name=name,
    )(at, *operands)


def block(index, length):
    return pl.ds(pl.multiple_of(index * length, length), length)


def place_rows(target, own_ref, far_ref, near_ref, t):
    for k, rows in ((0, own_ref[...]), (1, near_ref[0]), (2, far_ref[...]), (3, near_ref[1])):
        at = k if t is None else t ^ k
        target[block(at, ROWS), :] = rows


def place_weight(target, refs, at_ref, local):
    z, r, R = at_ref[0], at_ref[1], len(refs)
    for c in range(R):
        for d in range(E):
            target[block((z ^ d) * R + (r ^ c), local), :] = refs[c][d, :local, :]


def send_rows(source, out_ref, at_ref):
    R, _, local, _ = out_ref.shape
    for c in range(R):
        for d in range(E):
            at = block((at_ref[0] ^ d) * R + (at_ref[1] ^ c), local)
            out_ref[c, d] = source[at, :].astype(BF)


def attention_forward(
    at_ref,
    own_ref,
    far_ref,
    near_ref,
    gain_ref,
    rel_ref,
    slots_ref,
    *rest,
    pieces,
):
    refs, rest = rest[:pieces], rest[pieces:]
    normed_ref, qkv_ref, probs_ref, heads_ref, kept_ref, sent_ref, tokens_ref, weight_ref = rest
    t, length = at_ref[2], at_ref[3]
    if pieces == 1:
        weight_ref[...] = refs[0][...]
    else:
        place_weight(weight_ref, refs, at_ref, D // (pieces * E))
    place_rows(tokens_ref, own_ref, far_ref, near_ref, t)
    inputs = tokens_ref[...].astype(F32)
    normed_ref[...] = (inputs * norm_scale(inputs) * gain_ref[...]).astype(BF)
    qkv_ref[...] = mm(normed_ref[...], weight_ref[:, : 3 * LW], 1, 0).astype(BF)
    live = lax.broadcasted_iota(jnp.int32, (TILE, SEQ), 1) < length
    for h in range(LH):
        key = qkv_ref[:, LW + h * HD : LW + (h + 1) * HD]
        value = qkv_ref[:, 2 * LW + h * HD : 2 * LW + (h + 1) * HD]
        bias = jnp.broadcast_to(rel_ref[h : h + 1, :], (TILE, SPAN))
        for i in range(TILES):
            rows = slice(i * TILE, (i + 1) * TILE)
            query = qkv_ref[rows, h * HD : (h + 1) * HD]
            rolled = pltpu.roll(bias, SEQ + 1 + i * TILE, 1, stride=1, stride_axis=0)[:, :SEQ]
            scores = mm(query, key, 1, 1) * 0.125 + rolled
            scores = jnp.where(live, scores, -1e30)
            exponent = jnp.exp(scores - jnp.max(scores, axis=1, keepdims=True))
            probs = exponent / jnp.sum(exponent, axis=1, keepdims=True)
            probs_ref[h, rows, :] = probs
            heads_ref[rows, h * HD : (h + 1) * HD] = mm(probs.astype(BF), value, 1, 0).astype(BF)
    in_slots = mm(slots_ref[...], heads_ref[...], 1, 0).astype(BF)
    part = mm(in_slots, weight_ref[:, 3 * LW :], 1, 1).astype(BF)
    for k, out in ((0, kept_ref.at[0]), (1, sent_ref.at[0]), (2, kept_ref.at[1]), (3, sent_ref.at[1])):
        out[...] = part[k * ROWS : (k + 1) * ROWS]


def attention_backward(
    at_ref,
    own_ref,
    far_ref,
    near_ref,
    slots_ref,
    weight_ref,
    tokens_ref,
    normed_ref,
    qkv_ref,
    probs_ref,
    heads_ref,
    grads_ref,
    kept_ref,
    sent_ref,
    gain_ref,
    rel_ref,
    slot_scratch,
    heads_scratch,
    qkv_scratch,
    wide_scratch,
    weight_scratch,
):
    t = at_ref[2]
    place_rows(slot_scratch, own_ref, far_ref, near_ref, None)
    attended = mm(slots_ref[...], slot_scratch[...], 0, 0).astype(BF)
    heads_scratch[...] = mm(attended, weight_ref[:, 3 * LW :], 1, 0).astype(BF)
    weight_scratch[:, 3 * LW :] = mm(attended, heads_ref[...], 0, 0)
    flip = (
        lax.broadcasted_iota(jnp.int32, (TILE, TILE), 0)
        + lax.broadcasted_iota(jnp.int32, (TILE, TILE), 1)
        == TILE - 1
    ).astype(BF)
    rel_ref[...] = jnp.zeros_like(rel_ref)
    for h in range(LH):
        key = qkv_ref[:, LW + h * HD : LW + (h + 1) * HD]
        value = qkv_ref[:, 2 * LW + h * HD : 2 * LW + (h + 1) * HD]
        grad_key = jnp.zeros((SEQ, HD), F32)
        grad_value = jnp.zeros((SEQ, HD), F32)
        diagonal = [None] * (2 * TILES - 1)
        for i in range(TILES):
            rows = slice(i * TILE, (i + 1) * TILE)
            query = qkv_ref[rows, h * HD : (h + 1) * HD]
            grad = heads_scratch[rows, h * HD : (h + 1) * HD]
            probs = probs_ref[h, rows, :]
            grad_probs = mm(grad, value, 1, 1)
            inner = jnp.sum(probs * grad_probs, axis=1, keepdims=True)
            low = (probs * (grad_probs - inner)).astype(BF)
            qkv_scratch[rows, h * HD : (h + 1) * HD] = (mm(low, key, 1, 0) * 0.125).astype(BF)
            grad_key = grad_key + mm(low, query, 0, 0)
            grad_value = grad_value + mm(probs.astype(BF), grad, 0, 0)
            for j in range(TILES):
                turned = mm(low[:, j * TILE : (j + 1) * TILE], flip, 1, 0)
                at = i - j + TILES - 1
                diagonal[at] = turned if diagonal[at] is None else diagonal[at] + turned
        qkv_scratch[:, LW + h * HD : LW + (h + 1) * HD] = (grad_key * 0.125).astype(BF)
        qkv_scratch[:, 2 * LW + h * HD : 2 * LW + (h + 1) * HD] = grad_value.astype(BF)
        for at, part in enumerate(diagonal):
            wide = jnp.concatenate([part, jnp.zeros((TILE, TILE), F32)], axis=1)
            line = jnp.sum(pltpu.roll(wide, 0, 1, stride=1, stride_axis=0), axis=0, keepdims=True)
            rel_ref[h : h + 1, at * TILE : (at + 2) * TILE] += line
    weight_scratch[:, : 3 * LW] = mm(normed_ref[...], qkv_scratch[...], 0, 0)
    if len(grads_ref.shape) == 4:
        send_rows(weight_scratch, grads_ref, at_ref)
    else:
        grads_ref[...] = weight_scratch[...].astype(BF)
    wide_scratch[...] = mm(qkv_scratch[...], weight_ref[:, : 3 * LW], 1, 1)
    inputs = tokens_ref[...].astype(F32)
    gain_ref[...] = jnp.sum(
        wide_scratch[...] * inputs * norm_scale(inputs), axis=0, keepdims=True
    )
    for k, out in ((0, kept_ref.at[0]), (1, sent_ref.at[0]), (2, kept_ref.at[1]), (3, sent_ref.at[1])):
        out[...] = wide_scratch[block(t ^ k, ROWS), :].astype(BF)


def expert_layer(
    at_ref,
    own_ref,
    far_ref,
    near_ref,
    own_grad_ref,
    far_grad_ref,
    near_grad_ref,
    router_ref,
    *rest,
    pieces,
):
    in_refs, out_refs, rest = rest[:pieces], rest[pieces : 2 * pieces], rest[2 * pieces :]
    buffer_ref, grad_ref, activation_ref, grad_pre_ref, kept_ref, sent_ref, in_ref, out_ref = rest
    if pieces == 1:
        in_ref[...] = in_refs[0][...]
        out_ref[...] = out_refs[0][...]
    else:
        place_weight(in_ref, in_refs, at_ref, D // (pieces * E))
        place_weight(out_ref, out_refs, at_ref, D // (pieces * E))
    place_rows(buffer_ref, own_ref, far_ref, near_ref, None)
    place_rows(grad_ref, own_grad_ref, far_grad_ref, near_grad_ref, None)
    logits = mm(buffer_ref[...], router_ref[...], 1, 0)
    lane = lax.broadcasted_iota(jnp.int32, logits.shape, 1)
    logits = jnp.where(lane < E, logits, -1e30)
    exponent = jnp.exp(logits - jnp.max(logits, axis=1, keepdims=True))
    mine = jnp.sum(jnp.where(lane == at_ref[0], exponent, 0.0), axis=1, keepdims=True)
    gate = mine / jnp.sum(exponent, axis=1, keepdims=True)
    grad_ref[...] = (gate * grad_ref[...].astype(F32)).astype(BF)
    pre = mm(buffer_ref[...], in_ref[...], 1, 0)
    square = pre * pre
    tanh = jnp.tanh(0.7978845608028654 * (pre + 0.044715 * pre * square))
    half = 0.5 * (1.0 + tanh)
    activation_ref[...] = (pre * half).astype(BF)
    slope = half + 0.5 * pre * (1.0 - tanh * tanh) * (
        0.7978845608028654 * (1.0 + 3.0 * 0.044715 * square)
    )
    grad_act = mm(grad_ref[...], out_ref[...], 1, 0)
    grad_pre_ref[...] = (grad_act * slope).astype(BF)
    for k, out in ((0, kept_ref.at[0]), (1, sent_ref.at[0]), (2, kept_ref.at[1]), (3, sent_ref.at[1])):
        rows = slice(k * ROWS, (k + 1) * ROWS)
        out[:, :D] = mm(activation_ref[rows, :], out_ref[...], 1, 1).astype(BF)
        out[:, D:] = mm(grad_pre_ref[rows, :], in_ref[...], 1, 1).astype(BF)


def weight_gradient(at_ref, left_ref, right_ref, out_ref, scratch):
    scratch[...] = mm(left_ref[...], right_ref[...], 0, 0)
    if len(out_ref.shape) == 4:
        send_rows(scratch, out_ref, at_ref)
    else:
        out_ref[...] = scratch[...].astype(BF)


def norm_scale(values):
    return lax.rsqrt(jnp.mean(values * values, axis=-1, keepdims=True) + EPSILON)


def norm_back(grad, values, scale, gain):
    u = grad * gain
    inner = jnp.mean(u * values, axis=-1, keepdims=True)
    return scale * u - scale * scale * scale * values * inner


def body(
    tokens,
    cotangent,
    w_qkv,
    w_out_attn,
    w_router,
    w_in,
    w_out,
    norm1_gain,
    norm2_gain,
    bias_table,
    seq_length,
    expert_ids,
    expert_slots,
    buckets,
):
    n = lax.axis_size("dp")
    R = n // E
    at_dp = lax.axis_index("dp")
    z, r = at_dp // R, at_dp % R
    t = lax.axis_index("tensor")
    local = D // n
    width = w_in.shape[2]
    aligned = local % 16 == 0
    place_at = jnp.stack([z, r, t, seq_length[0]]).astype(jnp.int32)

    def whole(parts):
        if aligned:
            return [jnp.stack(part) if isinstance(part, list) else part for part in parts]
        rows = [jnp.stack(natural(list(part), z)) for part in parts]
        return [jnp.stack(natural(rows, r), axis=1).reshape(D, -1)]

    def blocks_to_send(grad):
        if aligned:
            return grad
        x = grad.reshape(E, R, local, -1)
        x = jnp.stack([pick(x, r ^ c, 1) for c in range(R)])
        return jnp.stack([pick(x, z ^ d, 1) for d in range(E)], axis=1)

    grads_shape = (R, E, local) if aligned else (D,)

    line = jnp.concatenate([w_router.T.reshape(-1), norm1_gain, norm2_gain, bias_table])
    line = jnp.pad(line, (0, -line.shape[0] % 128))[None]
    lines = lax.all_gather(line, "dp", axis=0, tiled=True)
    router_rows = lines[:, : local * E].reshape(n, E, local).transpose(1, 0, 2).reshape(E, D)
    gain_one = lines[:, local * E : local * (E + 1)].reshape(1, D).astype(F32)
    gain_two = lines[:, local * (E + 1) : local * (E + 2)].reshape(1, D).astype(F32)
    table_flat = lines[:, local * (E + 2) : local * (E + 2) + H * NB // n].reshape(-1)

    packed = jnp.concatenate([w_qkv.reshape(local, 3 * LW), w_out_attn], axis=1)
    packed_z = [packed] + [over_z(packed, d) for d in range(1, E)]
    packed_all = [packed_z] + [[over_r(part, c) for part in packed_z] for c in range(1, R)]

    both_parts = gather_t(jnp.concatenate([tokens, cotangent], axis=1))
    token_parts = [part[..., :D] for part in both_parts]
    cotangent_all = jnp.concatenate(natural([p[:, D:] for p in in_order(both_parts)], t), axis=0)

    sent = expert_slots >= 0
    absolute = jnp.where(sent, expert_ids * CAP + expert_slots, -1)
    position = jnp.arange(SEQ, dtype=jnp.int32)
    empty = ~jnp.any(absolute[None, :] == position[:, None], axis=1)
    before = position[None, :] <= position[:, None]
    empty_rank = jnp.sum((before & empty[None, :]).astype(jnp.int32), axis=1)
    unsent_rank = jnp.sum((before & ~sent[None, :]).astype(jnp.int32), axis=1)
    match = empty[None, :] & (empty_rank[None, :] == unsent_rank[:, None])
    spare = jnp.sum(jnp.where(match, position[None, :], 0), axis=1)
    slot = jnp.where(sent, absolute, spare)
    in_expert = slot % CAP
    place = ((in_expert // SUB) ^ t) * ROWS + ((slot // CAP) ^ z) * SUB + in_expert % SUB
    to_slots_mask = place[None, :] == position[:, None]
    to_slots = to_slots_mask.astype(BF)
    own_mask = to_slots_mask[:ROWS]
    sent_own = jnp.any(own_mask & sent[None, :], axis=1)
    chosen_own = jnp.sum(jnp.where(own_mask, expert_ids[None, :], 0), axis=1)
    own_tokens = lax.dynamic_slice_in_dim(place, t * ROWS, ROWS, 0)
    from_slots_own = (own_tokens[:, None] == position[None, :]).astype(BF)

    def dispatch_z(rows):
        rows = jnp.where(sent_own[:, None], rows, 0).astype(BF)
        return jnp.concatenate(deliver_z(rows.reshape(E, SUB, D)), axis=0)

    grad_output = mm(to_slots[:ROWS], cotangent_all, 1, 0)
    cotangent_z = dispatch_z(grad_output)
    in_parts = deliver_z(jnp.stack([pick(after(w_in, cotangent_z), z ^ d, 1) for d in range(E)]))
    out_parts = deliver_z(jnp.stack([pick(after(w_out, in_parts), z ^ d, 1) for d in range(E)]))
    in_columns, out_columns = jnp.stack(in_parts), jnp.stack(out_parts)
    in_weight = whole([in_columns] + [over_r(in_columns, c) for c in range(1, R)])
    out_weight = whole([out_columns] + [over_r(out_columns, c) for c in range(1, R)])
    cotangent_parts = gather_t(cotangent_z)

    table_rows = lax.dynamic_slice_in_dim(table_flat.astype(F32).reshape(H, NB), t * LH, LH, 0)
    bucket_table = (buckets[None, :] == jnp.arange(NB, dtype=jnp.int32)[:, None]).astype(F32)
    reversed_rel = jnp.dot(
        table_rows,
        jnp.pad(bucket_table[:, ::-1], ((0, 0), (0, 1))),
        precision=HIGHEST_PRECISION,
    )
    packed_refs = whole(packed_all)
    normed_all, qkv, probs, heads_all, kept, given, tokens_all, attention_weight = call(
        functools.partial(attention_forward, pieces=len(packed_refs)),
        "attention_forward",
        12,
        [
            ((SEQ, D), BF),
            ((SEQ, 3 * LW), BF),
            ((LH, SEQ, SEQ), F32),
            ((SEQ, LW), BF),
            ((2, ROWS, D), BF),
            ((2, ROWS, D), BF),
            ((SEQ, D), BF),
            ((D, 4 * LW), BF),
        ],
        [],
        place_at,
        *token_parts,
        gain_one,
        reversed_rel,
        after(to_slots, cotangent_z),
        *packed_refs,
    )
    attended = scatter_t(kept, after(given, in_columns, cotangent_parts[1]))
    inputs = mm(to_slots[:ROWS], tokens_all, 1, 0)
    middle = inputs + attended
    scale_two = norm_scale(middle)
    normed_two = (middle * scale_two * gain_two).astype(BF)

    buffer_parts = gather_t(dispatch_z(after(normed_two, out_columns, in_weight)))
    router = jnp.pad(router_rows.T, ((0, 0), (0, 128 - E)))
    buffer, grad_expert, activation, grad_pre, kept, given = call(
        functools.partial(expert_layer, pieces=len(in_weight)),
        "expert_layer",
        8,
        [
            ((SEQ, D), BF),
            ((SEQ, D), BF),
            ((SEQ, width), BF),
            ((SEQ, width), BF),
            ((2, ROWS, 2 * D), BF),
            ((2, ROWS, 2 * D), BF),
        ],
        [((D, width), BF), ((D, width), BF)],
        place_at,
        *buffer_parts,
        *cotangent_parts,
        router,
        *in_weight,
        *out_weight,
    )

    def expert_gradient(name, left, right):
        (out,) = call(
            weight_gradient,
            name,
            2,
            [((*grads_shape, width), BF)],
            [((D, width), F32)],
            place_at,
            left,
            right,
        )
        return blocks_to_send(out)

    out_terms = expert_gradient("grad_w_out", grad_expert, activation)
    in_terms = expert_gradient("grad_w_in", buffer, grad_pre)
    mine = scatter_t(kept, given).astype(BF)
    out_sums = swap_r(out_terms).astype(BF)
    returned = jnp.concatenate(deliver_z(mine.reshape(E, SUB, 2 * D)), axis=0).astype(F32)
    combined, grad_normed_two = returned[:, :D], returned[:, D:]
    in_sums = swap_r(after(in_terms, out_sums)).astype(BF)
    out_delivered = deliver_z(after(out_sums, returned))

    experts = jnp.arange(E, dtype=jnp.int32)[None, :]
    route = jax.nn.softmax(mm(normed_two, router_rows, 1, 1), axis=-1)
    chosen = experts == chosen_own[:, None]
    gate = jnp.sum(jnp.where(chosen, route, 0.0), axis=-1)
    layer_rows = (middle + gate[:, None] * combined).astype(BF)
    grad_gate = jnp.sum(grad_output * combined, axis=-1)
    grad_logits = gate[:, None] * (chosen.astype(F32) - route) * grad_gate[:, None]
    grad_router = lax.dot_general(
        grad_logits,
        normed_two.astype(F32),
        (((0,), (0,)), ((), ())),
        precision=HIGHEST_PRECISION,
    )
    grad_normed_two = grad_normed_two + jnp.dot(
        grad_logits, router_rows.astype(F32), precision=HIGHEST_PRECISION
    )
    grad_gain_two = jnp.sum(grad_normed_two * middle * scale_two, axis=0, keepdims=True)
    grad_middle = (grad_output + norm_back(grad_normed_two, middle, scale_two, gain_two)).astype(BF)
    grad_parts = gather_t(after(grad_middle, out_sums))
    layer_parts = gather_t(after(layer_rows, grad_parts))

    late_terms, kept, given, grad_gain_one, grad_rel = call(
        attention_backward,
        "attention_backward",
        12,
        [
            ((*grads_shape, 4 * LW), BF),
            ((2, ROWS, D), BF),
            ((2, ROWS, D), BF),
            ((1, D), F32),
            ((LH, SPAN), F32),
        ],
        [
            ((SEQ, D), BF),
            ((SEQ, LW), BF),
            ((SEQ, 3 * LW), BF),
            ((SEQ, D), F32),
            ((D, 4 * LW), F32),
        ],
        place_at,
        *grad_parts,
        after(to_slots, in_sums),
        attention_weight,
        tokens_all,
        normed_all,
        qkv,
        probs,
        heads_all,
    )
    in_delivered = deliver_z(after(in_sums, out_delivered, grad_parts))
    late_terms, kept, given, grad_gain_one, grad_rel = after(
        (late_terms, kept, given, grad_gain_one, grad_rel), in_delivered, layer_parts[1]
    )
    late_sums = swap_r(blocks_to_send(late_terms)).astype(BF)
    grad_normed_one = scatter_t(kept, given)
    own_inputs = tokens.astype(F32)
    grad_slots = jnp.concatenate(in_order(grad_parts), axis=0)
    grad_tokens = mm(from_slots_own, grad_slots, 1, 0) + norm_back(
        grad_normed_one, own_inputs, norm_scale(own_inputs), gain_one
    )
    layer_slots = jnp.concatenate(in_order(layer_parts), axis=0)
    layer_out = mm(from_slots_own, layer_slots, 1, 0).astype(BF)
    grad_table_rows = lax.dot_general(
        grad_rel[:, : 2 * SEQ - 1],
        bucket_table,
        (((1,), (1,)), ((), ())),
        precision=HIGHEST_PRECISION,
    )
    grad_table = lax.dynamic_update_slice_in_dim(
        jnp.zeros((H, NB), F32), grad_table_rows, t * LH, 0
    ).reshape(1, -1)
    small = sum_everywhere(
        jnp.concatenate(
            [
                grad_router,
                grad_gain_two,
                grad_gain_one,
                jnp.pad(grad_table, ((0, 0), (0, D - H * NB))),
                jnp.zeros((1, D), F32),
            ],
            axis=0,
        ),
        late_sums,
    )
    late_parts = deliver_z(late_sums)
    late = sum(part.astype(F32) for part in late_parts)
    small_own = lax.dynamic_slice_in_dim(small[: E + 2], at_dp * local, local, 1)
    table_own = lax.dynamic_slice_in_dim(small[E + 2], at_dp * (H * NB // n), H * NB // n, 0)
    return (
        layer_out,
        grad_tokens,
        late[:, : 3 * LW].reshape(local, 3, LW),
        late[:, 3 * LW :],
        small_own[:E].T,
        jnp.stack(natural(in_delivered, z), axis=1).astype(F32),
        jnp.stack(natural(out_delivered, z), axis=1).astype(F32),
        small_own[E + 1],
        small_own[E],
        table_own,
    )


def solution(mesh):
    in_specs = (
        P(("dp", "tensor"), None),
        P(("dp", "tensor"), None),
        P("dp", None, "tensor"),
        P("dp", "tensor"),
        P("dp", None),
        P("dp", None, "tensor"),
        P("dp", None, "tensor"),
        P("dp"),
        P("dp"),
        P("dp"),
        P("dp"),
        P("dp"),
        P("dp"),
        P(),
    )
    out_specs = (
        P(("dp", "tensor"), None),
        P(("dp", "tensor"), None),
        P("dp", None, "tensor"),
        P("dp", "tensor"),
        P("dp", None),
        P("dp", None, "tensor"),
        P("dp", None, "tensor"),
        P("dp"),
        P("dp"),
        P("dp"),
    )
    return jax.shard_map(body, mesh=mesh, in_specs=in_specs, out_specs=out_specs, check_vma=False)
```

```python
import functools

import jax
import jax.numpy as jnp
from jax import lax
from jax.experimental import pallas as pl
from jax.experimental.pallas import tpu as pltpu
from jax.sharding import PartitionSpec as P

D = 768
H = 12
HD = 64
NB = 32
E = 4
SEQ = 512
CAP = 128
T = 4
LH = H // T
LW = LH * HD
ROWS = SEQ // T
SUB = CAP // T
SPAN = 2 * SEQ
TILE = 128
TILES = SEQ // TILE

EPSILON = 1e-06
HIGHEST_PRECISION = lax.Precision.HIGHEST
BF = jnp.bfloat16
F32 = jnp.float32


def mm(a, b, ca, cb):
    return lax.dot_general(a, b, (((ca,), (cb,)), ((), ())), preferred_element_type=F32)


def over_t(x, k):
    return lax.ppermute(x, "tensor", [(i, i ^ k) for i in range(T)])


def over_z(x, d):
    n = lax.axis_size("dp")
    r = n // E
    return lax.ppermute(x, "dp", [(i, ((i // r) ^ d) * r + i % r) for i in range(n)])


def over_r(x, c):
    n = lax.axis_size("dp")
    r = n // E
    return lax.ppermute(x, "dp", [(i, (i // r) * r + ((i % r) ^ c)) for i in range(n)])


def natural(parts, index):
    bit = 1
    while bit < len(parts):
        flip = (index & bit) != 0
        parts = [jnp.where(flip, parts[j ^ bit], parts[j]) for j in range(len(parts))]
        bit *= 2
    return parts


def gather_t(x):
    far = over_t(x, 2)
    return x, far, over_t(jnp.stack([x, far]), 1)


def in_order(gathered):
    own, far, near = gathered
    return [own, near[0], far, near[1]]


def scatter_t(kept, sent, *earlier):
    first = over_t(sent, 1).astype(F32)
    away = after((kept[1].astype(F32) + first[1]).astype(BF), *earlier)
    return kept[0].astype(F32) + first[0] + over_t(away, 2).astype(F32)


def pick(x, index, axis):
    return lax.dynamic_index_in_dim(x, index, axis, keepdims=False)


def after(x, *others):
    return lax.optimization_barrier((x, others))[0]


def swap_r(x):
    total = x[0].astype(F32)
    for c in range(1, x.shape[0]):
        total = total + over_r(x[c], c).astype(F32)
    return total


def deliver_z(x):
    return [x[0]] + [over_z(x[d], d) for d in range(1, E)]


def sum_everywhere(x, *earlier):
    R = lax.axis_size("dp") // E
    for k in (1, 2):
        x = x + over_t(x, k)
    for d in (1, 2):
        x = x + over_z(x, d)
    x = after(x, *earlier)
    c = 1
    while c < R:
        x = x + over_r(x, c)
        c *= 2
    return x


def gather_lines(x, at_dp):
    R = lax.axis_size("dp") // E
    bit = 1
    while bit < E * R:
        other = over_r(x, bit) if bit < R else over_z(x, bit // R)
        upper = (at_dp & bit) != 0
        x = jnp.concatenate([jnp.where(upper, other, x), jnp.where(upper, x, other)], axis=0)
        bit *= 2
    return x


VMEM = pl.BlockSpec(memory_space=pltpu.VMEM)
SMEM = pl.BlockSpec(memory_space=pltpu.SMEM)
PARAMS = pltpu.CompilerParams(vmem_limit_bytes=48 * 2**20)


def call(kernel, name, micros, outs, scratch, at, *operands):
    moved = sum(a.size * a.dtype.itemsize for a in operands)
    return pl.pallas_call(
        kernel,
        out_shape=[jax.ShapeDtypeStruct(shape, kind) for shape, kind in outs],
        in_specs=[SMEM] + [VMEM] * len(operands),
        out_specs=[VMEM] * len(outs),
        scratch_shapes=[pltpu.VMEM(shape, kind) for shape, kind in scratch],
        compiler_params=PARAMS,
        cost_estimate=pl.CostEstimate(
            flops=micros * 10**9, bytes_accessed=moved, transcendentals=0
        ),
        name=name,
    )(at, *operands)


def block(index, length):
    return pl.ds(pl.multiple_of(index * length, length), length)


def place_rows(target, own_ref, far_ref, near_ref, t):
    for k, rows in ((0, own_ref[...]), (1, near_ref[0]), (2, far_ref[...]), (3, near_ref[1])):
        at = k if t is None else t ^ k
        target[block(at, ROWS), :] = rows


def place_weight(target, refs, at_ref, local):
    z, r, R = at_ref[0], at_ref[1], len(refs)
    for c in range(R):
        for d in range(E):
            target[block((z ^ d) * R + (r ^ c), local), :] = refs[c][d, :local, :]


def send_rows(source, out_ref, at_ref):
    R, _, local, _ = out_ref.shape
    for c in range(R):
        for d in range(E):
            at = block((at_ref[0] ^ d) * R + (at_ref[1] ^ c), local)
            out_ref[c, d] = source[at, :].astype(BF)


def attention_forward(
    at_ref,
    own_ref,
    far_ref,
    near_ref,
    gain_ref,
    rel_ref,
    slots_ref,
    *rest,
    pieces,
):
    refs, rest = rest[:pieces], rest[pieces:]
    normed_ref, qkv_ref, probs_ref, heads_ref, kept_ref, sent_ref, tokens_ref, weight_ref = rest
    t, length = at_ref[2], at_ref[3]
    if pieces == 1:
        weight_ref[...] = refs[0][...]
    else:
        place_weight(weight_ref, refs, at_ref, D // (pieces * E))
    place_rows(tokens_ref, own_ref, far_ref, near_ref, t)
    inputs = tokens_ref[...].astype(F32)
    normed_ref[...] = (inputs * norm_scale(inputs) * gain_ref[...]).astype(BF)
    qkv_ref[...] = mm(normed_ref[...], weight_ref[:, : 3 * LW], 1, 0).astype(BF)
    live = lax.broadcasted_iota(jnp.int32, (TILE, SEQ), 1) < length
    for h in range(LH):
        key = qkv_ref[:, LW + h * HD : LW + (h + 1) * HD]
        value = qkv_ref[:, 2 * LW + h * HD : 2 * LW + (h + 1) * HD]
        bias = jnp.broadcast_to(rel_ref[h : h + 1, :], (TILE, SPAN))
        for i in range(TILES):
            rows = slice(i * TILE, (i + 1) * TILE)
            query = qkv_ref[rows, h * HD : (h + 1) * HD]
            rolled = pltpu.roll(bias, SEQ + 1 + i * TILE, 1, stride=1, stride_axis=0)[:, :SEQ]
            scores = mm(query, key, 1, 1) * 0.125 + rolled
            scores = jnp.where(live, scores, -1e30)
            exponent = jnp.exp(scores - jnp.max(scores, axis=1, keepdims=True))
            probs = exponent / jnp.sum(exponent, axis=1, keepdims=True)
            probs_ref[h, rows, :] = probs
            heads_ref[rows, h * HD : (h + 1) * HD] = mm(probs.astype(BF), value, 1, 0).astype(BF)
    in_slots = mm(slots_ref[...], heads_ref[...], 1, 0).astype(BF)
    part = mm(in_slots, weight_ref[:, 3 * LW :], 1, 1).astype(BF)
    for k, out in ((0, kept_ref.at[0]), (1, sent_ref.at[0]), (2, kept_ref.at[1]), (3, sent_ref.at[1])):
        out[...] = part[k * ROWS : (k + 1) * ROWS]


def attention_backward(
    at_ref,
    own_ref,
    far_ref,
    near_ref,
    slots_ref,
    weight_ref,
    tokens_ref,
    normed_ref,
    qkv_ref,
    probs_ref,
    heads_ref,
    grads_ref,
    kept_ref,
    sent_ref,
    gain_ref,
    rel_ref,
    slot_scratch,
    heads_scratch,
    qkv_scratch,
    wide_scratch,
    weight_scratch,
):
    t = at_ref[2]
    place_rows(slot_scratch, own_ref, far_ref, near_ref, None)
    attended = mm(slots_ref[...], slot_scratch[...], 0, 0).astype(BF)
    heads_scratch[...] = mm(attended, weight_ref[:, 3 * LW :], 1, 0).astype(BF)
    weight_scratch[:, 3 * LW :] = mm(attended, heads_ref[...], 0, 0)
    flip = (
        lax.broadcasted_iota(jnp.int32, (TILE, TILE), 0)
        + lax.broadcasted_iota(jnp.int32, (TILE, TILE), 1)
        == TILE - 1
    ).astype(BF)
    rel_ref[...] = jnp.zeros_like(rel_ref)
    for h in range(LH):
        key = qkv_ref[:, LW + h * HD : LW + (h + 1) * HD]
        value = qkv_ref[:, 2 * LW + h * HD : 2 * LW + (h + 1) * HD]
        grad_key = jnp.zeros((SEQ, HD), F32)
        grad_value = jnp.zeros((SEQ, HD), F32)
        diagonal = [None] * (2 * TILES - 1)
        for i in range(TILES):
            rows = slice(i * TILE, (i + 1) * TILE)
            query = qkv_ref[rows, h * HD : (h + 1) * HD]
            grad = heads_scratch[rows, h * HD : (h + 1) * HD]
            probs = probs_ref[h, rows, :]
            grad_probs = mm(grad, value, 1, 1)
            inner = jnp.sum(probs * grad_probs, axis=1, keepdims=True)
            low = (probs * (grad_probs - inner)).astype(BF)
            qkv_scratch[rows, h * HD : (h + 1) * HD] = (mm(low, key, 1, 0) * 0.125).astype(BF)
            grad_key = grad_key + mm(low, query, 0, 0)
            grad_value = grad_value + mm(probs.astype(BF), grad, 0, 0)
            for j in range(TILES):
                turned = mm(low[:, j * TILE : (j + 1) * TILE], flip, 1, 0)
                at = i - j + TILES - 1
                diagonal[at] = turned if diagonal[at] is None else diagonal[at] + turned
        qkv_scratch[:, LW + h * HD : LW + (h + 1) * HD] = (grad_key * 0.125).astype(BF)
        qkv_scratch[:, 2 * LW + h * HD : 2 * LW + (h + 1) * HD] = grad_value.astype(BF)
        for at, part in enumerate(diagonal):
            wide = jnp.concatenate([part, jnp.zeros((TILE, TILE), F32)], axis=1)
            line = jnp.sum(pltpu.roll(wide, 0, 1, stride=1, stride_axis=0), axis=0, keepdims=True)
            rel_ref[h : h + 1, at * TILE : (at + 2) * TILE] += line
    weight_scratch[:, : 3 * LW] = mm(normed_ref[...], qkv_scratch[...], 0, 0)
    if len(grads_ref.shape) == 4:
        send_rows(weight_scratch, grads_ref, at_ref)
    else:
        grads_ref[...] = weight_scratch[...].astype(BF)
    wide_scratch[...] = mm(qkv_scratch[...], weight_ref[:, : 3 * LW], 1, 1)
    inputs = tokens_ref[...].astype(F32)
    gain_ref[...] = jnp.sum(
        wide_scratch[...] * inputs * norm_scale(inputs), axis=0, keepdims=True
    )
    for k, out in ((0, kept_ref.at[0]), (1, sent_ref.at[0]), (2, kept_ref.at[1]), (3, sent_ref.at[1])):
        out[...] = wide_scratch[block(t ^ k, ROWS), :].astype(BF)


def expert_layer(
    at_ref,
    own_ref,
    far_ref,
    near_ref,
    own_grad_ref,
    far_grad_ref,
    near_grad_ref,
    router_ref,
    *rest,
    pieces,
):
    in_refs, out_refs, rest = rest[:pieces], rest[pieces : 2 * pieces], rest[2 * pieces :]
    buffer_ref, grad_ref, activation_ref, grad_pre_ref, kept_ref, sent_ref, in_ref, out_ref = rest
    if pieces == 1:
        in_ref[...] = in_refs[0][...]
        out_ref[...] = out_refs[0][...]
    else:
        place_weight(in_ref, in_refs, at_ref, D // (pieces * E))
        place_weight(out_ref, out_refs, at_ref, D // (pieces * E))
    place_rows(buffer_ref, own_ref, far_ref, near_ref, None)
    place_rows(grad_ref, own_grad_ref, far_grad_ref, near_grad_ref, None)
    logits = mm(buffer_ref[...], router_ref[...], 1, 0)
    lane = lax.broadcasted_iota(jnp.int32, logits.shape, 1)
    logits = jnp.where(lane < E, logits, -1e30)
    exponent = jnp.exp(logits - jnp.max(logits, axis=1, keepdims=True))
    mine = jnp.sum(jnp.where(lane == at_ref[0], exponent, 0.0), axis=1, keepdims=True)
    gate = mine / jnp.sum(exponent, axis=1, keepdims=True)
    grad_ref[...] = (gate * grad_ref[...].astype(F32)).astype(BF)
    pre = mm(buffer_ref[...], in_ref[...], 1, 0)
    square = pre * pre
    tanh = jnp.tanh(0.7978845608028654 * (pre + 0.044715 * pre * square))
    half = 0.5 * (1.0 + tanh)
    activation_ref[...] = (pre * half).astype(BF)
    slope = half + 0.5 * pre * (1.0 - tanh * tanh) * (
        0.7978845608028654 * (1.0 + 3.0 * 0.044715 * square)
    )
    grad_act = mm(grad_ref[...], out_ref[...], 1, 0)
    grad_pre_ref[...] = (grad_act * slope).astype(BF)
    for k, out in ((0, kept_ref.at[0]), (1, sent_ref.at[0]), (2, kept_ref.at[1]), (3, sent_ref.at[1])):
        rows = slice(k * ROWS, (k + 1) * ROWS)
        out[:, :D] = mm(activation_ref[rows, :], out_ref[...], 1, 1).astype(BF)
        out[:, D:] = mm(grad_pre_ref[rows, :], in_ref[...], 1, 1).astype(BF)


def weight_gradient(at_ref, left_ref, right_ref, out_ref, scratch):
    scratch[...] = mm(left_ref[...], right_ref[...], 0, 0)
    if len(out_ref.shape) == 4:
        send_rows(scratch, out_ref, at_ref)
    else:
        out_ref[...] = scratch[...].astype(BF)


def norm_scale(values):
    return lax.rsqrt(jnp.mean(values * values, axis=-1, keepdims=True) + EPSILON)


def norm_back(grad, values, scale, gain):
    u = grad * gain
    inner = jnp.mean(u * values, axis=-1, keepdims=True)
    return scale * u - scale * scale * scale * values * inner


def body(
    tokens,
    cotangent,
    w_qkv,
    w_out_attn,
    w_router,
    w_in,
    w_out,
    norm1_gain,
    norm2_gain,
    bias_table,
    seq_length,
    expert_ids,
    expert_slots,
    buckets,
):
    n = lax.axis_size("dp")
    R = n // E
    at_dp = lax.axis_index("dp")
    z, r = at_dp // R, at_dp % R
    t = lax.axis_index("tensor")
    local = D // n
    width = w_in.shape[2]
    aligned = local % 16 == 0
    place_at = jnp.stack([z, r, t, seq_length[0]]).astype(jnp.int32)

    def whole(parts):
        if aligned:
            return [jnp.stack(part) if isinstance(part, list) else part for part in parts]
        rows = [jnp.stack(natural(list(part), z)) for part in parts]
        return [jnp.stack(natural(rows, r), axis=1).reshape(D, -1)]

    def blocks_to_send(grad):
        if aligned:
            return grad
        x = grad.reshape(E, R, local, -1)
        x = jnp.stack([pick(x, r ^ c, 1) for c in range(R)])
        return jnp.stack([pick(x, z ^ d, 1) for d in range(E)], axis=1)

    grads_shape = (R, E, local) if aligned else (D,)

    line = jnp.concatenate([w_router.T.reshape(-1), norm1_gain, norm2_gain, bias_table])
    line = jnp.pad(line, (0, -line.shape[0] % 128))[None]
    lines = gather_lines(line, at_dp)
    router_rows = lines[:, : local * E].reshape(n, E, local).transpose(1, 0, 2).reshape(E, D)
    gain_one = lines[:, local * E : local * (E + 1)].reshape(1, D).astype(F32)
    gain_two = lines[:, local * (E + 1) : local * (E + 2)].reshape(1, D).astype(F32)
    table_flat = lines[:, local * (E + 2) : local * (E + 2) + H * NB // n].reshape(-1)

    packed = jnp.concatenate([w_qkv.reshape(local, 3 * LW), w_out_attn], axis=1)
    packed_z = [packed] + [over_z(packed, d) for d in range(1, E)]
    packed_r = [over_r(packed, c) for c in range(1, R)]
    packed_rest = [over_r(jnp.stack(packed_z[1:]), c) for c in range(1, R)]
    packed_all = [packed_z] + [
        [first, *(rest[d] for d in range(E - 1))] for first, rest in zip(packed_r, packed_rest)
    ]

    both_parts = gather_t(jnp.concatenate([tokens, cotangent], axis=1))
    token_parts = [part[..., :D] for part in both_parts]
    cotangent_all = jnp.concatenate(natural([p[:, D:] for p in in_order(both_parts)], t), axis=0)

    sent = expert_slots >= 0
    absolute = jnp.where(sent, expert_ids * CAP + expert_slots, -1)
    position = jnp.arange(SEQ, dtype=jnp.int32)
    empty = ~jnp.any(absolute[None, :] == position[:, None], axis=1)
    before = position[None, :] <= position[:, None]
    empty_rank = jnp.sum((before & empty[None, :]).astype(jnp.int32), axis=1)
    unsent_rank = jnp.sum((before & ~sent[None, :]).astype(jnp.int32), axis=1)
    match = empty[None, :] & (empty_rank[None, :] == unsent_rank[:, None])
    spare = jnp.sum(jnp.where(match, position[None, :], 0), axis=1)
    slot = jnp.where(sent, absolute, spare)
    in_expert = slot % CAP
    place = ((in_expert // SUB) ^ t) * ROWS + ((slot // CAP) ^ z) * SUB + in_expert % SUB
    to_slots_mask = place[None, :] == position[:, None]
    to_slots = to_slots_mask.astype(BF)
    own_mask = to_slots_mask[:ROWS]
    sent_own = jnp.any(own_mask & sent[None, :], axis=1)
    chosen_own = jnp.sum(jnp.where(own_mask, expert_ids[None, :], 0), axis=1)
    own_tokens = lax.dynamic_slice_in_dim(place, t * ROWS, ROWS, 0)
    from_slots_own = (own_tokens[:, None] == position[None, :]).astype(BF)

    def dispatch_z(rows):
        rows = jnp.where(sent_own[:, None], rows, 0).astype(BF)
        return jnp.concatenate(deliver_z(rows.reshape(E, SUB, D)), axis=0)

    grad_output = mm(to_slots[:ROWS], cotangent_all, 1, 0)
    masked = jnp.where(sent_own[:, None], grad_output, 0).astype(BF).reshape(E, SUB, D)
    in_rows = after(w_in, packed_z, packed_r, both_parts)
    in_columns = jnp.stack(deliver_z(jnp.stack([pick(in_rows, z ^ d, 1) for d in range(E)])))
    out_rows = after(w_out, in_columns)
    out_rows = jnp.stack([pick(out_rows, z ^ d, 1) for d in range(E)])
    out_z = jnp.stack(deliver_z(jnp.concatenate([out_rows, masked], axis=1)))
    out_columns, cotangent_z = out_z[:, :local], out_z[:, local:].reshape(E * SUB, D)
    in_weight = whole([in_columns] + [over_r(in_columns, c) for c in range(1, R)])
    out_weight = whole([out_columns] + [over_r(out_columns, c) for c in range(1, R)])
    cotangent_parts = gather_t(cotangent_z)

    table_rows = lax.dynamic_slice_in_dim(table_flat.astype(F32).reshape(H, NB), t * LH, LH, 0)
    bucket_table = (buckets[None, :] == jnp.arange(NB, dtype=jnp.int32)[:, None]).astype(F32)
    reversed_rel = jnp.dot(
        table_rows,
        jnp.pad(bucket_table[:, ::-1], ((0, 0), (0, 1))),
        precision=HIGHEST_PRECISION,
    )
    packed_refs = whole(packed_all)
    forward = call(
        functools.partial(attention_forward, pieces=len(packed_refs)),
        "attention_forward",
        12,
        [
            ((SEQ, D), BF),
            ((SEQ, 3 * LW), BF),
            ((LH, SEQ, SEQ), F32),
            ((SEQ, LW), BF),
            ((2, ROWS, D), BF),
            ((2, ROWS, D), BF),
            ((SEQ, D), BF),
            ((D, 4 * LW), BF),
        ],
        [],
        place_at,
        *token_parts,
        gain_one,
        reversed_rel,
        to_slots,
        *packed_refs,
    )
    normed_all, qkv, probs, heads_all, kept, given, tokens_all, attention_weight = after(
        forward, in_columns
    )
    attended = scatter_t(kept, given)
    inputs = mm(to_slots[:ROWS], tokens_all, 1, 0)
    middle = inputs + attended
    scale_two = norm_scale(middle)
    normed_two = (middle * scale_two * gain_two).astype(BF)

    buffer_parts = gather_t(dispatch_z(after(normed_two, out_z, in_weight)))
    router = jnp.pad(router_rows.T, ((0, 0), (0, 128 - E)))
    buffer, grad_expert, activation, grad_pre, kept, given = call(
        functools.partial(expert_layer, pieces=len(in_weight)),
        "expert_layer",
        8,
        [
            ((SEQ, D), BF),
            ((SEQ, D), BF),
            ((SEQ, width), BF),
            ((SEQ, width), BF),
            ((2, ROWS, 2 * D), BF),
            ((2, ROWS, 2 * D), BF),
        ],
        [((D, width), BF), ((D, width), BF)],
        place_at,
        *buffer_parts,
        *cotangent_parts,
        router,
        *in_weight,
        *out_weight,
    )


    def expert_gradient(name, left, right):
        (out,) = call(
            weight_gradient,
            name,
            2,
            [((*grads_shape, width), BF)],
            [((D, width), F32)],
            place_at,
            left,
            right,
        )
        return blocks_to_send(out)

    out_terms = expert_gradient("grad_w_out", grad_expert, activation)
    in_terms = expert_gradient("grad_w_in", buffer, grad_pre)
    mine = scatter_t(kept, given).astype(BF)
    out_sums = swap_r(out_terms).astype(BF)
    in_sums = swap_r(after(in_terms, out_sums, mine)).astype(BF)
    returned = deliver_z(after(mine, out_sums).reshape(E, SUB, 2 * D))
    returned = jnp.concatenate(returned, axis=0).astype(F32)
    combined, grad_normed_two = returned[:, :D], returned[:, D:]

    experts = jnp.arange(E, dtype=jnp.int32)[None, :]
    route = jax.nn.softmax(mm(normed_two, router_rows, 1, 1), axis=-1)
    chosen = experts == chosen_own[:, None]
    gate = jnp.sum(jnp.where(chosen, route, 0.0), axis=-1)
    layer_rows = (middle + gate[:, None] * combined).astype(BF)
    grad_gate = jnp.sum(grad_output * combined, axis=-1)
    grad_logits = gate[:, None] * (chosen.astype(F32) - route) * grad_gate[:, None]
    grad_router = lax.dot_general(
        grad_logits,
        normed_two.astype(F32),
        (((0,), (0,)), ((), ())),
        precision=HIGHEST_PRECISION,
    )
    grad_normed_two = grad_normed_two + jnp.dot(
        grad_logits, router_rows.astype(F32), precision=HIGHEST_PRECISION
    )
    grad_gain_two = jnp.sum(grad_normed_two * middle * scale_two, axis=0, keepdims=True)
    grad_middle = (grad_output + norm_back(grad_normed_two, middle, scale_two, gain_two)).astype(BF)
    grad_parts = gather_t(after(grad_middle, in_sums))
    layer_parts = gather_t(after(layer_rows, grad_parts))

    late_terms, kept, given, grad_gain_one, grad_rel = call(
        attention_backward,
        "attention_backward",
        12,
        [
            ((*grads_shape, 4 * LW), BF),
            ((2, ROWS, D), BF),
            ((2, ROWS, D), BF),
            ((1, D), F32),
            ((LH, SPAN), F32),
        ],
        [
            ((SEQ, D), BF),
            ((SEQ, LW), BF),
            ((SEQ, 3 * LW), BF),
            ((SEQ, D), F32),
            ((D, 4 * LW), F32),
        ],
        place_at,
        *grad_parts,
        to_slots,
        attention_weight,
        tokens_all,
        normed_all,
        qkv,
        probs,
        heads_all,
    )
    expert_sums = jnp.stack([in_sums, out_sums], axis=1)
    delivered = deliver_z(after(expert_sums, grad_middle))
    late_terms, kept, given, grad_gain_one, grad_rel, delivered = after(
        (late_terms, kept, given, grad_gain_one, grad_rel, delivered), layer_parts[1]
    )
    late_terms = blocks_to_send(late_terms)
    far_sums = swap_r(late_terms[:, 2:]).astype(BF)
    near_sums = swap_r(after(late_terms[:, :2], far_sums)).astype(BF)
    grad_normed_one = scatter_t(kept, given)
    own_inputs = tokens.astype(F32)
    grad_slots = jnp.concatenate(in_order(grad_parts), axis=0)
    grad_tokens = mm(from_slots_own, grad_slots, 1, 0) + norm_back(
        grad_normed_one, own_inputs, norm_scale(own_inputs), gain_one
    )
    layer_slots = jnp.concatenate(in_order(layer_parts), axis=0)
    layer_out = mm(from_slots_own, layer_slots, 1, 0).astype(BF)
    grad_table_rows = lax.dot_general(
        grad_rel[:, : 2 * SEQ - 1],
        bucket_table,
        (((1,), (1,)), ((), ())),
        precision=HIGHEST_PRECISION,
    )
    grad_table = lax.dynamic_update_slice_in_dim(
        jnp.zeros((H, NB), F32), grad_table_rows, t * LH, 0
    ).reshape(1, -1)
    small = sum_everywhere(
        jnp.concatenate(
            [
                grad_router,
                grad_gain_two,
                grad_gain_one,
                jnp.pad(grad_table, ((0, 0), (0, D - H * NB))),
                jnp.zeros((1, D), F32),
            ],
            axis=0,
        ),
        far_sums,
    )
    late = near_sums[0].astype(F32)
    for d, part in ((2, far_sums[0]), (3, far_sums[1]), (1, near_sums[1])):
        late = late + over_z(part, d).astype(F32)
    small_own = lax.dynamic_slice_in_dim(small[: E + 2], at_dp * local, local, 1)
    table_own = lax.dynamic_slice_in_dim(small[E + 2], at_dp * (H * NB // n), H * NB // n, 0)
    return (
        layer_out,
        grad_tokens,
        late[:, : 3 * LW].reshape(local, 3, LW),
        late[:, 3 * LW :],
        small_own[:E].T,
        jnp.stack(natural([part[0] for part in delivered], z), axis=1).astype(F32),
        jnp.stack(natural([part[1] for part in delivered], z), axis=1).astype(F32),
        small_own[E + 1],
        small_own[E],
        table_own,
    )


def solution(mesh):
    in_specs = (
        P(("dp", "tensor"), None),
        P(("dp", "tensor"), None),
        P("dp", None, "tensor"),
        P("dp", "tensor"),
        P("dp", None),
        P("dp", None, "tensor"),
        P("dp", None, "tensor"),
        P("dp"),
        P("dp"),
        P("dp"),
        P("dp"),
        P("dp"),
        P("dp"),
        P(),
    )
    out_specs = (
        P(("dp", "tensor"), None),
        P(("dp", "tensor"), None),
        P("dp", None, "tensor"),
        P("dp", "tensor"),
        P("dp", None),
        P("dp", None, "tensor"),
        P("dp", None, "tensor"),
        P("dp"),
        P("dp"),
        P("dp"),
    )
    return jax.shard_map(body, mesh=mesh, in_specs=in_specs, out_specs=out_specs, check_vma=False)
```

```python
import functools

import jax
import jax.numpy as jnp
from jax import lax
from jax.experimental import pallas as pl
from jax.experimental.pallas import tpu as pltpu
from jax.sharding import PartitionSpec as P

D = 768
H = 12
HD = 64
NB = 32
E = 4
SEQ = 512
CAP = 128
T = 4
LH = H // T
LW = LH * HD
ROWS = SEQ // T
SUB = CAP // T
SPAN = 2 * SEQ
TILE = 128
TILES = SEQ // TILE

EPSILON = 1e-06
HIGHEST_PRECISION = lax.Precision.HIGHEST
BF = jnp.bfloat16
F32 = jnp.float32


def mm(a, b, ca, cb):
    return lax.dot_general(a, b, (((ca,), (cb,)), ((), ())), preferred_element_type=F32)


def over_t(x, k):
    return lax.ppermute(x, "tensor", [(i, i ^ k) for i in range(T)])


def over_z(x, d):
    n = lax.axis_size("dp")
    r = n // E
    return lax.ppermute(x, "dp", [(i, ((i // r) ^ d) * r + i % r) for i in range(n)])


def over_r(x, c):
    n = lax.axis_size("dp")
    r = n // E
    return lax.ppermute(x, "dp", [(i, (i // r) * r + ((i % r) ^ c)) for i in range(n)])


def natural(parts, index):
    bit = 1
    while bit < len(parts):
        flip = (index & bit) != 0
        parts = [jnp.where(flip, parts[j ^ bit], parts[j]) for j in range(len(parts))]
        bit *= 2
    return parts


def gather_t(x, *earlier):
    far = over_t(x, 2)
    return x, far, over_t(after(jnp.stack([x, far]), *earlier), 1)


def in_order(gathered):
    own, far, near = gathered
    return [own, near[0], far, near[1]]


def scatter_t(kept, sent, *earlier):
    first = over_t(sent, 1).astype(F32)
    away = after((kept[1].astype(F32) + first[1]).astype(BF), *earlier)
    return kept[0].astype(F32) + first[0] + over_t(away, 2).astype(F32)


def pick(x, index, axis):
    return lax.dynamic_index_in_dim(x, index, axis, keepdims=False)


def after(x, *others):
    return lax.optimization_barrier((x, others))[0]


def swap_r(x):
    return [x[0]] + [over_r(x[c], c) for c in range(1, x.shape[0])]


def add(terms):
    return sum(term.astype(F32) for term in terms)


def deliver_z(x):
    return [x[0]] + [over_z(x[d], d) for d in range(1, E)]


def sum_but_z(x):
    R = lax.axis_size("dp") // E
    c = 1
    while c < R:
        x = x + over_r(x, c)
        c *= 2
    for k in (1, 2):
        x = x + over_t(x, k)
    return x


VMEM = pl.BlockSpec(memory_space=pltpu.VMEM)
SMEM = pl.BlockSpec(memory_space=pltpu.SMEM)
PARAMS = pltpu.CompilerParams(vmem_limit_bytes=48 * 2**20)


def call(kernel, name, micros, outs, scratch, at, *operands):
    moved = sum(a.size * a.dtype.itemsize for a in operands)
    return pl.pallas_call(
        kernel,
        out_shape=[jax.ShapeDtypeStruct(shape, kind) for shape, kind in outs],
        in_specs=[SMEM] + [VMEM] * len(operands),
        out_specs=[VMEM] * len(outs),
        scratch_shapes=[pltpu.VMEM(shape, kind) for shape, kind in scratch],
        compiler_params=PARAMS,
        cost_estimate=pl.CostEstimate(
            flops=micros * 10**9, bytes_accessed=moved, transcendentals=0
        ),
        name=name,
    )(at, *operands)


def block(index, length):
    return pl.ds(pl.multiple_of(index * length, length), length)


def place_rows(target, own_ref, far_ref, near_ref, t):
    for k, rows in ((0, own_ref[...]), (1, near_ref[0]), (2, far_ref[...]), (3, near_ref[1])):
        at = k if t is None else t ^ k
        target[block(at, ROWS), :] = rows


def place_weight(target, refs, at_ref, local):
    z, r, R = at_ref[0], at_ref[1], len(refs)
    for c in range(R):
        for d in range(E):
            target[block((z ^ d) * R + (r ^ c), local), :] = refs[c][d, :local, :]


def send_rows(source, out_ref, at_ref):
    R, _, local, _ = out_ref.shape
    for c in range(R):
        for d in range(E):
            at = block((at_ref[0] ^ d) * R + (at_ref[1] ^ c), local)
            out_ref[c, d] = source[at, :].astype(BF)


def attention_forward(
    at_ref,
    own_ref,
    far_ref,
    near_ref,
    gain_ref,
    rel_ref,
    slots_ref,
    *rest,
    pieces,
):
    refs, rest = rest[:pieces], rest[pieces:]
    normed_ref, qkv_ref, probs_ref, heads_ref, kept_ref, sent_ref, tokens_ref, weight_ref = rest
    t, length = at_ref[2], at_ref[3]
    if pieces == 1:
        weight_ref[...] = refs[0][...]
    else:
        place_weight(weight_ref, refs, at_ref, D // (pieces * E))
    place_rows(tokens_ref, own_ref, far_ref, near_ref, t)
    inputs = tokens_ref[...].astype(F32)
    normed_ref[...] = (inputs * norm_scale(inputs) * gain_ref[...]).astype(BF)
    qkv_ref[...] = mm(normed_ref[...], weight_ref[:, : 3 * LW], 1, 0).astype(BF)
    live = lax.broadcasted_iota(jnp.int32, (TILE, SEQ), 1) < length
    for h in range(LH):
        key = qkv_ref[:, LW + h * HD : LW + (h + 1) * HD]
        value = qkv_ref[:, 2 * LW + h * HD : 2 * LW + (h + 1) * HD]
        bias = jnp.broadcast_to(rel_ref[h : h + 1, :], (TILE, SPAN))
        for i in range(TILES):
            rows = slice(i * TILE, (i + 1) * TILE)
            query = qkv_ref[rows, h * HD : (h + 1) * HD]
            rolled = pltpu.roll(bias, SEQ + 1 + i * TILE, 1, stride=1, stride_axis=0)[:, :SEQ]
            scores = mm(query, key, 1, 1) * 0.125 + rolled
            scores = jnp.where(live, scores, -1e30)
            exponent = jnp.exp(scores - jnp.max(scores, axis=1, keepdims=True))
            probs = exponent / jnp.sum(exponent, axis=1, keepdims=True)
            probs_ref[h, rows, :] = probs
            heads_ref[rows, h * HD : (h + 1) * HD] = mm(probs.astype(BF), value, 1, 0).astype(BF)
    in_slots = mm(slots_ref[...], heads_ref[...], 1, 0).astype(BF)
    part = mm(in_slots, weight_ref[:, 3 * LW :], 1, 1).astype(BF)
    for k, out in ((0, kept_ref.at[0]), (1, sent_ref.at[0]), (2, kept_ref.at[1]), (3, sent_ref.at[1])):
        out[...] = part[k * ROWS : (k + 1) * ROWS]


def attention_backward(
    at_ref,
    own_ref,
    far_ref,
    near_ref,
    slots_ref,
    weight_ref,
    tokens_ref,
    normed_ref,
    qkv_ref,
    probs_ref,
    heads_ref,
    grads_ref,
    kept_ref,
    sent_ref,
    gain_ref,
    rel_ref,
    slot_scratch,
    heads_scratch,
    qkv_scratch,
    wide_scratch,
    weight_scratch,
):
    t = at_ref[2]
    place_rows(slot_scratch, own_ref, far_ref, near_ref, None)
    attended = mm(slots_ref[...], slot_scratch[...], 0, 0).astype(BF)
    heads_scratch[...] = mm(attended, weight_ref[:, 3 * LW :], 1, 0).astype(BF)
    weight_scratch[:, 3 * LW :] = mm(attended, heads_ref[...], 0, 0)
    flip = (
        lax.broadcasted_iota(jnp.int32, (TILE, TILE), 0)
        + lax.broadcasted_iota(jnp.int32, (TILE, TILE), 1)
        == TILE - 1
    ).astype(BF)
    rel_ref[...] = jnp.zeros_like(rel_ref)
    for h in range(LH):
        key = qkv_ref[:, LW + h * HD : LW + (h + 1) * HD]
        value = qkv_ref[:, 2 * LW + h * HD : 2 * LW + (h + 1) * HD]
        grad_key = jnp.zeros((SEQ, HD), F32)
        grad_value = jnp.zeros((SEQ, HD), F32)
        diagonal = [None] * (2 * TILES - 1)
        for i in range(TILES):
            rows = slice(i * TILE, (i + 1) * TILE)
            query = qkv_ref[rows, h * HD : (h + 1) * HD]
            grad = heads_scratch[rows, h * HD : (h + 1) * HD]
            probs = probs_ref[h, rows, :]
            grad_probs = mm(grad, value, 1, 1)
            inner = jnp.sum(probs * grad_probs, axis=1, keepdims=True)
            low = (probs * (grad_probs - inner)).astype(BF)
            qkv_scratch[rows, h * HD : (h + 1) * HD] = (mm(low, key, 1, 0) * 0.125).astype(BF)
            grad_key = grad_key + mm(low, query, 0, 0)
            grad_value = grad_value + mm(probs.astype(BF), grad, 0, 0)
            for j in range(TILES):
                turned = mm(low[:, j * TILE : (j + 1) * TILE], flip, 1, 0)
                at = i - j + TILES - 1
                diagonal[at] = turned if diagonal[at] is None else diagonal[at] + turned
        qkv_scratch[:, LW + h * HD : LW + (h + 1) * HD] = (grad_key * 0.125).astype(BF)
        qkv_scratch[:, 2 * LW + h * HD : 2 * LW + (h + 1) * HD] = grad_value.astype(BF)
        for at, part in enumerate(diagonal):
            wide = jnp.concatenate([part, jnp.zeros((TILE, TILE), F32)], axis=1)
            line = jnp.sum(pltpu.roll(wide, 0, 1, stride=1, stride_axis=0), axis=0, keepdims=True)
            rel_ref[h : h + 1, at * TILE : (at + 2) * TILE] += line
    weight_scratch[:, : 3 * LW] = mm(normed_ref[...], qkv_scratch[...], 0, 0)
    if len(grads_ref.shape) == 4:
        send_rows(weight_scratch, grads_ref, at_ref)
    else:
        grads_ref[...] = weight_scratch[...].astype(BF)
    wide_scratch[...] = mm(qkv_scratch[...], weight_ref[:, : 3 * LW], 1, 1)
    inputs = tokens_ref[...].astype(F32)
    gain_ref[...] = jnp.sum(
        wide_scratch[...] * inputs * norm_scale(inputs), axis=0, keepdims=True
    )
    for k, out in ((0, kept_ref.at[0]), (1, sent_ref.at[0]), (2, kept_ref.at[1]), (3, sent_ref.at[1])):
        out[...] = wide_scratch[block(t ^ k, ROWS), :].astype(BF)


def expert_layer(
    at_ref,
    own_ref,
    far_ref,
    near_ref,
    own_grad_ref,
    far_grad_ref,
    near_grad_ref,
    router_ref,
    *rest,
    pieces,
):
    in_refs, out_refs, rest = rest[:pieces], rest[pieces : 2 * pieces], rest[2 * pieces :]
    buffer_ref, grad_ref, activation_ref, grad_pre_ref, kept_ref, sent_ref, in_ref, out_ref = rest
    if pieces == 1:
        in_ref[...] = in_refs[0][...]
        out_ref[...] = out_refs[0][...]
    else:
        place_weight(in_ref, in_refs, at_ref, D // (pieces * E))
        place_weight(out_ref, out_refs, at_ref, D // (pieces * E))
    place_rows(buffer_ref, own_ref, far_ref, near_ref, None)
    place_rows(grad_ref, own_grad_ref, far_grad_ref, near_grad_ref, None)
    logits = mm(buffer_ref[...], router_ref[...], 1, 0)
    lane = lax.broadcasted_iota(jnp.int32, logits.shape, 1)
    logits = jnp.where(lane < E, logits, -1e30)
    exponent = jnp.exp(logits - jnp.max(logits, axis=1, keepdims=True))
    mine = jnp.sum(jnp.where(lane == at_ref[0], exponent, 0.0), axis=1, keepdims=True)
    gate = mine / jnp.sum(exponent, axis=1, keepdims=True)
    grad_ref[...] = (gate * grad_ref[...].astype(F32)).astype(BF)
    pre = mm(buffer_ref[...], in_ref[...], 1, 0)
    square = pre * pre
    tanh = jnp.tanh(0.7978845608028654 * (pre + 0.044715 * pre * square))
    half = 0.5 * (1.0 + tanh)
    activation_ref[...] = (pre * half).astype(BF)
    slope = half + 0.5 * pre * (1.0 - tanh * tanh) * (
        0.7978845608028654 * (1.0 + 3.0 * 0.044715 * square)
    )
    grad_act = mm(grad_ref[...], out_ref[...], 1, 0)
    grad_pre_ref[...] = (grad_act * slope).astype(BF)
    for k, out in ((0, kept_ref.at[0]), (1, sent_ref.at[0]), (2, kept_ref.at[1]), (3, sent_ref.at[1])):
        rows = slice(k * ROWS, (k + 1) * ROWS)
        out[:, :D] = mm(activation_ref[rows, :], out_ref[...], 1, 1).astype(BF)
        out[:, D:] = mm(grad_pre_ref[rows, :], in_ref[...], 1, 1).astype(BF)


def weight_gradient(at_ref, left_ref, right_ref, out_ref, scratch):
    scratch[...] = mm(left_ref[...], right_ref[...], 0, 0)
    if len(out_ref.shape) == 4:
        send_rows(scratch, out_ref, at_ref)
    else:
        out_ref[...] = scratch[...].astype(BF)


def norm_scale(values):
    return lax.rsqrt(jnp.mean(values * values, axis=-1, keepdims=True) + EPSILON)


def norm_back(grad, values, scale, gain):
    u = grad * gain
    inner = jnp.mean(u * values, axis=-1, keepdims=True)
    return scale * u - scale * scale * scale * values * inner


def body(
    tokens,
    cotangent,
    w_qkv,
    w_out_attn,
    w_router,
    w_in,
    w_out,
    norm1_gain,
    norm2_gain,
    bias_table,
    seq_length,
    expert_ids,
    expert_slots,
    buckets,
):
    n = lax.axis_size("dp")
    R = n // E
    at_dp = lax.axis_index("dp")
    z, r = at_dp // R, at_dp % R
    t = lax.axis_index("tensor")
    local = D // n
    width = w_in.shape[2]
    aligned = local % 16 == 0
    place_at = jnp.stack([z, r, t, seq_length[0]]).astype(jnp.int32)

    def whole(parts):
        if aligned:
            return [jnp.stack(part) if isinstance(part, list) else part for part in parts]
        rows = [jnp.stack(natural(list(part), z)) for part in parts]
        return [jnp.stack(natural(rows, r), axis=1).reshape(D, -1)]

    def blocks_to_send(grad):
        if aligned:
            return grad
        x = grad.reshape(E, R, local, -1)
        x = jnp.stack([pick(x, r ^ c, 1) for c in range(R)])
        return jnp.stack([pick(x, z ^ d, 1) for d in range(E)], axis=1)

    grads_shape = (R, E, local) if aligned else (D,)

    line = jnp.concatenate([w_router.T.reshape(-1), norm1_gain, norm2_gain, bias_table])
    line = jnp.pad(line, (0, 4 * LW - line.shape[0]))[None]
    packed = jnp.concatenate(
        [jnp.concatenate([w_qkv.reshape(local, 3 * LW), w_out_attn], axis=1), line], axis=0
    )
    packed_z = [packed] + [over_z(packed, d) for d in range(1, E)]
    packed_r = [
        [over_r(packed, c), *over_r(jnp.stack([part[:local] for part in packed_z[1:]]), c)]
        for c in range(1, R)
    ]
    packed_all = [[part[:local] for part in parts] for parts in [packed_z] + packed_r]
    lines = jnp.stack(natural([part[local] for part in packed_z], z))
    lines = [lines] + [over_r(lines, c) for c in range(1, R)]
    lines = jnp.stack(natural(lines, r), axis=1).reshape(n, -1)
    router_rows = lines[:, : local * E].reshape(n, E, local).transpose(1, 0, 2).reshape(E, D)
    gain_one = lines[:, local * E : local * (E + 1)].reshape(1, D).astype(F32)
    gain_two = lines[:, local * (E + 1) : local * (E + 2)].reshape(1, D).astype(F32)
    table_flat = lines[:, local * (E + 2) : local * (E + 2) + H * NB // n].reshape(-1)

    both_parts = gather_t(jnp.concatenate([tokens, cotangent], axis=1))
    token_parts = [part[..., :D] for part in both_parts]
    cotangent_all = jnp.concatenate(natural([p[:, D:] for p in in_order(both_parts)], t), axis=0)

    sent = expert_slots >= 0
    absolute = jnp.where(sent, expert_ids * CAP + expert_slots, -1)
    position = jnp.arange(SEQ, dtype=jnp.int32)
    empty = ~jnp.any(absolute[None, :] == position[:, None], axis=1)
    before = position[None, :] <= position[:, None]
    empty_rank = jnp.sum((before & empty[None, :]).astype(jnp.int32), axis=1)
    unsent_rank = jnp.sum((before & ~sent[None, :]).astype(jnp.int32), axis=1)
    match = empty[None, :] & (empty_rank[None, :] == unsent_rank[:, None])
    spare = jnp.sum(jnp.where(match, position[None, :], 0), axis=1)
    slot = jnp.where(sent, absolute, spare)
    in_expert = slot % CAP
    place = ((in_expert // SUB) ^ t) * ROWS + ((slot // CAP) ^ z) * SUB + in_expert % SUB
    to_slots_mask = place[None, :] == position[:, None]
    to_slots = to_slots_mask.astype(BF)
    own_mask = to_slots_mask[:ROWS]
    sent_own = jnp.any(own_mask & sent[None, :], axis=1)
    chosen_own = jnp.sum(jnp.where(own_mask, expert_ids[None, :], 0), axis=1)
    own_tokens = lax.dynamic_slice_in_dim(place, t * ROWS, ROWS, 0)
    from_slots_own = (own_tokens[:, None] == position[None, :]).astype(BF)

    def dispatch_z(rows):
        rows = jnp.where(sent_own[:, None], rows, 0).astype(BF)
        return jnp.concatenate(deliver_z(rows.reshape(E, SUB, D)), axis=0)

    grad_output = mm(to_slots[:ROWS], cotangent_all, 1, 0)
    masked = jnp.where(sent_own[:, None], grad_output, 0).astype(BF).reshape(E, SUB, D)
    in_rows = after(w_in, packed_z)
    in_columns = jnp.stack(deliver_z(jnp.stack([pick(in_rows, z ^ d, 1) for d in range(E)])))
    out_rows = after(w_out, in_columns)
    out_rows = jnp.stack([pick(out_rows, z ^ d, 1) for d in range(E)])
    out_z = jnp.stack(deliver_z(jnp.concatenate([out_rows, masked], axis=1)))
    out_columns, cotangent_z = out_z[:, :local], out_z[:, local:].reshape(E * SUB, D)
    in_weight = whole([in_columns] + [over_r(in_columns, c) for c in range(1, R)])
    out_weight = whole([out_columns] + [over_r(out_columns, c) for c in range(1, R)])
    cotangent_parts = gather_t(cotangent_z)

    table_rows = lax.dynamic_slice_in_dim(table_flat.astype(F32).reshape(H, NB), t * LH, LH, 0)
    bucket_table = (buckets[None, :] == jnp.arange(NB, dtype=jnp.int32)[:, None]).astype(F32)
    reversed_rel = jnp.dot(
        table_rows,
        jnp.pad(bucket_table[:, ::-1], ((0, 0), (0, 1))),
        precision=HIGHEST_PRECISION,
    )
    packed_refs = whole(packed_all)
    forward = call(
        functools.partial(attention_forward, pieces=len(packed_refs)),
        "attention_forward",
        12,
        [
            ((SEQ, D), BF),
            ((SEQ, 3 * LW), BF),
            ((LH, SEQ, SEQ), F32),
            ((SEQ, LW), BF),
            ((2, ROWS, D), BF),
            ((2, ROWS, D), BF),
            ((SEQ, D), BF),
            ((D, 4 * LW), BF),
        ],
        [],
        place_at,
        *token_parts,
        gain_one,
        reversed_rel,
        after(to_slots, in_columns),
        *packed_refs,
    )
    normed_all, qkv, probs, heads_all, kept, given, tokens_all, attention_weight = forward
    attended = scatter_t(kept, given)
    inputs = mm(to_slots[:ROWS], tokens_all, 1, 0)
    middle = inputs + attended
    scale_two = norm_scale(middle)
    normed_two = (middle * scale_two * gain_two).astype(BF)

    buffer_parts = gather_t(dispatch_z(after(normed_two, out_z, in_weight)), out_weight)
    router = jnp.pad(router_rows.T, ((0, 0), (0, 128 - E)))
    buffer, grad_expert, activation, grad_pre, kept, given = call(
        functools.partial(expert_layer, pieces=len(in_weight)),
        "expert_layer",
        8,
        [
            ((SEQ, D), BF),
            ((SEQ, D), BF),
            ((SEQ, width), BF),
            ((SEQ, width), BF),
            ((2, ROWS, 2 * D), BF),
            ((2, ROWS, 2 * D), BF),
        ],
        [((D, width), BF), ((D, width), BF)],
        place_at,
        *buffer_parts,
        *cotangent_parts,
        router,
        *in_weight,
        *out_weight,
    )


    def expert_gradient(name, left, right):
        (out,) = call(
            weight_gradient,
            name,
            2,
            [((*grads_shape, width), BF)],
            [((D, width), F32)],
            place_at,
            left,
            right,
        )
        return blocks_to_send(out)

    out_terms = expert_gradient("grad_w_out", grad_expert, activation)
    in_terms = expert_gradient("grad_w_in", buffer, grad_pre)
    mine = scatter_t(kept, given).astype(BF)
    out_sums = add(swap_r(out_terms)).astype(BF)
    in_sums = add(swap_r(after(in_terms, out_sums, mine))).astype(BF)
    returned = deliver_z(after(mine, out_sums).reshape(E, SUB, 2 * D))
    returned = jnp.concatenate(returned, axis=0).astype(F32)
    combined, grad_normed_two = returned[:, :D], returned[:, D:]

    experts = jnp.arange(E, dtype=jnp.int32)[None, :]
    route = jax.nn.softmax(mm(normed_two, router_rows, 1, 1), axis=-1)
    chosen = experts == chosen_own[:, None]
    gate = jnp.sum(jnp.where(chosen, route, 0.0), axis=-1)
    layer_rows = (middle + gate[:, None] * combined).astype(BF)
    grad_gate = jnp.sum(grad_output * combined, axis=-1)
    grad_logits = gate[:, None] * (chosen.astype(F32) - route) * grad_gate[:, None]
    grad_router = lax.dot_general(
        grad_logits,
        normed_two.astype(F32),
        (((0,), (0,)), ((), ())),
        precision=HIGHEST_PRECISION,
    )
    grad_normed_two = grad_normed_two + jnp.dot(
        grad_logits, router_rows.astype(F32), precision=HIGHEST_PRECISION
    )
    grad_gain_two = jnp.sum(grad_normed_two * middle * scale_two, axis=0, keepdims=True)
    grad_middle = (grad_output + norm_back(grad_normed_two, middle, scale_two, gain_two)).astype(BF)
    grad_parts = gather_t(grad_middle, in_sums)
    layer_parts = gather_t(after(layer_rows, grad_parts))

    late_terms, kept, given, grad_gain_one, grad_rel = call(
        attention_backward,
        "attention_backward",
        12,
        [
            ((*grads_shape, 4 * LW), BF),
            ((2, ROWS, D), BF),
            ((2, ROWS, D), BF),
            ((1, D), F32),
            ((LH, SPAN), F32),
        ],
        [
            ((SEQ, D), BF),
            ((SEQ, LW), BF),
            ((SEQ, 3 * LW), BF),
            ((SEQ, D), F32),
            ((D, 4 * LW), F32),
        ],
        place_at,
        *grad_parts,
        to_slots,
        attention_weight,
        tokens_all,
        normed_all,
        qkv,
        probs,
        heads_all,
    )
    expert_sums = jnp.stack([in_sums, out_sums], axis=1)
    delivered = deliver_z(after(expert_sums, grad_middle))
    late_terms, kept, given, grad_gain_one, grad_rel, delivered = after(
        (late_terms, kept, given, grad_gain_one, grad_rel, delivered), layer_parts[1]
    )
    late_terms = blocks_to_send(late_terms)
    far_sums = add(swap_r(late_terms[:, 2:])).astype(BF)
    near_terms = swap_r(after(late_terms[:, :2], far_sums))
    grad_normed_one = scatter_t(kept, given)
    own_inputs = tokens.astype(F32)
    grad_slots = jnp.concatenate(in_order(grad_parts), axis=0)
    grad_tokens = mm(from_slots_own, grad_slots, 1, 0) + norm_back(
        grad_normed_one, own_inputs, norm_scale(own_inputs), gain_one
    )
    layer_slots = jnp.concatenate(in_order(layer_parts), axis=0)
    layer_out = mm(from_slots_own, layer_slots, 1, 0).astype(BF)
    grad_table_rows = lax.dot_general(
        grad_rel[:, : 2 * SEQ - 1],
        bucket_table,
        (((1,), (1,)), ((), ())),
        precision=HIGHEST_PRECISION,
    )
    grad_table = lax.dynamic_update_slice_in_dim(
        jnp.zeros((H, NB), F32), grad_table_rows, t * LH, 0
    ).reshape(1, -1)
    small = sum_but_z(
        jnp.concatenate(
            [
                grad_router,
                grad_gain_two,
                grad_gain_one,
                jnp.pad(grad_table, ((0, 0), (0, D - H * NB))),
                jnp.zeros((1, D), F32),
            ],
            axis=0,
        )
    )
    low = small.astype(BF)
    far = [over_z(jnp.concatenate([far_sums[d - 2], low], axis=0), d) for d in (2, 3)]
    near_sums = add(after(near_terms, far))
    near = over_z(jnp.concatenate([near_sums[1].astype(BF), low], axis=0), 1)
    late = jnp.concatenate([near_sums[0], small], axis=0)
    late = late + far[0].astype(F32) + far[1].astype(F32) + near.astype(F32)
    late, small = late[:local], late[local:]
    small_own = lax.dynamic_slice_in_dim(small[: E + 2], at_dp * local, local, 1)
    table_own = lax.dynamic_slice_in_dim(small[E + 2], at_dp * (H * NB // n), H * NB // n, 0)
    return (
        layer_out,
        grad_tokens,
        late[:, : 3 * LW].reshape(local, 3, LW),
        late[:, 3 * LW :],
        small_own[:E].T,
        jnp.stack(natural([part[0] for part in delivered], z), axis=1).astype(F32),
        jnp.stack(natural([part[1] for part in delivered], z), axis=1).astype(F32),
        small_own[E + 1],
        small_own[E],
        table_own,
    )


def solution(mesh):
    in_specs = (
        P(("dp", "tensor"), None),
        P(("dp", "tensor"), None),
        P("dp", None, "tensor"),
        P("dp", "tensor"),
        P("dp", None),
        P("dp", None, "tensor"),
        P("dp", None, "tensor"),
        P("dp"),
        P("dp"),
        P("dp"),
        P("dp"),
        P("dp"),
        P("dp"),
        P(),
    )
    out_specs = (
        P(("dp", "tensor"), None),
        P(("dp", "tensor"), None),
        P("dp", None, "tensor"),
        P("dp", "tensor"),
        P("dp", None),
        P("dp", None, "tensor"),
        P("dp", None, "tensor"),
        P("dp"),
        P("dp"),
        P("dp"),
    )
    return jax.shard_map(body, mesh=mesh, in_specs=in_specs, out_specs=out_specs, check_vma=False)
```

```python
import functools

import jax
import jax.numpy as jnp
from jax import lax
from jax.experimental import pallas as pl
from jax.experimental.pallas import tpu as pltpu
from jax.sharding import PartitionSpec as P

D = 768
H = 12
HD = 64
NB = 32
E = 4
SEQ = 512
CAP = 128
T = 4
LH = H // T
LW = LH * HD
ROWS = SEQ // T
SUB = CAP // T
SPAN = 2 * SEQ
TILE = 128
TILES = SEQ // TILE

EPSILON = 1e-06
HIGHEST_PRECISION = lax.Precision.HIGHEST
BF = jnp.bfloat16
F32 = jnp.float32


def mm(a, b, ca, cb):
    return lax.dot_general(a, b, (((ca,), (cb,)), ((), ())), preferred_element_type=F32)


def over_t(x, k):
    return lax.ppermute(x, "tensor", [(i, i ^ k) for i in range(T)])


def over_z(x, d):
    n = lax.axis_size("dp")
    r = n // E
    return lax.ppermute(x, "dp", [(i, ((i // r) ^ d) * r + i % r) for i in range(n)])


def over_r(x, c):
    n = lax.axis_size("dp")
    r = n // E
    return lax.ppermute(x, "dp", [(i, (i // r) * r + ((i % r) ^ c)) for i in range(n)])


def natural(parts, index):
    bit = 1
    while bit < len(parts):
        flip = (index & bit) != 0
        parts = [jnp.where(flip, parts[j ^ bit], parts[j]) for j in range(len(parts))]
        bit *= 2
    return parts


def gather_t(x, *earlier):
    far = over_t(x, 2)
    return x, far, over_t(after(jnp.stack([x, far]), *earlier), 1)


def in_order(gathered):
    own, far, near = gathered
    return [own, near[0], far, near[1]]


def scatter_t(kept, sent, *earlier):
    first = over_t(sent, 1).astype(F32)
    away = after((kept[1].astype(F32) + first[1]).astype(BF), *earlier)
    return kept[0].astype(F32) + first[0] + over_t(away, 2).astype(F32)


def pick(x, index, axis):
    return lax.dynamic_index_in_dim(x, index, axis, keepdims=False)


def after(x, *others):
    return lax.optimization_barrier((x, others))[0]


def swap_r(x):
    return [x[0]] + [over_r(x[c], c) for c in range(1, x.shape[0])]


def add(terms):
    return sum(term.astype(F32) for term in terms)


def deliver_z(x):
    return [x[0]] + [over_z(x[d], d) for d in range(1, E)]


def sum_but_z(x):
    R = lax.axis_size("dp") // E
    c = 1
    while c < R:
        x = x + over_r(x, c)
        c *= 2
    for k in (1, 2):
        x = x + over_t(x, k)
    return x


VMEM = pl.BlockSpec(memory_space=pltpu.VMEM)
SMEM = pl.BlockSpec(memory_space=pltpu.SMEM)
PARAMS = pltpu.CompilerParams(vmem_limit_bytes=48 * 2**20)


def call(kernel, name, micros, outs, scratch, at, *operands):
    moved = sum(a.size * a.dtype.itemsize for a in operands)
    return pl.pallas_call(
        kernel,
        out_shape=[jax.ShapeDtypeStruct(shape, kind) for shape, kind in outs],
        in_specs=[SMEM] + [VMEM] * len(operands),
        out_specs=[VMEM] * len(outs),
        scratch_shapes=[pltpu.VMEM(shape, kind) for shape, kind in scratch],
        compiler_params=PARAMS,
        cost_estimate=pl.CostEstimate(
            flops=micros * 10**9, bytes_accessed=moved, transcendentals=0
        ),
        name=name,
    )(at, *operands)


def block(index, length):
    return pl.ds(pl.multiple_of(index * length, length), length)


def place_rows(target, own_ref, far_ref, near_ref, t):
    for k, rows in ((0, own_ref[...]), (1, near_ref[0]), (2, far_ref[...]), (3, near_ref[1])):
        at = k if t is None else t ^ k
        target[block(at, ROWS), :] = rows


def place_weight(target, refs, at_ref):
    pieces = []
    for ref in refs:
        pieces += [ref] if len(ref.shape) == 2 else [ref.at[i] for i in range(ref.shape[0])]
    z, r, R = at_ref[0], at_ref[1], len(pieces) // E
    local = D // len(pieces)
    for c in range(R):
        for d in range(E):
            at = block((z ^ d) * R + (r ^ c), local)
            target[at, :] = pieces[c * E + d][:local, :]


def load_weight(target, refs, at_ref):
    if refs[0].shape == target.shape:
        target[...] = refs[0][...]
    else:
        place_weight(target, refs, at_ref)


def send_rows(source, out_ref, at_ref):
    R, _, local, _ = out_ref.shape
    for c in range(R):
        for d in range(E):
            at = block((at_ref[0] ^ d) * R + (at_ref[1] ^ c), local)
            out_ref[c, d] = source[at, :].astype(BF)


def attention_forward(
    at_ref,
    own_ref,
    far_ref,
    near_ref,
    gain_ref,
    rel_ref,
    slots_ref,
    *rest,
    pieces,
):
    refs, rest = rest[:pieces], rest[pieces:]
    normed_ref, qkv_ref, probs_ref, heads_ref, kept_ref, sent_ref, tokens_ref, weight_ref = rest
    t, length = at_ref[2], at_ref[3]
    load_weight(weight_ref, refs, at_ref)
    place_rows(tokens_ref, own_ref, far_ref, near_ref, t)
    inputs = tokens_ref[...].astype(F32)
    normed_ref[...] = (inputs * norm_scale(inputs) * gain_ref[...]).astype(BF)
    qkv_ref[...] = mm(normed_ref[...], weight_ref[:, : 3 * LW], 1, 0).astype(BF)
    live = lax.broadcasted_iota(jnp.int32, (TILE, SEQ), 1) < length
    for h in range(LH):
        key = qkv_ref[:, LW + h * HD : LW + (h + 1) * HD]
        value = qkv_ref[:, 2 * LW + h * HD : 2 * LW + (h + 1) * HD]
        bias = jnp.broadcast_to(rel_ref[h : h + 1, :], (TILE, SPAN))
        for i in range(TILES):
            rows = slice(i * TILE, (i + 1) * TILE)
            query = qkv_ref[rows, h * HD : (h + 1) * HD]
            rolled = pltpu.roll(bias, SEQ + 1 + i * TILE, 1, stride=1, stride_axis=0)[:, :SEQ]
            scores = mm(query, key, 1, 1) * 0.125 + rolled
            scores = jnp.where(live, scores, -1e30)
            exponent = jnp.exp(scores - jnp.max(scores, axis=1, keepdims=True))
            probs = exponent / jnp.sum(exponent, axis=1, keepdims=True)
            probs_ref[h, rows, :] = probs
            heads_ref[rows, h * HD : (h + 1) * HD] = mm(probs.astype(BF), value, 1, 0).astype(BF)
    in_slots = mm(slots_ref[...], heads_ref[...], 1, 0).astype(BF)
    part = mm(in_slots, weight_ref[:, 3 * LW :], 1, 1).astype(BF)
    for k, out in ((0, kept_ref.at[0]), (1, sent_ref.at[0]), (2, kept_ref.at[1]), (3, sent_ref.at[1])):
        out[...] = part[k * ROWS : (k + 1) * ROWS]


def attention_backward(
    at_ref,
    own_ref,
    far_ref,
    near_ref,
    slots_ref,
    weight_ref,
    tokens_ref,
    normed_ref,
    qkv_ref,
    probs_ref,
    heads_ref,
    grads_ref,
    kept_ref,
    sent_ref,
    gain_ref,
    rel_ref,
    slot_scratch,
    heads_scratch,
    qkv_scratch,
    wide_scratch,
    weight_scratch,
):
    t = at_ref[2]
    place_rows(slot_scratch, own_ref, far_ref, near_ref, None)
    attended = mm(slots_ref[...], slot_scratch[...], 0, 0).astype(BF)
    heads_scratch[...] = mm(attended, weight_ref[:, 3 * LW :], 1, 0).astype(BF)
    weight_scratch[:, 3 * LW :] = mm(attended, heads_ref[...], 0, 0)
    flip = (
        lax.broadcasted_iota(jnp.int32, (TILE, TILE), 0)
        + lax.broadcasted_iota(jnp.int32, (TILE, TILE), 1)
        == TILE - 1
    ).astype(BF)
    rel_ref[...] = jnp.zeros_like(rel_ref)
    for h in range(LH):
        key = qkv_ref[:, LW + h * HD : LW + (h + 1) * HD]
        value = qkv_ref[:, 2 * LW + h * HD : 2 * LW + (h + 1) * HD]
        grad_key = jnp.zeros((SEQ, HD), F32)
        grad_value = jnp.zeros((SEQ, HD), F32)
        diagonal = [None] * (2 * TILES - 1)
        for i in range(TILES):
            rows = slice(i * TILE, (i + 1) * TILE)
            query = qkv_ref[rows, h * HD : (h + 1) * HD]
            grad = heads_scratch[rows, h * HD : (h + 1) * HD]
            probs = probs_ref[h, rows, :]
            grad_probs = mm(grad, value, 1, 1)
            inner = jnp.sum(probs * grad_probs, axis=1, keepdims=True)
            low = (probs * (grad_probs - inner)).astype(BF)
            qkv_scratch[rows, h * HD : (h + 1) * HD] = (mm(low, key, 1, 0) * 0.125).astype(BF)
            grad_key = grad_key + mm(low, query, 0, 0)
            grad_value = grad_value + mm(probs.astype(BF), grad, 0, 0)
            for j in range(TILES):
                turned = mm(low[:, j * TILE : (j + 1) * TILE], flip, 1, 0)
                at = i - j + TILES - 1
                diagonal[at] = turned if diagonal[at] is None else diagonal[at] + turned
        qkv_scratch[:, LW + h * HD : LW + (h + 1) * HD] = (grad_key * 0.125).astype(BF)
        qkv_scratch[:, 2 * LW + h * HD : 2 * LW + (h + 1) * HD] = grad_value.astype(BF)
        for at, part in enumerate(diagonal):
            wide = jnp.concatenate([part, jnp.zeros((TILE, TILE), F32)], axis=1)
            line = jnp.sum(pltpu.roll(wide, 0, 1, stride=1, stride_axis=0), axis=0, keepdims=True)
            rel_ref[h : h + 1, at * TILE : (at + 2) * TILE] += line
    weight_scratch[:, : 3 * LW] = mm(normed_ref[...], qkv_scratch[...], 0, 0)
    if len(grads_ref.shape) == 4:
        send_rows(weight_scratch, grads_ref, at_ref)
    else:
        grads_ref[...] = weight_scratch[...].astype(BF)
    wide_scratch[...] = mm(qkv_scratch[...], weight_ref[:, : 3 * LW], 1, 1)
    inputs = tokens_ref[...].astype(F32)
    gain_ref[...] = jnp.sum(
        wide_scratch[...] * inputs * norm_scale(inputs), axis=0, keepdims=True
    )
    for k, out in ((0, kept_ref.at[0]), (1, sent_ref.at[0]), (2, kept_ref.at[1]), (3, sent_ref.at[1])):
        out[...] = wide_scratch[block(t ^ k, ROWS), :].astype(BF)


def expert_layer(
    at_ref,
    own_ref,
    far_ref,
    near_ref,
    own_grad_ref,
    far_grad_ref,
    near_grad_ref,
    router_ref,
    *rest,
    pieces,
):
    in_refs, out_refs, rest = rest[:pieces], rest[pieces : 2 * pieces], rest[2 * pieces :]
    buffer_ref, grad_ref, activation_ref, grad_pre_ref, kept_ref, sent_ref, in_ref, out_ref = rest
    load_weight(in_ref, in_refs, at_ref)
    load_weight(out_ref, out_refs, at_ref)
    place_rows(buffer_ref, own_ref, far_ref, near_ref, None)
    place_rows(grad_ref, own_grad_ref, far_grad_ref, near_grad_ref, None)
    logits = mm(buffer_ref[...], router_ref[...], 1, 0)
    lane = lax.broadcasted_iota(jnp.int32, logits.shape, 1)
    logits = jnp.where(lane < E, logits, -1e30)
    exponent = jnp.exp(logits - jnp.max(logits, axis=1, keepdims=True))
    mine = jnp.sum(jnp.where(lane == at_ref[0], exponent, 0.0), axis=1, keepdims=True)
    gate = mine / jnp.sum(exponent, axis=1, keepdims=True)
    grad_ref[...] = (gate * grad_ref[...].astype(F32)).astype(BF)
    pre = mm(buffer_ref[...], in_ref[...], 1, 0)
    square = pre * pre
    tanh = jnp.tanh(0.7978845608028654 * (pre + 0.044715 * pre * square))
    half = 0.5 * (1.0 + tanh)
    activation_ref[...] = (pre * half).astype(BF)
    slope = half + 0.5 * pre * (1.0 - tanh * tanh) * (
        0.7978845608028654 * (1.0 + 3.0 * 0.044715 * square)
    )
    grad_act = mm(grad_ref[...], out_ref[...], 1, 0)
    grad_pre_ref[...] = (grad_act * slope).astype(BF)
    for k, out in ((0, kept_ref.at[0]), (1, sent_ref.at[0]), (2, kept_ref.at[1]), (3, sent_ref.at[1])):
        rows = slice(k * ROWS, (k + 1) * ROWS)
        out[:, :D] = mm(activation_ref[rows, :], out_ref[...], 1, 1).astype(BF)
        out[:, D:] = mm(grad_pre_ref[rows, :], in_ref[...], 1, 1).astype(BF)


def weight_gradient(at_ref, left_ref, right_ref, out_ref, scratch):
    scratch[...] = mm(left_ref[...], right_ref[...], 0, 0)
    if len(out_ref.shape) == 4:
        send_rows(scratch, out_ref, at_ref)
    else:
        out_ref[...] = scratch[...].astype(BF)


def norm_scale(values):
    return lax.rsqrt(jnp.mean(values * values, axis=-1, keepdims=True) + EPSILON)


def norm_back(grad, values, scale, gain):
    u = grad * gain
    inner = jnp.mean(u * values, axis=-1, keepdims=True)
    return scale * u - scale * scale * scale * values * inner


def body(
    tokens,
    cotangent,
    w_qkv,
    w_out_attn,
    w_router,
    w_in,
    w_out,
    norm1_gain,
    norm2_gain,
    bias_table,
    seq_length,
    expert_ids,
    expert_slots,
    buckets,
):
    n = lax.axis_size("dp")
    R = n // E
    at_dp = lax.axis_index("dp")
    z, r = at_dp // R, at_dp % R
    t = lax.axis_index("tensor")
    local = D // n
    width = w_in.shape[2]
    aligned = local % 16 == 0
    place_at = jnp.stack([z, r, t, seq_length[0]]).astype(jnp.int32)

    def whole(parts):
        if aligned:
            return parts
        pieces = []
        for part in parts:
            pieces += [part] if part.ndim == 2 else list(part)
        pieces = [piece[:local] for piece in pieces]
        rows = [jnp.stack(natural(pieces[c * E : (c + 1) * E], z)) for c in range(R)]
        return [jnp.stack(natural(rows, r), axis=1).reshape(D, -1)]

    def blocks_to_send(grad):
        if aligned:
            return grad
        x = grad.reshape(E, R, local, -1)
        x = jnp.stack([pick(x, r ^ c, 1) for c in range(R)])
        return jnp.stack([pick(x, z ^ d, 1) for d in range(E)], axis=1)

    grads_shape = (R, E, local) if aligned else (D,)

    line = jnp.concatenate([w_router.T.reshape(-1), norm1_gain, norm2_gain, bias_table])
    line = jnp.pad(line, (0, 4 * LW - line.shape[0]))[None]
    packed = jnp.concatenate(
        [jnp.concatenate([w_qkv.reshape(local, 3 * LW), w_out_attn], axis=1), line], axis=0
    )
    packed_z = [packed] + [over_z(packed, d) for d in range(1, E)]
    packed_own = [over_r(packed, c) for c in range(1, R)]
    packed_rest = after(jnp.stack([part[:local] for part in packed_z[1:]]), packed_own)
    packed_all = list(packed_z)
    for c in range(1, R):
        packed_all += [packed_own[c - 1], over_r(packed_rest, c)]
    lines = jnp.stack(natural([part[local] for part in packed_z], z))
    lines = [lines] + [over_r(lines, c) for c in range(1, R)]
    lines = jnp.stack(natural(lines, r), axis=1).reshape(n, -1)
    router_rows = lines[:, : local * E].reshape(n, E, local).transpose(1, 0, 2).reshape(E, D)
    gain_one = lines[:, local * E : local * (E + 1)].reshape(1, D).astype(F32)
    gain_two = lines[:, local * (E + 1) : local * (E + 2)].reshape(1, D).astype(F32)
    table_flat = lines[:, local * (E + 2) : local * (E + 2) + H * NB // n].reshape(-1)

    both_parts = gather_t(jnp.concatenate([tokens, cotangent], axis=1))
    token_parts = [part[..., :D] for part in both_parts]
    cotangent_all = jnp.concatenate(natural([p[:, D:] for p in in_order(both_parts)], t), axis=0)

    sent = expert_slots >= 0
    absolute = jnp.where(sent, expert_ids * CAP + expert_slots, -1)
    position = jnp.arange(SEQ, dtype=jnp.int32)
    empty = ~jnp.any(absolute[None, :] == position[:, None], axis=1)
    before = position[None, :] <= position[:, None]
    empty_rank = jnp.sum((before & empty[None, :]).astype(jnp.int32), axis=1)
    unsent_rank = jnp.sum((before & ~sent[None, :]).astype(jnp.int32), axis=1)
    match = empty[None, :] & (empty_rank[None, :] == unsent_rank[:, None])
    spare = jnp.sum(jnp.where(match, position[None, :], 0), axis=1)
    slot = jnp.where(sent, absolute, spare)
    in_expert = slot % CAP
    place = ((in_expert // SUB) ^ t) * ROWS + ((slot // CAP) ^ z) * SUB + in_expert % SUB
    to_slots_mask = place[None, :] == position[:, None]
    to_slots = to_slots_mask.astype(BF)
    own_mask = to_slots_mask[:ROWS]
    sent_own = jnp.any(own_mask & sent[None, :], axis=1)
    chosen_own = jnp.sum(jnp.where(own_mask, expert_ids[None, :], 0), axis=1)
    own_tokens = lax.dynamic_slice_in_dim(place, t * ROWS, ROWS, 0)
    from_slots_own = (own_tokens[:, None] == position[None, :]).astype(BF)

    def dispatch_z(rows):
        rows = jnp.where(sent_own[:, None], rows, 0).astype(BF)
        return jnp.concatenate(deliver_z(rows.reshape(E, SUB, D)), axis=0)

    grad_output = mm(to_slots[:ROWS], cotangent_all, 1, 0)
    masked = jnp.where(sent_own[:, None], grad_output, 0).astype(BF).reshape(E, SUB, D)
    in_rows = jnp.stack([pick(w_in, z ^ d, 1) for d in range(E)])
    out_rows = jnp.stack([pick(w_out, z ^ d, 1) for d in range(E)])
    out_rows = jnp.concatenate([out_rows, masked], axis=1)
    in_columns = jnp.stack(deliver_z(after(in_rows, packed_z, packed_own, both_parts[1])))
    in_swapped = [over_r(in_columns, c) for c in range(1, R)]
    out_z = deliver_z(after(out_rows, in_columns))
    out_columns = jnp.stack([part[:local] for part in out_z])
    out_swapped = [over_r(out_columns, c) for c in range(1, R)]
    in_weight = whole([in_columns] + in_swapped)
    out_weight = whole([out_columns] + out_swapped)
    router = jnp.pad(router_rows.T, ((0, 0), (0, 128 - E)))

    table_rows = lax.dynamic_slice_in_dim(table_flat.astype(F32).reshape(H, NB), t * LH, LH, 0)
    bucket_table = (buckets[None, :] == jnp.arange(NB, dtype=jnp.int32)[:, None]).astype(F32)
    reversed_rel = jnp.dot(
        table_rows,
        jnp.pad(bucket_table[:, ::-1], ((0, 0), (0, 1))),
        precision=HIGHEST_PRECISION,
    )
    packed_refs = whole(packed_all)
    forward = call(
        functools.partial(attention_forward, pieces=len(packed_refs)),
        "attention_forward",
        12,
        [
            ((SEQ, D), BF),
            ((SEQ, 3 * LW), BF),
            ((LH, SEQ, SEQ), F32),
            ((SEQ, LW), BF),
            ((2, ROWS, D), BF),
            ((2, ROWS, D), BF),
            ((SEQ, D), BF),
            ((D, 4 * LW), BF),
        ],
        [],
        place_at,
        *token_parts,
        gain_one,
        reversed_rel,
        after(to_slots, in_columns, out_rows, router, chosen_own, from_slots_own, gain_two),
        *packed_refs,
    )
    normed_all, qkv, probs, heads_all, kept, given, tokens_all, attention_weight = after(
        forward, in_swapped, out_z
    )
    cotangent_z = jnp.concatenate([part[local:] for part in out_z], axis=0)
    cotangent_parts = gather_t(cotangent_z)
    attended = scatter_t(kept, given)
    inputs = mm(to_slots[:ROWS], tokens_all, 1, 0)
    middle = inputs + attended
    scale_two = norm_scale(middle)
    normed_two = (middle * scale_two * gain_two).astype(BF)

    buffer_parts = gather_t(dispatch_z(normed_two), out_weight)
    buffer, grad_expert, activation, grad_pre, kept, given = call(
        functools.partial(expert_layer, pieces=len(in_weight)),
        "expert_layer",
        8,
        [
            ((SEQ, D), BF),
            ((SEQ, D), BF),
            ((SEQ, width), BF),
            ((SEQ, width), BF),
            ((2, ROWS, 2 * D), BF),
            ((2, ROWS, 2 * D), BF),
        ],
        [((D, width), BF), ((D, width), BF)],
        place_at,
        *buffer_parts,
        *cotangent_parts,
        router,
        *in_weight,
        *out_weight,
    )


    def expert_gradient(name, left, right):
        (out,) = call(
            weight_gradient,
            name,
            2,
            [((*grads_shape, width), BF)],
            [((D, width), F32)],
            place_at,
            left,
            right,
        )
        return blocks_to_send(out)

    out_terms = expert_gradient("grad_w_out", grad_expert, activation)
    in_terms = expert_gradient("grad_w_in", buffer, grad_pre)
    mine = scatter_t(kept, given).astype(BF)
    out_sums = add(swap_r(out_terms)).astype(BF)
    in_sums = add(swap_r(after(in_terms, out_sums, mine))).astype(BF)
    returned = deliver_z(after(mine, out_sums).reshape(E, SUB, 2 * D))
    returned = jnp.concatenate(returned, axis=0).astype(F32)
    combined, grad_normed_two = returned[:, :D], returned[:, D:]

    experts = jnp.arange(E, dtype=jnp.int32)[None, :]
    route = jax.nn.softmax(mm(normed_two, router_rows, 1, 1), axis=-1)
    chosen = experts == chosen_own[:, None]
    gate = jnp.sum(jnp.where(chosen, route, 0.0), axis=-1)
    layer_rows = (middle + gate[:, None] * combined).astype(BF)
    grad_gate = jnp.sum(grad_output * combined, axis=-1)
    grad_logits = gate[:, None] * (chosen.astype(F32) - route) * grad_gate[:, None]
    grad_router = lax.dot_general(
        grad_logits,
        normed_two.astype(F32),
        (((0,), (0,)), ((), ())),
        precision=HIGHEST_PRECISION,
    )
    grad_normed_two = grad_normed_two + jnp.dot(
        grad_logits, router_rows.astype(F32), precision=HIGHEST_PRECISION
    )
    grad_gain_two = jnp.sum(grad_normed_two * middle * scale_two, axis=0, keepdims=True)
    grad_middle = (grad_output + norm_back(grad_normed_two, middle, scale_two, gain_two)).astype(BF)
    grad_parts = gather_t(grad_middle, in_sums)
    layer_parts = gather_t(after(layer_rows, grad_parts))

    late_terms, kept, given, grad_gain_one, grad_rel = call(
        attention_backward,
        "attention_backward",
        12,
        [
            ((*grads_shape, 4 * LW), BF),
            ((2, ROWS, D), BF),
            ((2, ROWS, D), BF),
            ((1, D), F32),
            ((LH, SPAN), F32),
        ],
        [
            ((SEQ, D), BF),
            ((SEQ, LW), BF),
            ((SEQ, 3 * LW), BF),
            ((SEQ, D), F32),
            ((D, 4 * LW), F32),
        ],
        place_at,
        *grad_parts,
        to_slots,
        attention_weight,
        tokens_all,
        normed_all,
        qkv,
        probs,
        heads_all,
    )
    expert_sums = jnp.stack([in_sums, out_sums], axis=1)
    expert_sums = after(expert_sums, grad_middle)
    delivered = [expert_sums[0], over_z(expert_sums[1], 1), over_z(expert_sums[2], 2)]
    late_terms, kept, given, grad_gain_one, grad_rel, delivered, last = after(
        (late_terms, kept, given, grad_gain_one, grad_rel, delivered, expert_sums[3]),
        layer_parts[1],
    )
    delivered = delivered + [over_z(last, 3)]
    late_terms = blocks_to_send(late_terms)
    far_sums = add(swap_r(late_terms[:, 2:])).astype(BF)
    near_terms = swap_r(after(late_terms[:, :2], far_sums))
    grad_normed_one = scatter_t(kept, given)
    own_inputs = tokens.astype(F32)
    grad_slots = jnp.concatenate(in_order(grad_parts), axis=0)
    grad_tokens = mm(from_slots_own, grad_slots, 1, 0) + norm_back(
        grad_normed_one, own_inputs, norm_scale(own_inputs), gain_one
    )
    layer_slots = jnp.concatenate(in_order(layer_parts), axis=0)
    layer_out = mm(from_slots_own, layer_slots, 1, 0).astype(BF)
    grad_table_rows = lax.dot_general(
        grad_rel[:, : 2 * SEQ - 1],
        bucket_table,
        (((1,), (1,)), ((), ())),
        precision=HIGHEST_PRECISION,
    )
    grad_table = lax.dynamic_update_slice_in_dim(
        jnp.zeros((H, NB), F32), grad_table_rows, t * LH, 0
    ).reshape(1, -1)
    small = sum_but_z(
        jnp.concatenate(
            [
                grad_router,
                grad_gain_two,
                grad_gain_one,
                jnp.pad(grad_table, ((0, 0), (0, D - H * NB))),
                jnp.zeros((1, D), F32),
            ],
            axis=0,
        )
    )
    low = small.astype(BF)
    far = [over_z(jnp.concatenate([far_sums[d - 2], low], axis=0), d) for d in (2, 3)]
    near_sums = add(after(near_terms, far, delivered))
    near = over_z(jnp.concatenate([near_sums[1].astype(BF), low], axis=0), 1)
    late = jnp.concatenate([near_sums[0], small], axis=0)
    late = late + far[0].astype(F32) + far[1].astype(F32) + near.astype(F32)
    late, small = late[:local], late[local:]
    small_own = lax.dynamic_slice_in_dim(small[: E + 2], at_dp * local, local, 1)
    table_own = lax.dynamic_slice_in_dim(small[E + 2], at_dp * (H * NB // n), H * NB // n, 0)
    return (
        layer_out,
        grad_tokens,
        late[:, : 3 * LW].reshape(local, 3, LW),
        late[:, 3 * LW :],
        small_own[:E].T,
        jnp.stack(natural([part[0] for part in delivered], z), axis=1).astype(F32),
        jnp.stack(natural([part[1] for part in delivered], z), axis=1).astype(F32),
        small_own[E + 1],
        small_own[E],
        table_own,
    )


def solution(mesh):
    in_specs = (
        P(("dp", "tensor"), None),
        P(("dp", "tensor"), None),
        P("dp", None, "tensor"),
        P("dp", "tensor"),
        P("dp", None),
        P("dp", None, "tensor"),
        P("dp", None, "tensor"),
        P("dp"),
        P("dp"),
        P("dp"),
        P("dp"),
        P("dp"),
        P("dp"),
        P(),
    )
    out_specs = (
        P(("dp", "tensor"), None),
        P(("dp", "tensor"), None),
        P("dp", None, "tensor"),
        P("dp", "tensor"),
        P("dp", None),
        P("dp", None, "tensor"),
        P("dp", None, "tensor"),
        P("dp"),
        P("dp"),
        P("dp"),
    )
    return jax.shard_map(body, mesh=mesh, in_specs=in_specs, out_specs=out_specs, check_vma=False)
```

```python
import functools

import jax
import jax.numpy as jnp
from jax import lax
from jax.experimental import pallas as pl
from jax.experimental.pallas import tpu as pltpu
from jax.sharding import PartitionSpec as P

D = 768
H = 12
HD = 64
NB = 32
E = 4
SEQ = 512
CAP = 128
T = 4
LH = H // T
LW = LH * HD
ROWS = SEQ // T
SUB = CAP // T
SPAN = 2 * SEQ
TILE = 128
TILES = SEQ // TILE

EPSILON = 1e-06
HIGHEST_PRECISION = lax.Precision.HIGHEST
BF = jnp.bfloat16
F32 = jnp.float32


def mm(a, b, ca, cb):
    return lax.dot_general(a, b, (((ca,), (cb,)), ((), ())), preferred_element_type=F32)


def over_t(x, k):
    return lax.ppermute(x, "tensor", [(i, i ^ k) for i in range(T)])


def over_z(x, d):
    n = lax.axis_size("dp")
    r = n // E
    return lax.ppermute(x, "dp", [(i, ((i // r) ^ d) * r + i % r) for i in range(n)])


def over_r(x, c):
    n = lax.axis_size("dp")
    r = n // E
    return lax.ppermute(x, "dp", [(i, (i // r) * r + ((i % r) ^ c)) for i in range(n)])


def natural(parts, index):
    bit = 1
    while bit < len(parts):
        flip = (index & bit) != 0
        parts = [jnp.where(flip, parts[j ^ bit], parts[j]) for j in range(len(parts))]
        bit *= 2
    return parts


def gather_t(x, *earlier):
    far = over_t(x, 2)
    return x, far, over_t(after(jnp.stack([x, far]), *earlier), 1)


def in_order(gathered):
    own, far, near = gathered
    return [own, near[0], far, near[1]]


def scatter_t(kept, sent, *earlier):
    first = over_t(sent, 1).astype(F32)
    away = after((kept[1].astype(F32) + first[1]).astype(BF), *earlier)
    return kept[0].astype(F32) + first[0] + over_t(away, 2).astype(F32)


def pick(x, index, axis):
    return lax.dynamic_index_in_dim(x, index, axis, keepdims=False)


def after(x, *others):
    return lax.optimization_barrier((x, others))[0]


def swap_r(x):
    return [x[0]] + [over_r(x[c], c) for c in range(1, x.shape[0])]


def add(terms):
    return sum(term.astype(F32) for term in terms)


def deliver_z(x):
    return [x[0]] + [over_z(x[d], d) for d in range(1, E)]


def sum_but_z(x, *earlier):
    R = lax.axis_size("dp") // E
    x = x + over_t(x, 2)
    c = 1
    while c < R:
        x = x + over_r(x, c)
        c *= 2
    x = after(x, *earlier)
    return x + over_t(x, 1)


VMEM = pl.BlockSpec(memory_space=pltpu.VMEM)
SMEM = pl.BlockSpec(memory_space=pltpu.SMEM)
PARAMS = pltpu.CompilerParams(vmem_limit_bytes=48 * 2**20)


def call(kernel, name, micros, outs, scratch, at, *operands):
    moved = sum(a.size * a.dtype.itemsize for a in operands)
    return pl.pallas_call(
        kernel,
        out_shape=[jax.ShapeDtypeStruct(shape, kind) for shape, kind in outs],
        in_specs=[SMEM] + [VMEM] * len(operands),
        out_specs=[VMEM] * len(outs),
        scratch_shapes=[pltpu.VMEM(shape, kind) for shape, kind in scratch],
        compiler_params=PARAMS,
        cost_estimate=pl.CostEstimate(
            flops=micros * 10**9, bytes_accessed=moved, transcendentals=0
        ),
        name=name,
    )(at, *operands)


def block(index, length):
    return pl.ds(pl.multiple_of(index * length, length), length)


def place_rows(target, own_ref, far_ref, near_ref, t):
    for k, rows in ((0, own_ref[...]), (1, near_ref[0]), (2, far_ref[...]), (3, near_ref[1])):
        at = k if t is None else t ^ k
        target[block(at, ROWS), :] = rows


def place_weight(target, refs, at_ref):
    pieces = []
    for ref in refs:
        pieces += [ref] if len(ref.shape) == 2 else [ref.at[i] for i in range(ref.shape[0])]
    z, r, R = at_ref[0], at_ref[1], len(pieces) // E
    local = D // len(pieces)
    for c in range(R):
        for d in range(E):
            at = block((z ^ d) * R + (r ^ c), local)
            target[at, :] = pieces[c * E + d][:local, :]


def load_weight(target, refs, at_ref):
    if refs[0].shape == target.shape:
        target[...] = refs[0][...]
    else:
        place_weight(target, refs, at_ref)


def send_rows(source, out_ref, at_ref):
    R, _, local, _ = out_ref.shape
    for c in range(R):
        for d in range(E):
            at = block((at_ref[0] ^ d) * R + (at_ref[1] ^ c), local)
            out_ref[c, d] = source[at, :].astype(BF)


def attention_forward(
    at_ref,
    own_ref,
    far_ref,
    near_ref,
    gain_ref,
    rel_ref,
    slots_ref,
    *rest,
    pieces,
):
    refs, rest = rest[:pieces], rest[pieces:]
    normed_ref, qkv_ref, probs_ref, heads_ref, kept_ref, sent_ref, tokens_ref, weight_ref = rest
    t, length = at_ref[2], at_ref[3]
    load_weight(weight_ref, refs, at_ref)
    place_rows(tokens_ref, own_ref, far_ref, near_ref, t)
    inputs = tokens_ref[...].astype(F32)
    normed_ref[...] = (inputs * norm_scale(inputs) * gain_ref[...]).astype(BF)
    qkv_ref[...] = mm(normed_ref[...], weight_ref[:, : 3 * LW], 1, 0).astype(BF)
    live = lax.broadcasted_iota(jnp.int32, (TILE, SEQ), 1) < length
    for h in range(LH):
        key = qkv_ref[:, LW + h * HD : LW + (h + 1) * HD]
        value = qkv_ref[:, 2 * LW + h * HD : 2 * LW + (h + 1) * HD]
        bias = jnp.broadcast_to(rel_ref[h : h + 1, :], (TILE, SPAN))
        for i in range(TILES):
            rows = slice(i * TILE, (i + 1) * TILE)
            query = qkv_ref[rows, h * HD : (h + 1) * HD]
            rolled = pltpu.roll(bias, SEQ + 1 + i * TILE, 1, stride=1, stride_axis=0)[:, :SEQ]
            scores = mm(query, key, 1, 1) * 0.125 + rolled
            scores = jnp.where(live, scores, -1e30)
            exponent = jnp.exp(scores - jnp.max(scores, axis=1, keepdims=True))
            probs = exponent / jnp.sum(exponent, axis=1, keepdims=True)
            probs_ref[h, rows, :] = probs
            heads_ref[rows, h * HD : (h + 1) * HD] = mm(probs.astype(BF), value, 1, 0).astype(BF)
    in_slots = mm(slots_ref[...], heads_ref[...], 1, 0).astype(BF)
    part = mm(in_slots, weight_ref[:, 3 * LW :], 1, 1).astype(BF)
    for k, out in ((0, kept_ref.at[0]), (1, sent_ref.at[0]), (2, kept_ref.at[1]), (3, sent_ref.at[1])):
        out[...] = part[k * ROWS : (k + 1) * ROWS]


def attention_backward(
    at_ref,
    own_ref,
    far_ref,
    near_ref,
    slots_ref,
    weight_ref,
    tokens_ref,
    normed_ref,
    qkv_ref,
    probs_ref,
    heads_ref,
    grads_ref,
    kept_ref,
    sent_ref,
    gain_ref,
    rel_ref,
    slot_scratch,
    heads_scratch,
    qkv_scratch,
    wide_scratch,
    weight_scratch,
):
    t = at_ref[2]
    place_rows(slot_scratch, own_ref, far_ref, near_ref, None)
    attended = mm(slots_ref[...], slot_scratch[...], 0, 0).astype(BF)
    heads_scratch[...] = mm(attended, weight_ref[:, 3 * LW :], 1, 0).astype(BF)
    weight_scratch[:, 3 * LW :] = mm(attended, heads_ref[...], 0, 0)
    flip = (
        lax.broadcasted_iota(jnp.int32, (TILE, TILE), 0)
        + lax.broadcasted_iota(jnp.int32, (TILE, TILE), 1)
        == TILE - 1
    ).astype(BF)
    rel_ref[...] = jnp.zeros_like(rel_ref)
    for h in range(LH):
        key = qkv_ref[:, LW + h * HD : LW + (h + 1) * HD]
        value = qkv_ref[:, 2 * LW + h * HD : 2 * LW + (h + 1) * HD]
        grad_key = jnp.zeros((SEQ, HD), F32)
        grad_value = jnp.zeros((SEQ, HD), F32)
        diagonal = [None] * (2 * TILES - 1)
        for i in range(TILES):
            rows = slice(i * TILE, (i + 1) * TILE)
            query = qkv_ref[rows, h * HD : (h + 1) * HD]
            grad = heads_scratch[rows, h * HD : (h + 1) * HD]
            probs = probs_ref[h, rows, :]
            grad_probs = mm(grad, value, 1, 1)
            inner = jnp.sum(probs * grad_probs, axis=1, keepdims=True)
            low = (probs * (grad_probs - inner)).astype(BF)
            qkv_scratch[rows, h * HD : (h + 1) * HD] = (mm(low, key, 1, 0) * 0.125).astype(BF)
            grad_key = grad_key + mm(low, query, 0, 0)
            grad_value = grad_value + mm(probs.astype(BF), grad, 0, 0)
            for j in range(TILES):
                turned = mm(low[:, j * TILE : (j + 1) * TILE], flip, 1, 0)
                at = i - j + TILES - 1
                diagonal[at] = turned if diagonal[at] is None else diagonal[at] + turned
        qkv_scratch[:, LW + h * HD : LW + (h + 1) * HD] = (grad_key * 0.125).astype(BF)
        qkv_scratch[:, 2 * LW + h * HD : 2 * LW + (h + 1) * HD] = grad_value.astype(BF)
        for at, part in enumerate(diagonal):
            wide = jnp.concatenate([part, jnp.zeros((TILE, TILE), F32)], axis=1)
            line = jnp.sum(pltpu.roll(wide, 0, 1, stride=1, stride_axis=0), axis=0, keepdims=True)
            rel_ref[h : h + 1, at * TILE : (at + 2) * TILE] += line
    weight_scratch[:, : 3 * LW] = mm(normed_ref[...], qkv_scratch[...], 0, 0)
    if len(grads_ref.shape) == 4:
        send_rows(weight_scratch, grads_ref, at_ref)
    else:
        grads_ref[...] = weight_scratch[...].astype(BF)
    wide_scratch[...] = mm(qkv_scratch[...], weight_ref[:, : 3 * LW], 1, 1)
    inputs = tokens_ref[...].astype(F32)
    gain_ref[...] = jnp.sum(
        wide_scratch[...] * inputs * norm_scale(inputs), axis=0, keepdims=True
    )
    for k, out in ((0, kept_ref.at[0]), (1, sent_ref.at[0]), (2, kept_ref.at[1]), (3, sent_ref.at[1])):
        out[...] = wide_scratch[block(t ^ k, ROWS), :].astype(BF)


def expert_layer(
    at_ref,
    own_ref,
    far_ref,
    near_ref,
    own_grad_ref,
    far_grad_ref,
    near_grad_ref,
    router_ref,
    *rest,
    pieces,
):
    in_refs, out_refs, rest = rest[:pieces], rest[pieces : 2 * pieces], rest[2 * pieces :]
    buffer_ref, grad_ref, activation_ref, grad_pre_ref, kept_ref, sent_ref, in_ref, out_ref = rest
    load_weight(in_ref, in_refs, at_ref)
    load_weight(out_ref, out_refs, at_ref)
    place_rows(buffer_ref, own_ref, far_ref, near_ref, None)
    place_rows(grad_ref, own_grad_ref, far_grad_ref, near_grad_ref, None)
    logits = mm(buffer_ref[...], router_ref[...], 1, 0)
    lane = lax.broadcasted_iota(jnp.int32, logits.shape, 1)
    logits = jnp.where(lane < E, logits, -1e30)
    exponent = jnp.exp(logits - jnp.max(logits, axis=1, keepdims=True))
    mine = jnp.sum(jnp.where(lane == at_ref[0], exponent, 0.0), axis=1, keepdims=True)
    gate = mine / jnp.sum(exponent, axis=1, keepdims=True)
    grad_ref[...] = (gate * grad_ref[...].astype(F32)).astype(BF)
    pre = mm(buffer_ref[...], in_ref[...], 1, 0)
    square = pre * pre
    tanh = jnp.tanh(0.7978845608028654 * (pre + 0.044715 * pre * square))
    half = 0.5 * (1.0 + tanh)
    activation_ref[...] = (pre * half).astype(BF)
    slope = half + 0.5 * pre * (1.0 - tanh * tanh) * (
        0.7978845608028654 * (1.0 + 3.0 * 0.044715 * square)
    )
    grad_act = mm(grad_ref[...], out_ref[...], 1, 0)
    grad_pre_ref[...] = (grad_act * slope).astype(BF)
    for k, out in ((0, kept_ref.at[0]), (1, sent_ref.at[0]), (2, kept_ref.at[1]), (3, sent_ref.at[1])):
        rows = slice(k * ROWS, (k + 1) * ROWS)
        out[:, :D] = mm(activation_ref[rows, :], out_ref[...], 1, 1).astype(BF)
        out[:, D:] = mm(grad_pre_ref[rows, :], in_ref[...], 1, 1).astype(BF)


def weight_gradient(at_ref, left_ref, right_ref, out_ref, scratch):
    scratch[...] = mm(left_ref[...], right_ref[...], 0, 0)
    if len(out_ref.shape) == 4:
        send_rows(scratch, out_ref, at_ref)
    else:
        out_ref[...] = scratch[...].astype(BF)


def norm_scale(values):
    return lax.rsqrt(jnp.mean(values * values, axis=-1, keepdims=True) + EPSILON)


def norm_back(grad, values, scale, gain):
    u = grad * gain
    inner = jnp.mean(u * values, axis=-1, keepdims=True)
    return scale * u - scale * scale * scale * values * inner


def body(
    tokens,
    cotangent,
    w_qkv,
    w_out_attn,
    w_router,
    w_in,
    w_out,
    norm1_gain,
    norm2_gain,
    bias_table,
    seq_length,
    expert_ids,
    expert_slots,
    buckets,
):
    n = lax.axis_size("dp")
    R = n // E
    at_dp = lax.axis_index("dp")
    z, r = at_dp // R, at_dp % R
    t = lax.axis_index("tensor")
    local = D // n
    width = w_in.shape[2]
    aligned = local % 16 == 0
    place_at = jnp.stack([z, r, t, seq_length[0]]).astype(jnp.int32)

    def whole(parts):
        if aligned:
            return parts
        pieces = []
        for part in parts:
            pieces += [part] if part.ndim == 2 else list(part)
        pieces = [piece[:local] for piece in pieces]
        rows = [jnp.stack(natural(pieces[c * E : (c + 1) * E], z)) for c in range(R)]
        return [jnp.stack(natural(rows, r), axis=1).reshape(D, -1)]

    def blocks_to_send(grad):
        if aligned:
            return grad
        x = grad.reshape(E, R, local, -1)
        x = jnp.stack([pick(x, r ^ c, 1) for c in range(R)])
        return jnp.stack([pick(x, z ^ d, 1) for d in range(E)], axis=1)

    grads_shape = (R, E, local) if aligned else (D,)

    line = jnp.concatenate([w_router.T.reshape(-1), norm1_gain, norm2_gain, bias_table])
    line = jnp.pad(line, (0, 4 * LW - line.shape[0]))[None]
    packed = jnp.concatenate(
        [jnp.concatenate([w_qkv.reshape(local, 3 * LW), w_out_attn], axis=1), line], axis=0
    )
    packed_z = [packed] + [over_z(packed, d) for d in range(1, E)]
    packed_own = [over_r(packed, c) for c in range(1, R)]
    packed_rest = after(jnp.stack([part[:local] for part in packed_z[1:]]), packed_own)
    packed_all = list(packed_z)
    for c in range(1, R):
        packed_all += [packed_own[c - 1], over_r(packed_rest, c)]
    lines = jnp.stack(natural([part[local] for part in packed_z], z))
    lines = [lines] + [over_r(lines, c) for c in range(1, R)]
    lines = jnp.stack(natural(lines, r), axis=1).reshape(n, -1)
    router_rows = lines[:, : local * E].reshape(n, E, local).transpose(1, 0, 2).reshape(E, D)
    gain_one = lines[:, local * E : local * (E + 1)].reshape(1, D).astype(F32)
    gain_two = lines[:, local * (E + 1) : local * (E + 2)].reshape(1, D).astype(F32)
    table_flat = lines[:, local * (E + 2) : local * (E + 2) + H * NB // n].reshape(-1)

    both_parts = gather_t(jnp.concatenate([tokens, cotangent], axis=1))
    token_parts = [part[..., :D] for part in both_parts]
    cotangent_all = jnp.concatenate(natural([p[:, D:] for p in in_order(both_parts)], t), axis=0)

    sent = expert_slots >= 0
    absolute = jnp.where(sent, expert_ids * CAP + expert_slots, -1)
    position = jnp.arange(SEQ, dtype=jnp.int32)
    empty = ~jnp.any(absolute[None, :] == position[:, None], axis=1)
    before = position[None, :] <= position[:, None]
    empty_rank = jnp.sum((before & empty[None, :]).astype(jnp.int32), axis=1)
    unsent_rank = jnp.sum((before & ~sent[None, :]).astype(jnp.int32), axis=1)
    match = empty[None, :] & (empty_rank[None, :] == unsent_rank[:, None])
    spare = jnp.sum(jnp.where(match, position[None, :], 0), axis=1)
    slot = jnp.where(sent, absolute, spare)
    in_expert = slot % CAP
    place = ((in_expert // SUB) ^ t) * ROWS + ((slot // CAP) ^ z) * SUB + in_expert % SUB
    to_slots_mask = place[None, :] == position[:, None]
    to_slots = to_slots_mask.astype(BF)
    own_mask = to_slots_mask[:ROWS]
    sent_own = jnp.any(own_mask & sent[None, :], axis=1)
    chosen_own = jnp.sum(jnp.where(own_mask, expert_ids[None, :], 0), axis=1)
    own_tokens = lax.dynamic_slice_in_dim(place, t * ROWS, ROWS, 0)
    from_slots_own = (own_tokens[:, None] == position[None, :]).astype(BF)

    def dispatch_z(rows):
        rows = jnp.where(sent_own[:, None], rows, 0).astype(BF)
        return jnp.concatenate(deliver_z(rows.reshape(E, SUB, D)), axis=0)

    grad_output = mm(to_slots[:ROWS], cotangent_all, 1, 0)
    masked = jnp.where(sent_own[:, None], grad_output, 0).astype(BF).reshape(E, SUB, D)
    in_rows = after(w_in, packed_z, packed_own, both_parts[1])
    in_z = deliver_z(jnp.stack([pick(in_rows, z ^ d, 1) for d in range(E)]))
    in_columns = jnp.stack(after(in_z, packed_all))
    in_swapped = [over_r(in_columns, c) for c in range(1, R)]
    out_rows = after(w_out, in_z)
    out_rows = jnp.stack([pick(out_rows, z ^ d, 1) for d in range(E)])
    out_z = deliver_z(jnp.concatenate([out_rows, masked], axis=1))
    out_columns = jnp.stack([part[:local] for part in out_z])
    out_swapped = [over_r(out_columns, c) for c in range(1, R)]
    in_weight = whole([in_columns] + in_swapped)
    out_weight = whole([out_columns] + out_swapped)
    router = jnp.pad(router_rows.T, ((0, 0), (0, 128 - E)))

    table_rows = lax.dynamic_slice_in_dim(table_flat.astype(F32).reshape(H, NB), t * LH, LH, 0)
    bucket_table = (buckets[None, :] == jnp.arange(NB, dtype=jnp.int32)[:, None]).astype(F32)
    reversed_rel = jnp.dot(
        table_rows,
        jnp.pad(bucket_table[:, ::-1], ((0, 0), (0, 1))),
        precision=HIGHEST_PRECISION,
    )
    packed_refs = whole(packed_all)
    forward = call(
        functools.partial(attention_forward, pieces=len(packed_refs)),
        "attention_forward",
        12,
        [
            ((SEQ, D), BF),
            ((SEQ, 3 * LW), BF),
            ((LH, SEQ, SEQ), F32),
            ((SEQ, LW), BF),
            ((2, ROWS, D), BF),
            ((2, ROWS, D), BF),
            ((SEQ, D), BF),
            ((D, 4 * LW), BF),
        ],
        [],
        place_at,
        *token_parts,
        gain_one,
        reversed_rel,
        after(to_slots, in_z, masked, router, chosen_own, from_slots_own, gain_two),
        *packed_refs,
    )
    normed_all, qkv, probs, heads_all, kept, given, tokens_all, attention_weight = after(
        forward, in_swapped
    )
    cotangent_z = jnp.concatenate([part[local:] for part in out_z], axis=0)
    cotangent_parts = gather_t(cotangent_z)
    attended = scatter_t(kept, given)
    inputs = mm(to_slots[:ROWS], tokens_all, 1, 0)
    middle = inputs + attended
    scale_two = norm_scale(middle)
    normed_two = (middle * scale_two * gain_two).astype(BF)

    buffer_parts = gather_t(dispatch_z(after(normed_two, out_z)), out_weight)
    buffer, grad_expert, activation, grad_pre, kept, given = call(
        functools.partial(expert_layer, pieces=len(in_weight)),
        "expert_layer",
        8,
        [
            ((SEQ, D), BF),
            ((SEQ, D), BF),
            ((SEQ, width), BF),
            ((SEQ, width), BF),
            ((2, ROWS, 2 * D), BF),
            ((2, ROWS, 2 * D), BF),
        ],
        [((D, width), BF), ((D, width), BF)],
        place_at,
        *buffer_parts,
        *cotangent_parts,
        router,
        *in_weight,
        *out_weight,
    )


    def expert_gradient(name, left, right):
        (out,) = call(
            weight_gradient,
            name,
            2,
            [((*grads_shape, width), BF)],
            [((D, width), F32)],
            place_at,
            left,
            right,
        )
        return blocks_to_send(out)

    out_terms = expert_gradient("grad_w_out", grad_expert, activation)
    in_terms = expert_gradient("grad_w_in", buffer, grad_pre)
    mine = scatter_t(kept, given).astype(BF)
    out_sums = add(swap_r(out_terms)).astype(BF)
    in_sums = add(swap_r(after(in_terms, out_sums, mine))).astype(BF)
    returned = deliver_z(after(mine, out_sums).reshape(E, SUB, 2 * D))
    returned = jnp.concatenate(returned, axis=0).astype(F32)
    combined, grad_normed_two = returned[:, :D], returned[:, D:]

    experts = jnp.arange(E, dtype=jnp.int32)[None, :]
    route = jax.nn.softmax(mm(normed_two, router_rows, 1, 1), axis=-1)
    chosen = experts == chosen_own[:, None]
    gate = jnp.sum(jnp.where(chosen, route, 0.0), axis=-1)
    layer_rows = (middle + gate[:, None] * combined).astype(BF)
    grad_gate = jnp.sum(grad_output * combined, axis=-1)
    grad_logits = gate[:, None] * (chosen.astype(F32) - route) * grad_gate[:, None]
    grad_router = lax.dot_general(
        grad_logits,
        normed_two.astype(F32),
        (((0,), (0,)), ((), ())),
        precision=HIGHEST_PRECISION,
    )
    grad_normed_two = grad_normed_two + jnp.dot(
        grad_logits, router_rows.astype(F32), precision=HIGHEST_PRECISION
    )
    grad_gain_two = jnp.sum(grad_normed_two * middle * scale_two, axis=0, keepdims=True)
    grad_middle = (grad_output + norm_back(grad_normed_two, middle, scale_two, gain_two)).astype(BF)
    grad_parts = gather_t(grad_middle, in_sums)
    layer_parts = gather_t(after(layer_rows, grad_parts))

    late_terms, kept, given, grad_gain_one, grad_rel = call(
        attention_backward,
        "attention_backward",
        12,
        [
            ((*grads_shape, 4 * LW), BF),
            ((2, ROWS, D), BF),
            ((2, ROWS, D), BF),
            ((1, D), F32),
            ((LH, SPAN), F32),
        ],
        [
            ((SEQ, D), BF),
            ((SEQ, LW), BF),
            ((SEQ, 3 * LW), BF),
            ((SEQ, D), F32),
            ((D, 4 * LW), F32),
        ],
        place_at,
        *grad_parts,
        to_slots,
        attention_weight,
        tokens_all,
        normed_all,
        qkv,
        probs,
        heads_all,
    )
    expert_sums = jnp.stack([in_sums, out_sums], axis=1)
    expert_sums = after(expert_sums, grad_middle)
    delivered = [expert_sums[0], over_z(expert_sums[1], 1), over_z(expert_sums[2], 2)]
    late_terms, kept, given, grad_gain_one, grad_rel, delivered, last = after(
        (late_terms, kept, given, grad_gain_one, grad_rel, delivered, expert_sums[3]),
        layer_parts[1],
    )
    delivered = delivered + [over_z(last, 3)]
    late_terms = blocks_to_send(late_terms)
    far_terms = swap_r(late_terms[:, 2:])
    far_sums = add(far_terms).astype(BF)
    near_terms = swap_r(after(late_terms[:, :2], far_sums))
    grad_normed_one = scatter_t(kept, given)
    own_inputs = tokens.astype(F32)
    grad_slots = jnp.concatenate(in_order(grad_parts), axis=0)
    grad_tokens = mm(from_slots_own, grad_slots, 1, 0) + norm_back(
        grad_normed_one, own_inputs, norm_scale(own_inputs), gain_one
    )
    layer_slots = jnp.concatenate(in_order(layer_parts), axis=0)
    layer_out = mm(from_slots_own, layer_slots, 1, 0).astype(BF)
    grad_table_rows = lax.dot_general(
        grad_rel[:, : 2 * SEQ - 1],
        bucket_table,
        (((1,), (1,)), ((), ())),
        precision=HIGHEST_PRECISION,
    )
    grad_table = lax.dynamic_update_slice_in_dim(
        jnp.zeros((H, NB), F32), grad_table_rows, t * LH, 0
    ).reshape(1, -1)
    small = sum_but_z(
        jnp.concatenate(
            [
                grad_router,
                grad_gain_two,
                grad_gain_one,
                jnp.pad(grad_table, ((0, 0), (0, D - H * NB))),
                jnp.zeros((1, D), F32),
            ],
            axis=0,
        ),
        far_terms,
    )
    low = small.astype(BF)
    far = [over_z(jnp.concatenate([far_sums[d - 2], low], axis=0), d) for d in (2, 3)]
    near_sums = add(after(near_terms, far, delivered))
    near = over_z(jnp.concatenate([near_sums[1].astype(BF), low], axis=0), 1)
    late = jnp.concatenate([near_sums[0], small], axis=0)
    late = late + far[0].astype(F32) + far[1].astype(F32) + near.astype(F32)
    late, small = late[:local], late[local:]
    small_own = lax.dynamic_slice_in_dim(small[: E + 2], at_dp * local, local, 1)
    table_own = lax.dynamic_slice_in_dim(small[E + 2], at_dp * (H * NB // n), H * NB // n, 0)
    return (
        layer_out,
        grad_tokens,
        late[:, : 3 * LW].reshape(local, 3, LW),
        late[:, 3 * LW :],
        small_own[:E].T,
        jnp.stack(natural([part[0] for part in delivered], z), axis=1).astype(F32),
        jnp.stack(natural([part[1] for part in delivered], z), axis=1).astype(F32),
        small_own[E + 1],
        small_own[E],
        table_own,
    )


def solution(mesh):
    in_specs = (
        P(("dp", "tensor"), None),
        P(("dp", "tensor"), None),
        P("dp", None, "tensor"),
        P("dp", "tensor"),
        P("dp", None),
        P("dp", None, "tensor"),
        P("dp", None, "tensor"),
        P("dp"),
        P("dp"),
        P("dp"),
        P("dp"),
        P("dp"),
        P("dp"),
        P(),
    )
    out_specs = (
        P(("dp", "tensor"), None),
        P(("dp", "tensor"), None),
        P("dp", None, "tensor"),
        P("dp", "tensor"),
        P("dp", None),
        P("dp", None, "tensor"),
        P("dp", None, "tensor"),
        P("dp"),
        P("dp"),
        P("dp"),
    )
    return jax.shard_map(body, mesh=mesh, in_specs=in_specs, out_specs=out_specs, check_vma=False)
```

```python
import functools

import jax
import jax.numpy as jnp
from jax import lax
from jax.experimental import pallas as pl
from jax.experimental.pallas import tpu as pltpu
from jax.sharding import PartitionSpec as P

D = 768
H = 12
HD = 64
NB = 32
E = 4
SEQ = 512
CAP = 128
T = 4
LH = H // T
LW = LH * HD
ROWS = SEQ // T
SUB = CAP // T
SPAN = 2 * SEQ
TILE = 128
TILES = SEQ // TILE

EPSILON = 1e-06
HIGHEST_PRECISION = lax.Precision.HIGHEST
BF = jnp.bfloat16
F32 = jnp.float32


def mm(a, b, ca, cb):
    return lax.dot_general(a, b, (((ca,), (cb,)), ((), ())), preferred_element_type=F32)


def over_t(x, k):
    return lax.ppermute(x, "tensor", [(i, i ^ k) for i in range(T)])


def over_z(x, d):
    n = lax.axis_size("dp")
    r = n // E
    return lax.ppermute(x, "dp", [(i, ((i // r) ^ d) * r + i % r) for i in range(n)])


def over_r(x, c):
    n = lax.axis_size("dp")
    r = n // E
    return lax.ppermute(x, "dp", [(i, (i // r) * r + ((i % r) ^ c)) for i in range(n)])


def natural(parts, index):
    bit = 1
    while bit < len(parts):
        flip = (index & bit) != 0
        parts = [jnp.where(flip, parts[j ^ bit], parts[j]) for j in range(len(parts))]
        bit *= 2
    return parts


def gather_t(x, *earlier):
    far = over_t(x, 2)
    return x, far, over_t(after(jnp.stack([x, far]), *earlier), 1)


def in_order(gathered):
    own, far, near = gathered
    return [own, near[0], far, near[1]]


def scatter_t(kept, sent):
    return finish_scatter(kept, over_t(sent, 1))


def finish_scatter(kept, first):
    first = first.astype(F32)
    away = (kept[1].astype(F32) + first[1]).astype(BF)
    return kept[0].astype(F32) + first[0] + over_t(away, 2).astype(F32)


def pick(x, index, axis):
    return lax.dynamic_index_in_dim(x, index, axis, keepdims=False)


def after(x, *others):
    return lax.optimization_barrier((x, others))[0]


def swap_r(x):
    return [x[0]] + [over_r(x[c], c) for c in range(1, x.shape[0])]


def add(terms):
    return sum(term.astype(F32) for term in terms)


def deliver_z(x):
    return [x[0]] + [over_z(x[d], d) for d in range(1, E)]


def sum_but_z(x, *earlier):
    R = lax.axis_size("dp") // E
    x = x + over_t(x, 2)
    c = 1
    while c < R:
        x = x + over_r(x, c)
        c *= 2
    x = after(x, *earlier)
    return x + over_t(x, 1)


VMEM = pl.BlockSpec(memory_space=pltpu.VMEM)
SMEM = pl.BlockSpec(memory_space=pltpu.SMEM)
PARAMS = pltpu.CompilerParams(vmem_limit_bytes=48 * 2**20)


def call(kernel, name, micros, outs, scratch, at, *operands):
    moved = sum(a.size * a.dtype.itemsize for a in operands)
    return pl.pallas_call(
        kernel,
        out_shape=[jax.ShapeDtypeStruct(shape, kind) for shape, kind in outs],
        in_specs=[SMEM] + [VMEM] * len(operands),
        out_specs=[VMEM] * len(outs),
        scratch_shapes=[pltpu.VMEM(shape, kind) for shape, kind in scratch],
        compiler_params=PARAMS,
        cost_estimate=pl.CostEstimate(
            flops=micros * 10**9, bytes_accessed=moved, transcendentals=0
        ),
        name=name,
    )(at, *operands)


def block(index, length):
    return pl.ds(pl.multiple_of(index * length, length), length)


def place_rows(target, own_ref, far_ref, near_ref, t):
    for k, rows in ((0, own_ref[...]), (1, near_ref[0]), (2, far_ref[...]), (3, near_ref[1])):
        at = k if t is None else t ^ k
        target[block(at, ROWS), :] = rows


def place_weight(target, refs, at_ref):
    pieces = []
    for ref in refs:
        pieces += [ref] if len(ref.shape) == 2 else [ref.at[i] for i in range(ref.shape[0])]
    z, r, R = at_ref[0], at_ref[1], len(pieces) // E
    local = D // len(pieces)
    for c in range(R):
        for d in range(E):
            at = block((z ^ d) * R + (r ^ c), local)
            target[at, :] = pieces[c * E + d][:local, :]


def load_weight(target, refs, at_ref):
    if refs[0].shape == target.shape:
        target[...] = refs[0][...]
    else:
        place_weight(target, refs, at_ref)


def send_rows(source, out_ref, at_ref):
    R, _, local, _ = out_ref.shape
    for c in range(R):
        for d in range(E):
            at = block((at_ref[0] ^ d) * R + (at_ref[1] ^ c), local)
            out_ref[c, d] = source[at, :].astype(BF)


def attention_forward(
    at_ref,
    own_ref,
    far_ref,
    near_ref,
    gain_ref,
    rel_ref,
    slots_ref,
    *rest,
    pieces,
):
    refs, rest = rest[:pieces], rest[pieces:]
    normed_ref, qkv_ref, probs_ref, heads_ref, kept_ref, sent_ref, tokens_ref, weight_ref = rest
    t, length = at_ref[2], at_ref[3]
    load_weight(weight_ref, refs, at_ref)
    place_rows(tokens_ref, own_ref, far_ref, near_ref, t)
    inputs = tokens_ref[...].astype(F32)
    normed_ref[...] = (inputs * norm_scale(inputs) * gain_ref[...]).astype(BF)
    qkv_ref[...] = mm(normed_ref[...], weight_ref[:, : 3 * LW], 1, 0).astype(BF)
    live = lax.broadcasted_iota(jnp.int32, (TILE, SEQ), 1) < length
    for h in range(LH):
        key = qkv_ref[:, LW + h * HD : LW + (h + 1) * HD]
        value = qkv_ref[:, 2 * LW + h * HD : 2 * LW + (h + 1) * HD]
        bias = jnp.broadcast_to(rel_ref[h : h + 1, :], (TILE, SPAN))
        for i in range(TILES):
            rows = slice(i * TILE, (i + 1) * TILE)
            query = qkv_ref[rows, h * HD : (h + 1) * HD]
            rolled = pltpu.roll(bias, SEQ + 1 + i * TILE, 1, stride=1, stride_axis=0)[:, :SEQ]
            scores = mm(query, key, 1, 1) * 0.125 + rolled
            scores = jnp.where(live, scores, -1e30)
            exponent = jnp.exp(scores - jnp.max(scores, axis=1, keepdims=True))
            probs = exponent / jnp.sum(exponent, axis=1, keepdims=True)
            probs_ref[h, rows, :] = probs
            heads_ref[rows, h * HD : (h + 1) * HD] = mm(probs.astype(BF), value, 1, 0).astype(BF)
    in_slots = mm(slots_ref[...], heads_ref[...], 1, 0).astype(BF)
    part = mm(in_slots, weight_ref[:, 3 * LW :], 1, 1).astype(BF)
    for k, out in ((0, kept_ref.at[0]), (1, sent_ref.at[0]), (2, kept_ref.at[1]), (3, sent_ref.at[1])):
        out[...] = part[k * ROWS : (k + 1) * ROWS]


def attention_backward(
    at_ref,
    own_ref,
    far_ref,
    near_ref,
    slots_ref,
    weight_ref,
    tokens_ref,
    normed_ref,
    qkv_ref,
    probs_ref,
    heads_ref,
    grads_ref,
    kept_ref,
    sent_ref,
    gain_ref,
    rel_ref,
    slot_scratch,
    heads_scratch,
    qkv_scratch,
    wide_scratch,
    weight_scratch,
):
    t = at_ref[2]
    place_rows(slot_scratch, own_ref, far_ref, near_ref, None)
    attended = mm(slots_ref[...], slot_scratch[...], 0, 0).astype(BF)
    heads_scratch[...] = mm(attended, weight_ref[:, 3 * LW :], 1, 0).astype(BF)
    weight_scratch[:, 3 * LW :] = mm(attended, heads_ref[...], 0, 0)
    flip = (
        lax.broadcasted_iota(jnp.int32, (TILE, TILE), 0)
        + lax.broadcasted_iota(jnp.int32, (TILE, TILE), 1)
        == TILE - 1
    ).astype(BF)
    rel_ref[...] = jnp.zeros_like(rel_ref)
    for h in range(LH):
        key = qkv_ref[:, LW + h * HD : LW + (h + 1) * HD]
        value = qkv_ref[:, 2 * LW + h * HD : 2 * LW + (h + 1) * HD]
        grad_key = jnp.zeros((SEQ, HD), F32)
        grad_value = jnp.zeros((SEQ, HD), F32)
        diagonal = [None] * (2 * TILES - 1)
        for i in range(TILES):
            rows = slice(i * TILE, (i + 1) * TILE)
            query = qkv_ref[rows, h * HD : (h + 1) * HD]
            grad = heads_scratch[rows, h * HD : (h + 1) * HD]
            probs = probs_ref[h, rows, :]
            grad_probs = mm(grad, value, 1, 1)
            inner = jnp.sum(probs * grad_probs, axis=1, keepdims=True)
            low = (probs * (grad_probs - inner)).astype(BF)
            qkv_scratch[rows, h * HD : (h + 1) * HD] = (mm(low, key, 1, 0) * 0.125).astype(BF)
            grad_key = grad_key + mm(low, query, 0, 0)
            grad_value = grad_value + mm(probs.astype(BF), grad, 0, 0)
            for j in range(TILES):
                turned = mm(low[:, j * TILE : (j + 1) * TILE], flip, 1, 0)
                at = i - j + TILES - 1
                diagonal[at] = turned if diagonal[at] is None else diagonal[at] + turned
        qkv_scratch[:, LW + h * HD : LW + (h + 1) * HD] = (grad_key * 0.125).astype(BF)
        qkv_scratch[:, 2 * LW + h * HD : 2 * LW + (h + 1) * HD] = grad_value.astype(BF)
        for at, part in enumerate(diagonal):
            wide = jnp.concatenate([part, jnp.zeros((TILE, TILE), F32)], axis=1)
            line = jnp.sum(pltpu.roll(wide, 0, 1, stride=1, stride_axis=0), axis=0, keepdims=True)
            rel_ref[h : h + 1, at * TILE : (at + 2) * TILE] += line
    weight_scratch[:, : 3 * LW] = mm(normed_ref[...], qkv_scratch[...], 0, 0)
    if len(grads_ref.shape) == 4:
        send_rows(weight_scratch, grads_ref, at_ref)
    else:
        grads_ref[...] = weight_scratch[...].astype(BF)
    wide_scratch[...] = mm(qkv_scratch[...], weight_ref[:, : 3 * LW], 1, 1)
    inputs = tokens_ref[...].astype(F32)
    gain_ref[...] = jnp.sum(
        wide_scratch[...] * inputs * norm_scale(inputs), axis=0, keepdims=True
    )
    for k, out in ((0, kept_ref.at[0]), (1, sent_ref.at[0]), (2, kept_ref.at[1]), (3, sent_ref.at[1])):
        out[...] = wide_scratch[block(t ^ k, ROWS), :].astype(BF)


def expert_layer(
    at_ref,
    own_ref,
    far_ref,
    near_ref,
    own_grad_ref,
    far_grad_ref,
    near_grad_ref,
    router_ref,
    *rest,
    pieces,
):
    in_refs, out_refs, rest = rest[:pieces], rest[pieces : 2 * pieces], rest[2 * pieces :]
    buffer_ref, grad_ref, activation_ref, grad_pre_ref, kept_ref, sent_ref, in_ref, out_ref = rest
    load_weight(in_ref, in_refs, at_ref)
    load_weight(out_ref, out_refs, at_ref)
    place_rows(buffer_ref, own_ref, far_ref, near_ref, None)
    place_rows(grad_ref, own_grad_ref, far_grad_ref, near_grad_ref, None)
    logits = mm(buffer_ref[...], router_ref[...], 1, 0)
    lane = lax.broadcasted_iota(jnp.int32, logits.shape, 1)
    logits = jnp.where(lane < E, logits, -1e30)
    exponent = jnp.exp(logits - jnp.max(logits, axis=1, keepdims=True))
    mine = jnp.sum(jnp.where(lane == at_ref[0], exponent, 0.0), axis=1, keepdims=True)
    gate = mine / jnp.sum(exponent, axis=1, keepdims=True)
    grad_ref[...] = (gate * grad_ref[...].astype(F32)).astype(BF)
    pre = mm(buffer_ref[...], in_ref[...], 1, 0)
    square = pre * pre
    tanh = jnp.tanh(0.7978845608028654 * (pre + 0.044715 * pre * square))
    half = 0.5 * (1.0 + tanh)
    activation_ref[...] = (pre * half).astype(BF)
    slope = half + 0.5 * pre * (1.0 - tanh * tanh) * (
        0.7978845608028654 * (1.0 + 3.0 * 0.044715 * square)
    )
    grad_act = mm(grad_ref[...], out_ref[...], 1, 0)
    grad_pre_ref[...] = (grad_act * slope).astype(BF)
    for k, out in ((0, kept_ref.at[0]), (1, sent_ref.at[0]), (2, kept_ref.at[1]), (3, sent_ref.at[1])):
        rows = slice(k * ROWS, (k + 1) * ROWS)
        out[:, :D] = mm(activation_ref[rows, :], out_ref[...], 1, 1).astype(BF)
        out[:, D:] = mm(grad_pre_ref[rows, :], in_ref[...], 1, 1).astype(BF)


def weight_gradient(at_ref, left_ref, right_ref, out_ref, scratch):
    scratch[...] = mm(left_ref[...], right_ref[...], 0, 0)
    if len(out_ref.shape) == 4:
        send_rows(scratch, out_ref, at_ref)
    else:
        out_ref[...] = scratch[...].astype(BF)


def norm_scale(values):
    return lax.rsqrt(jnp.mean(values * values, axis=-1, keepdims=True) + EPSILON)


def norm_back(grad, values, scale, gain):
    u = grad * gain
    inner = jnp.mean(u * values, axis=-1, keepdims=True)
    return scale * u - scale * scale * scale * values * inner


def body(
    tokens,
    cotangent,
    w_qkv,
    w_out_attn,
    w_router,
    w_in,
    w_out,
    norm1_gain,
    norm2_gain,
    bias_table,
    seq_length,
    expert_ids,
    expert_slots,
    buckets,
):
    n = lax.axis_size("dp")
    R = n // E
    at_dp = lax.axis_index("dp")
    z, r = at_dp // R, at_dp % R
    t = lax.axis_index("tensor")
    local = D // n
    width = w_in.shape[2]
    aligned = local % 16 == 0
    place_at = jnp.stack([z, r, t, seq_length[0]]).astype(jnp.int32)

    def whole(parts):
        if aligned:
            return parts
        pieces = []
        for part in parts:
            pieces += [part] if part.ndim == 2 else list(part)
        pieces = [piece[:local] for piece in pieces]
        rows = [jnp.stack(natural(pieces[c * E : (c + 1) * E], z)) for c in range(R)]
        return [jnp.stack(natural(rows, r), axis=1).reshape(D, -1)]

    def blocks_to_send(grad):
        if aligned:
            return grad
        x = grad.reshape(E, R, local, -1)
        x = jnp.stack([pick(x, r ^ c, 1) for c in range(R)])
        return jnp.stack([pick(x, z ^ d, 1) for d in range(E)], axis=1)

    grads_shape = (R, E, local) if aligned else (D,)

    line = jnp.concatenate([w_router.T.reshape(-1), norm1_gain, norm2_gain, bias_table])
    line = jnp.pad(line, (0, 4 * LW - line.shape[0]))[None]
    packed = jnp.concatenate(
        [jnp.concatenate([w_qkv.reshape(local, 3 * LW), w_out_attn], axis=1), line], axis=0
    )
    packed_z = [packed] + [over_z(packed, d) for d in range(1, E)]
    packed_own = [over_r(packed, c) for c in range(1, R)]
    packed_rest = after(jnp.stack([part[:local] for part in packed_z[1:]]), packed_own)
    packed_all = list(packed_z)
    for c in range(1, R):
        packed_all += [packed_own[c - 1], over_r(packed_rest, c)]
    lines = jnp.stack(natural([part[local] for part in packed_z], z))
    lines = [lines] + [over_r(lines, c) for c in range(1, R)]
    lines = jnp.stack(natural(lines, r), axis=1).reshape(n, -1)
    router_rows = lines[:, : local * E].reshape(n, E, local).transpose(1, 0, 2).reshape(E, D)
    gain_one = lines[:, local * E : local * (E + 1)].reshape(1, D).astype(F32)
    gain_two = lines[:, local * (E + 1) : local * (E + 2)].reshape(1, D).astype(F32)
    table_flat = lines[:, local * (E + 2) : local * (E + 2) + H * NB // n].reshape(-1)

    both_parts = gather_t(jnp.concatenate([tokens, cotangent], axis=1))
    token_parts = [part[..., :D] for part in both_parts]
    cotangent_all = jnp.concatenate(natural([p[:, D:] for p in in_order(both_parts)], t), axis=0)

    sent = expert_slots >= 0
    absolute = jnp.where(sent, expert_ids * CAP + expert_slots, -1)
    position = jnp.arange(SEQ, dtype=jnp.int32)
    empty = ~jnp.any(absolute[None, :] == position[:, None], axis=1)
    before = position[None, :] <= position[:, None]
    empty_rank = jnp.sum((before & empty[None, :]).astype(jnp.int32), axis=1)
    unsent_rank = jnp.sum((before & ~sent[None, :]).astype(jnp.int32), axis=1)
    match = empty[None, :] & (empty_rank[None, :] == unsent_rank[:, None])
    spare = jnp.sum(jnp.where(match, position[None, :], 0), axis=1)
    slot = jnp.where(sent, absolute, spare)
    in_expert = slot % CAP
    place = ((in_expert // SUB) ^ t) * ROWS + ((slot // CAP) ^ z) * SUB + in_expert % SUB
    to_slots_mask = place[None, :] == position[:, None]
    to_slots = to_slots_mask.astype(BF)
    own_mask = to_slots_mask[:ROWS]
    sent_own = jnp.any(own_mask & sent[None, :], axis=1)
    chosen_own = jnp.sum(jnp.where(own_mask, expert_ids[None, :], 0), axis=1)
    own_tokens = lax.dynamic_slice_in_dim(place, t * ROWS, ROWS, 0)
    from_slots_own = (own_tokens[:, None] == position[None, :]).astype(BF)

    def dispatch_z(rows):
        rows = jnp.where(sent_own[:, None], rows, 0).astype(BF)
        return jnp.concatenate(deliver_z(rows.reshape(E, SUB, D)), axis=0)

    grad_output = mm(to_slots[:ROWS], cotangent_all, 1, 0)
    masked = jnp.where(sent_own[:, None], grad_output, 0).astype(BF).reshape(E, SUB, D)
    in_rows = after(w_in, packed_z, packed_own, both_parts[1])
    in_z = deliver_z(jnp.stack([pick(in_rows, z ^ d, 1) for d in range(E)]))
    out_rows = after(w_out, in_z[1:3])
    out_rows = jnp.stack([pick(out_rows, z ^ d, 1) for d in range(E)])
    out_rows = jnp.concatenate([out_rows, masked], axis=1)
    router = jnp.pad(router_rows.T, ((0, 0), (0, 128 - E)))

    table_rows = lax.dynamic_slice_in_dim(table_flat.astype(F32).reshape(H, NB), t * LH, LH, 0)
    bucket_table = (buckets[None, :] == jnp.arange(NB, dtype=jnp.int32)[:, None]).astype(F32)
    reversed_rel = jnp.dot(
        table_rows,
        jnp.pad(bucket_table[:, ::-1], ((0, 0), (0, 1))),
        precision=HIGHEST_PRECISION,
    )
    packed_refs = whole(packed_all)
    forward = call(
        functools.partial(attention_forward, pieces=len(packed_refs)),
        "attention_forward",
        12,
        [
            ((SEQ, D), BF),
            ((SEQ, 3 * LW), BF),
            ((LH, SEQ, SEQ), F32),
            ((SEQ, LW), BF),
            ((2, ROWS, D), BF),
            ((2, ROWS, D), BF),
            ((SEQ, D), BF),
            ((D, 4 * LW), BF),
        ],
        [],
        place_at,
        *token_parts,
        gain_one,
        reversed_rel,
        after(to_slots, in_z[1:3], out_rows, router, chosen_own, from_slots_own, gain_two),
        *packed_refs,
    )
    normed_all, qkv, probs, heads_all, kept, given, tokens_all, attention_weight = after(
        forward, in_z
    )
    in_z, out_rows = after((in_z, out_rows), kept)
    in_columns = jnp.stack(in_z)
    in_swapped = [over_r(in_columns, c) for c in range(1, R)]
    in_weight = whole([in_columns] + in_swapped)
    out_z = deliver_z(out_rows)
    out_columns = jnp.stack([part[:local] for part in out_z])
    out_swapped = [over_r(out_columns, c) for c in range(1, R)]
    out_weight = whole([out_columns] + out_swapped)
    cotangent_z = jnp.concatenate([part[local:] for part in out_z], axis=0)
    cotangent_parts = gather_t(cotangent_z)
    attended = scatter_t(kept, given)
    inputs = mm(to_slots[:ROWS], tokens_all, 1, 0)
    middle = inputs + attended
    scale_two = norm_scale(middle)
    normed_two = (middle * scale_two * gain_two).astype(BF)

    buffer_z = dispatch_z(after(normed_two, out_z))
    buffer_parts = gather_t(after(buffer_z, in_swapped), out_weight)
    buffer, grad_expert, activation, grad_pre, kept, given = call(
        functools.partial(expert_layer, pieces=len(in_weight)),
        "expert_layer",
        8,
        [
            ((SEQ, D), BF),
            ((SEQ, D), BF),
            ((SEQ, width), BF),
            ((SEQ, width), BF),
            ((2, ROWS, 2 * D), BF),
            ((2, ROWS, 2 * D), BF),
        ],
        [((D, width), BF), ((D, width), BF)],
        place_at,
        *buffer_parts,
        *cotangent_parts,
        router,
        *in_weight,
        *out_weight,
    )


    def expert_gradient(name, left, right):
        (out,) = call(
            weight_gradient,
            name,
            2,
            [((*grads_shape, width), BF)],
            [((D, width), F32)],
            place_at,
            left,
            right,
        )
        return blocks_to_send(out)

    out_terms = expert_gradient("grad_w_out", grad_expert, activation)
    in_terms = expert_gradient("grad_w_in", buffer, grad_pre)
    mine = scatter_t(kept, given).astype(BF)
    out_sums = add(swap_r(out_terms)).astype(BF)
    in_sums = add(swap_r(after(in_terms, out_sums, mine))).astype(BF)
    returned = deliver_z(after(mine, out_sums).reshape(E, SUB, 2 * D))
    returned = jnp.concatenate(returned, axis=0).astype(F32)
    combined, grad_normed_two = returned[:, :D], returned[:, D:]

    experts = jnp.arange(E, dtype=jnp.int32)[None, :]
    route = jax.nn.softmax(mm(normed_two, router_rows, 1, 1), axis=-1)
    chosen = experts == chosen_own[:, None]
    gate = jnp.sum(jnp.where(chosen, route, 0.0), axis=-1)
    layer_rows = (middle + gate[:, None] * combined).astype(BF)
    grad_gate = jnp.sum(grad_output * combined, axis=-1)
    grad_logits = gate[:, None] * (chosen.astype(F32) - route) * grad_gate[:, None]
    grad_router = lax.dot_general(
        grad_logits,
        normed_two.astype(F32),
        (((0,), (0,)), ((), ())),
        precision=HIGHEST_PRECISION,
    )
    grad_normed_two = grad_normed_two + jnp.dot(
        grad_logits, router_rows.astype(F32), precision=HIGHEST_PRECISION
    )
    grad_gain_two = jnp.sum(grad_normed_two * middle * scale_two, axis=0, keepdims=True)
    grad_middle = (grad_output + norm_back(grad_normed_two, middle, scale_two, gain_two)).astype(BF)
    grad_parts = gather_t(grad_middle, in_sums)
    layer_parts = gather_t(after(layer_rows, grad_parts))

    late_terms, kept, given, grad_gain_one, grad_rel = call(
        attention_backward,
        "attention_backward",
        12,
        [
            ((*grads_shape, 4 * LW), BF),
            ((2, ROWS, D), BF),
            ((2, ROWS, D), BF),
            ((1, D), F32),
            ((LH, SPAN), F32),
        ],
        [
            ((SEQ, D), BF),
            ((SEQ, LW), BF),
            ((SEQ, 3 * LW), BF),
            ((SEQ, D), F32),
            ((D, 4 * LW), F32),
        ],
        place_at,
        *grad_parts,
        to_slots,
        attention_weight,
        tokens_all,
        normed_all,
        qkv,
        probs,
        heads_all,
    )
    expert_sums = jnp.stack([in_sums, out_sums], axis=1)
    expert_sums = after(expert_sums, grad_middle)
    delivered = deliver_z(expert_sums)
    late_terms, kept, given, grad_gain_one, grad_rel = after(
        (late_terms, kept, given, grad_gain_one, grad_rel), layer_parts[1]
    )
    late_terms = blocks_to_send(late_terms)
    far_terms = swap_r(late_terms[:, 2:])
    delivered = after(delivered, far_terms)
    far_sums = add(far_terms).astype(BF)
    near_terms = swap_r(after(late_terms[:, :2], far_sums))
    given = over_t(given, 1)
    grad_normed_one = finish_scatter(kept, given)
    own_inputs = tokens.astype(F32)
    grad_slots = jnp.concatenate(in_order(grad_parts), axis=0)
    grad_tokens = mm(from_slots_own, grad_slots, 1, 0) + norm_back(
        grad_normed_one, own_inputs, norm_scale(own_inputs), gain_one
    )
    layer_slots = jnp.concatenate(in_order(layer_parts), axis=0)
    layer_out = mm(from_slots_own, layer_slots, 1, 0).astype(BF)
    grad_table_rows = lax.dot_general(
        grad_rel[:, : 2 * SEQ - 1],
        bucket_table,
        (((1,), (1,)), ((), ())),
        precision=HIGHEST_PRECISION,
    )
    grad_table = lax.dynamic_update_slice_in_dim(
        jnp.zeros((H, NB), F32), grad_table_rows, t * LH, 0
    ).reshape(1, -1)
    small = sum_but_z(
        jnp.concatenate(
            [
                grad_router,
                grad_gain_two,
                grad_gain_one,
                jnp.pad(grad_table, ((0, 0), (0, D - H * NB))),
                jnp.zeros((1, D), F32),
            ],
            axis=0,
        ),
        far_terms,
        given,
        layer_parts[2],
    )
    low = after(small, delivered).astype(BF)
    far = [over_z(jnp.concatenate([far_sums[d - 2], low], axis=0), d) for d in (2, 3)]
    near_sums = add(after(near_terms, far))
    near = over_z(jnp.concatenate([near_sums[1].astype(BF), low], axis=0), 1)
    late = jnp.concatenate([near_sums[0], small], axis=0)
    late = late + far[0].astype(F32) + far[1].astype(F32) + near.astype(F32)
    late, small = late[:local], late[local:]
    small_own = lax.dynamic_slice_in_dim(small[: E + 2], at_dp * local, local, 1)
    table_own = lax.dynamic_slice_in_dim(small[E + 2], at_dp * (H * NB // n), H * NB // n, 0)
    return (
        layer_out,
        grad_tokens,
        late[:, : 3 * LW].reshape(local, 3, LW),
        late[:, 3 * LW :],
        small_own[:E].T,
        jnp.stack(natural([part[0] for part in delivered], z), axis=1).astype(F32),
        jnp.stack(natural([part[1] for part in delivered], z), axis=1).astype(F32),
        small_own[E + 1],
        small_own[E],
        table_own,
    )


def solution(mesh):
    in_specs = (
        P(("dp", "tensor"), None),
        P(("dp", "tensor"), None),
        P("dp", None, "tensor"),
        P("dp", "tensor"),
        P("dp", None),
        P("dp", None, "tensor"),
        P("dp", None, "tensor"),
        P("dp"),
        P("dp"),
        P("dp"),
        P("dp"),
        P("dp"),
        P("dp"),
        P(),
    )
    out_specs = (
        P(("dp", "tensor"), None),
        P(("dp", "tensor"), None),
        P("dp", None, "tensor"),
        P("dp", "tensor"),
        P("dp", None),
        P("dp", None, "tensor"),
        P("dp", None, "tensor"),
        P("dp"),
        P("dp"),
        P("dp"),
    )
    return jax.shard_map(body, mesh=mesh, in_specs=in_specs, out_specs=out_specs, check_vma=False)
```

```python
import functools

import jax
import jax.numpy as jnp
from jax import lax
from jax.experimental import pallas as pl
from jax.experimental.pallas import tpu as pltpu
from jax.sharding import PartitionSpec as P

D = 768
H = 12
HD = 64
NB = 32
E = 4
SEQ = 512
CAP = 128
T = 4
LH = H // T
LW = LH * HD
ROWS = SEQ // T
SUB = CAP // T
SPAN = 2 * SEQ
TILE = 128
TILES = SEQ // TILE

EPSILON = 1e-06
HIGHEST_PRECISION = lax.Precision.HIGHEST
BF = jnp.bfloat16
F32 = jnp.float32


def mm(a, b, ca, cb):
    return lax.dot_general(a, b, (((ca,), (cb,)), ((), ())), preferred_element_type=F32)


def over_t(x, k):
    return lax.ppermute(x, "tensor", [(i, i ^ k) for i in range(T)])


def over_z(x, d):
    n = lax.axis_size("dp")
    r = n // E
    return lax.ppermute(x, "dp", [(i, ((i // r) ^ d) * r + i % r) for i in range(n)])


def over_r(x, c):
    n = lax.axis_size("dp")
    r = n // E
    return lax.ppermute(x, "dp", [(i, (i // r) * r + ((i % r) ^ c)) for i in range(n)])


def natural(parts, index):
    bit = 1
    while bit < len(parts):
        flip = (index & bit) != 0
        parts = [jnp.where(flip, parts[j ^ bit], parts[j]) for j in range(len(parts))]
        bit *= 2
    return parts


def gather_t(x, *earlier):
    far = over_t(x, 2)
    return x, far, over_t(after(jnp.stack([x, far]), *earlier), 1)


def in_order(gathered):
    own, far, near = gathered
    return [own, near[0], far, near[1]]


def scatter_t(kept, sent):
    return finish_scatter(kept, over_t(sent, 1))


def finish_scatter(kept, first):
    first = first.astype(F32)
    away = (kept[1].astype(F32) + first[1]).astype(BF)
    return kept[0].astype(F32) + first[0] + over_t(away, 2).astype(F32)


def pick(x, index, axis):
    return lax.dynamic_index_in_dim(x, index, axis, keepdims=False)


def after(x, *others):
    return lax.optimization_barrier((x, others))[0]


def swap_r(x):
    return [x[0]] + [over_r(x[c], c) for c in range(1, x.shape[0])]


def add(terms):
    return sum(term.astype(F32) for term in terms)


def deliver_z(x):
    return [x[0]] + [over_z(x[d], d) for d in range(1, E)]


def sum_but_z(x, *earlier):
    R = lax.axis_size("dp") // E
    c = 1
    while c < R:
        x = x + over_r(x, c)
        c *= 2
    x = x + over_t(x, 2)
    x = after(x, *earlier)
    return x + over_t(x, 1)


VMEM = pl.BlockSpec(memory_space=pltpu.VMEM)
SMEM = pl.BlockSpec(memory_space=pltpu.SMEM)
PARAMS = pltpu.CompilerParams(vmem_limit_bytes=48 * 2**20)


def call(kernel, name, micros, outs, scratch, at, *operands):
    moved = sum(a.size * a.dtype.itemsize for a in operands)
    return pl.pallas_call(
        kernel,
        out_shape=[jax.ShapeDtypeStruct(shape, kind) for shape, kind in outs],
        in_specs=[SMEM] + [VMEM] * len(operands),
        out_specs=[VMEM] * len(outs),
        scratch_shapes=[pltpu.VMEM(shape, kind) for shape, kind in scratch],
        compiler_params=PARAMS,
        cost_estimate=pl.CostEstimate(
            flops=micros * 10**9, bytes_accessed=moved, transcendentals=0
        ),
        name=name,
    )(at, *operands)


def block(index, length):
    return pl.ds(pl.multiple_of(index * length, length), length)


def place_rows(target, own_ref, far_ref, near_ref, t):
    for k, rows in ((0, own_ref[...]), (1, near_ref[0]), (2, far_ref[...]), (3, near_ref[1])):
        at = k if t is None else t ^ k
        target[block(at, ROWS), :] = rows


def place_weight(target, refs, at_ref):
    pieces = []
    for ref in refs:
        pieces += [ref] if len(ref.shape) == 2 else [ref.at[i] for i in range(ref.shape[0])]
    z, r, R = at_ref[0], at_ref[1], len(pieces) // E
    local = D // len(pieces)
    for c in range(R):
        for d in range(E):
            at = block((z ^ d) * R + (r ^ c), local)
            target[at, :] = pieces[c * E + d][:local, :]


def load_weight(target, refs, at_ref):
    if refs[0].shape == target.shape:
        target[...] = refs[0][...]
    else:
        place_weight(target, refs, at_ref)


def send_rows(source, out_ref, at_ref):
    R, _, local, _ = out_ref.shape
    for c in range(R):
        for d in range(E):
            at = block((at_ref[0] ^ d) * R + (at_ref[1] ^ c), local)
            out_ref[c, d] = source[at, :].astype(BF)


def attention_forward(
    at_ref,
    own_ref,
    far_ref,
    near_ref,
    gain_ref,
    rel_ref,
    slots_ref,
    *rest,
    pieces,
):
    refs, rest = rest[:pieces], rest[pieces:]
    normed_ref, qkv_ref, probs_ref, heads_ref, kept_ref, sent_ref, tokens_ref, weight_ref = rest
    t, length = at_ref[2], at_ref[3]
    load_weight(weight_ref, refs, at_ref)
    place_rows(tokens_ref, own_ref, far_ref, near_ref, t)
    inputs = tokens_ref[...].astype(F32)
    normed_ref[...] = (inputs * norm_scale(inputs) * gain_ref[...]).astype(BF)
    qkv_ref[...] = mm(normed_ref[...], weight_ref[:, : 3 * LW], 1, 0).astype(BF)
    live = lax.broadcasted_iota(jnp.int32, (TILE, SEQ), 1) < length
    for h in range(LH):
        key = qkv_ref[:, LW + h * HD : LW + (h + 1) * HD]
        value = qkv_ref[:, 2 * LW + h * HD : 2 * LW + (h + 1) * HD]
        bias = jnp.broadcast_to(rel_ref[h : h + 1, :], (TILE, SPAN))
        for i in range(TILES):
            rows = slice(i * TILE, (i + 1) * TILE)
            query = qkv_ref[rows, h * HD : (h + 1) * HD]
            rolled = pltpu.roll(bias, SEQ + 1 + i * TILE, 1, stride=1, stride_axis=0)[:, :SEQ]
            scores = mm(query, key, 1, 1) * 0.125 + rolled
            scores = jnp.where(live, scores, -1e30)
            exponent = jnp.exp(scores - jnp.max(scores, axis=1, keepdims=True))
            probs = exponent / jnp.sum(exponent, axis=1, keepdims=True)
            probs_ref[h, rows, :] = probs
            heads_ref[rows, h * HD : (h + 1) * HD] = mm(probs.astype(BF), value, 1, 0).astype(BF)
    in_slots = mm(slots_ref[...], heads_ref[...], 1, 0).astype(BF)
    part = mm(in_slots, weight_ref[:, 3 * LW :], 1, 1).astype(BF)
    for k, out in ((0, kept_ref.at[0]), (1, sent_ref.at[0]), (2, kept_ref.at[1]), (3, sent_ref.at[1])):
        out[...] = part[k * ROWS : (k + 1) * ROWS]


def attention_backward(
    at_ref,
    own_ref,
    far_ref,
    near_ref,
    slots_ref,
    weight_ref,
    tokens_ref,
    normed_ref,
    qkv_ref,
    probs_ref,
    heads_ref,
    grads_ref,
    kept_ref,
    sent_ref,
    gain_ref,
    rel_ref,
    slot_scratch,
    heads_scratch,
    qkv_scratch,
    wide_scratch,
    weight_scratch,
):
    t = at_ref[2]
    place_rows(slot_scratch, own_ref, far_ref, near_ref, None)
    attended = mm(slots_ref[...], slot_scratch[...], 0, 0).astype(BF)
    heads_scratch[...] = mm(attended, weight_ref[:, 3 * LW :], 1, 0).astype(BF)
    weight_scratch[:, 3 * LW :] = mm(attended, heads_ref[...], 0, 0)
    flip = (
        lax.broadcasted_iota(jnp.int32, (TILE, TILE), 0)
        + lax.broadcasted_iota(jnp.int32, (TILE, TILE), 1)
        == TILE - 1
    ).astype(BF)
    rel_ref[...] = jnp.zeros_like(rel_ref)
    for h in range(LH):
        key = qkv_ref[:, LW + h * HD : LW + (h + 1) * HD]
        value = qkv_ref[:, 2 * LW + h * HD : 2 * LW + (h + 1) * HD]
        grad_key = jnp.zeros((SEQ, HD), F32)
        grad_value = jnp.zeros((SEQ, HD), F32)
        diagonal = [None] * (2 * TILES - 1)
        for i in range(TILES):
            rows = slice(i * TILE, (i + 1) * TILE)
            query = qkv_ref[rows, h * HD : (h + 1) * HD]
            grad = heads_scratch[rows, h * HD : (h + 1) * HD]
            probs = probs_ref[h, rows, :]
            grad_probs = mm(grad, value, 1, 1)
            inner = jnp.sum(probs * grad_probs, axis=1, keepdims=True)
            low = (probs * (grad_probs - inner)).astype(BF)
            qkv_scratch[rows, h * HD : (h + 1) * HD] = (mm(low, key, 1, 0) * 0.125).astype(BF)
            grad_key = grad_key + mm(low, query, 0, 0)
            grad_value = grad_value + mm(probs.astype(BF), grad, 0, 0)
            for j in range(TILES):
                turned = mm(low[:, j * TILE : (j + 1) * TILE], flip, 1, 0)
                at = i - j + TILES - 1
                diagonal[at] = turned if diagonal[at] is None else diagonal[at] + turned
        qkv_scratch[:, LW + h * HD : LW + (h + 1) * HD] = (grad_key * 0.125).astype(BF)
        qkv_scratch[:, 2 * LW + h * HD : 2 * LW + (h + 1) * HD] = grad_value.astype(BF)
        for at, part in enumerate(diagonal):
            wide = jnp.concatenate([part, jnp.zeros((TILE, TILE), F32)], axis=1)
            line = jnp.sum(pltpu.roll(wide, 0, 1, stride=1, stride_axis=0), axis=0, keepdims=True)
            rel_ref[h : h + 1, at * TILE : (at + 2) * TILE] += line
    weight_scratch[:, : 3 * LW] = mm(normed_ref[...], qkv_scratch[...], 0, 0)
    if len(grads_ref.shape) == 4:
        send_rows(weight_scratch, grads_ref, at_ref)
    else:
        grads_ref[...] = weight_scratch[...].astype(BF)
    wide_scratch[...] = mm(qkv_scratch[...], weight_ref[:, : 3 * LW], 1, 1)
    inputs = tokens_ref[...].astype(F32)
    gain_ref[...] = jnp.sum(
        wide_scratch[...] * inputs * norm_scale(inputs), axis=0, keepdims=True
    )
    for k, out in ((0, kept_ref.at[0]), (1, sent_ref.at[0]), (2, kept_ref.at[1]), (3, sent_ref.at[1])):
        out[...] = wide_scratch[block(t ^ k, ROWS), :].astype(BF)


def expert_layer(
    at_ref,
    own_ref,
    far_ref,
    near_ref,
    own_grad_ref,
    far_grad_ref,
    near_grad_ref,
    router_ref,
    *rest,
    pieces,
):
    in_refs, out_refs, rest = rest[:pieces], rest[pieces : 2 * pieces], rest[2 * pieces :]
    buffer_ref, grad_ref, activation_ref, grad_pre_ref, kept_ref, sent_ref, in_ref, out_ref = rest
    load_weight(in_ref, in_refs, at_ref)
    load_weight(out_ref, out_refs, at_ref)
    place_rows(buffer_ref, own_ref, far_ref, near_ref, None)
    place_rows(grad_ref, own_grad_ref, far_grad_ref, near_grad_ref, None)
    logits = mm(buffer_ref[...], router_ref[...], 1, 0)
    lane = lax.broadcasted_iota(jnp.int32, logits.shape, 1)
    logits = jnp.where(lane < E, logits, -1e30)
    exponent = jnp.exp(logits - jnp.max(logits, axis=1, keepdims=True))
    mine = jnp.sum(jnp.where(lane == at_ref[0], exponent, 0.0), axis=1, keepdims=True)
    gate = mine / jnp.sum(exponent, axis=1, keepdims=True)
    grad_ref[...] = (gate * grad_ref[...].astype(F32)).astype(BF)
    pre = mm(buffer_ref[...], in_ref[...], 1, 0)
    square = pre * pre
    tanh = jnp.tanh(0.7978845608028654 * (pre + 0.044715 * pre * square))
    half = 0.5 * (1.0 + tanh)
    activation_ref[...] = (pre * half).astype(BF)
    slope = half + 0.5 * pre * (1.0 - tanh * tanh) * (
        0.7978845608028654 * (1.0 + 3.0 * 0.044715 * square)
    )
    grad_act = mm(grad_ref[...], out_ref[...], 1, 0)
    grad_pre_ref[...] = (grad_act * slope).astype(BF)
    for k, out in ((0, kept_ref.at[0]), (1, sent_ref.at[0]), (2, kept_ref.at[1]), (3, sent_ref.at[1])):
        rows = slice(k * ROWS, (k + 1) * ROWS)
        out[:, :D] = mm(activation_ref[rows, :], out_ref[...], 1, 1).astype(BF)
        out[:, D:] = mm(grad_pre_ref[rows, :], in_ref[...], 1, 1).astype(BF)


def weight_gradient(at_ref, left_ref, right_ref, out_ref, scratch):
    scratch[...] = mm(left_ref[...], right_ref[...], 0, 0)
    if len(out_ref.shape) == 4:
        send_rows(scratch, out_ref, at_ref)
    else:
        out_ref[...] = scratch[...].astype(BF)


def norm_scale(values):
    return lax.rsqrt(jnp.mean(values * values, axis=-1, keepdims=True) + EPSILON)


def norm_back(grad, values, scale, gain):
    u = grad * gain
    inner = jnp.mean(u * values, axis=-1, keepdims=True)
    return scale * u - scale * scale * scale * values * inner


def body(
    tokens,
    cotangent,
    w_qkv,
    w_out_attn,
    w_router,
    w_in,
    w_out,
    norm1_gain,
    norm2_gain,
    bias_table,
    seq_length,
    expert_ids,
    expert_slots,
    buckets,
):
    n = lax.axis_size("dp")
    R = n // E
    at_dp = lax.axis_index("dp")
    z, r = at_dp // R, at_dp % R
    t = lax.axis_index("tensor")
    local = D // n
    width = w_in.shape[2]
    aligned = local % 16 == 0
    place_at = jnp.stack([z, r, t, seq_length[0]]).astype(jnp.int32)

    def whole(parts):
        if aligned:
            return parts
        pieces = []
        for part in parts:
            pieces += [part] if part.ndim == 2 else list(part)
        pieces = [piece[:local] for piece in pieces]
        rows = [jnp.stack(natural(pieces[c * E : (c + 1) * E], z)) for c in range(R)]
        return [jnp.stack(natural(rows, r), axis=1).reshape(D, -1)]

    def blocks_to_send(grad):
        if aligned:
            return grad
        x = grad.reshape(E, R, local, -1)
        x = jnp.stack([pick(x, r ^ c, 1) for c in range(R)])
        return jnp.stack([pick(x, z ^ d, 1) for d in range(E)], axis=1)

    grads_shape = (R, E, local) if aligned else (D,)

    line = jnp.concatenate([w_router.T.reshape(-1), norm1_gain, norm2_gain, bias_table])
    line = jnp.pad(line, (0, 4 * LW - line.shape[0]))[None]
    packed = jnp.concatenate(
        [jnp.concatenate([w_qkv.reshape(local, 3 * LW), w_out_attn], axis=1), line], axis=0
    )
    packed_z = [packed] + [over_z(packed, d) for d in range(1, E)]
    packed_own = [over_r(packed, c) for c in range(1, R)]
    packed_rest = after(jnp.stack([part[:local] for part in packed_z[1:]]), packed_own)
    packed_all = list(packed_z)
    for c in range(1, R):
        packed_all += [packed_own[c - 1], over_r(packed_rest, c)]
    lines = jnp.stack(natural([part[local] for part in packed_z], z))
    lines = [lines] + [over_r(lines, c) for c in range(1, R)]
    lines = jnp.stack(natural(lines, r), axis=1).reshape(n, -1)
    router_rows = lines[:, : local * E].reshape(n, E, local).transpose(1, 0, 2).reshape(E, D)
    gain_one = lines[:, local * E : local * (E + 1)].reshape(1, D).astype(F32)
    gain_two = lines[:, local * (E + 1) : local * (E + 2)].reshape(1, D).astype(F32)
    table_flat = lines[:, local * (E + 2) : local * (E + 2) + H * NB // n].reshape(-1)

    both_parts = gather_t(jnp.concatenate([tokens, cotangent], axis=1))
    token_parts = [part[..., :D] for part in both_parts]
    cotangent_all = jnp.concatenate(natural([p[:, D:] for p in in_order(both_parts)], t), axis=0)

    sent = expert_slots >= 0
    absolute = jnp.where(sent, expert_ids * CAP + expert_slots, -1)
    position = jnp.arange(SEQ, dtype=jnp.int32)
    empty = ~jnp.any(absolute[None, :] == position[:, None], axis=1)
    before = position[None, :] <= position[:, None]
    empty_rank = jnp.sum((before & empty[None, :]).astype(jnp.int32), axis=1)
    unsent_rank = jnp.sum((before & ~sent[None, :]).astype(jnp.int32), axis=1)
    match = empty[None, :] & (empty_rank[None, :] == unsent_rank[:, None])
    spare = jnp.sum(jnp.where(match, position[None, :], 0), axis=1)
    slot = jnp.where(sent, absolute, spare)
    in_expert = slot % CAP
    place = ((in_expert // SUB) ^ t) * ROWS + ((slot // CAP) ^ z) * SUB + in_expert % SUB
    to_slots_mask = place[None, :] == position[:, None]
    to_slots = to_slots_mask.astype(BF)
    own_mask = to_slots_mask[:ROWS]
    sent_own = jnp.any(own_mask & sent[None, :], axis=1)
    chosen_own = jnp.sum(jnp.where(own_mask, expert_ids[None, :], 0), axis=1)
    own_tokens = lax.dynamic_slice_in_dim(place, t * ROWS, ROWS, 0)
    from_slots_own = (own_tokens[:, None] == position[None, :]).astype(BF)

    def dispatch_z(rows):
        rows = jnp.where(sent_own[:, None], rows, 0).astype(BF)
        return jnp.concatenate(deliver_z(rows.reshape(E, SUB, D)), axis=0)

    grad_output = mm(to_slots[:ROWS], cotangent_all, 1, 0)
    masked = jnp.where(sent_own[:, None], grad_output, 0).astype(BF).reshape(E, SUB, D)
    in_rows = after(w_in, packed_z, packed_own, both_parts[1])
    in_z = deliver_z(jnp.stack([pick(in_rows, z ^ d, 1) for d in range(E)]))
    out_rows = after(w_out, in_z[1:3])
    out_rows = jnp.stack([pick(out_rows, z ^ d, 1) for d in range(E)])
    out_rows = jnp.concatenate([out_rows, masked], axis=1)
    router = jnp.pad(router_rows.T, ((0, 0), (0, 128 - E)))

    table_rows = lax.dynamic_slice_in_dim(table_flat.astype(F32).reshape(H, NB), t * LH, LH, 0)
    bucket_table = (buckets[None, :] == jnp.arange(NB, dtype=jnp.int32)[:, None]).astype(F32)
    reversed_rel = jnp.dot(
        table_rows,
        jnp.pad(bucket_table[:, ::-1], ((0, 0), (0, 1))),
        precision=HIGHEST_PRECISION,
    )
    packed_refs = whole(packed_all)
    forward = call(
        functools.partial(attention_forward, pieces=len(packed_refs)),
        "attention_forward",
        12,
        [
            ((SEQ, D), BF),
            ((SEQ, 3 * LW), BF),
            ((LH, SEQ, SEQ), F32),
            ((SEQ, LW), BF),
            ((2, ROWS, D), BF),
            ((2, ROWS, D), BF),
            ((SEQ, D), BF),
            ((D, 4 * LW), BF),
        ],
        [],
        place_at,
        *token_parts,
        gain_one,
        reversed_rel,
        after(to_slots, in_z[1:3], out_rows, router, chosen_own, from_slots_own, gain_two),
        *packed_refs,
    )
    normed_all, qkv, probs, heads_all, kept, given, tokens_all, attention_weight = after(
        forward, in_z
    )
    given = over_t(given, 1)
    out_rows = after(out_rows, given)
    in_columns = jnp.stack(after(in_z, given))
    in_swapped = [over_r(in_columns, c) for c in range(1, R)]
    in_weight = whole([in_columns] + in_swapped)
    out_z = deliver_z(out_rows)
    out_columns = jnp.stack([part[:local] for part in out_z])
    out_swapped = [over_r(out_columns, c) for c in range(1, R)]
    out_weight = whole([out_columns] + out_swapped)
    cotangent_z = jnp.concatenate([part[local:] for part in out_z], axis=0)
    cotangent_parts = gather_t(cotangent_z)
    attended = finish_scatter(kept, given)
    inputs = mm(to_slots[:ROWS], tokens_all, 1, 0)
    middle = inputs + attended
    scale_two = norm_scale(middle)
    normed_two = (middle * scale_two * gain_two).astype(BF)

    buffer_z = dispatch_z(after(normed_two, out_z))
    buffer_parts = gather_t(after(buffer_z, in_swapped), out_weight)
    buffer, grad_expert, activation, grad_pre, kept, given = call(
        functools.partial(expert_layer, pieces=len(in_weight)),
        "expert_layer",
        8,
        [
            ((SEQ, D), BF),
            ((SEQ, D), BF),
            ((SEQ, width), BF),
            ((SEQ, width), BF),
            ((2, ROWS, 2 * D), BF),
            ((2, ROWS, 2 * D), BF),
        ],
        [((D, width), BF), ((D, width), BF)],
        place_at,
        *buffer_parts,
        *cotangent_parts,
        router,
        *in_weight,
        *out_weight,
    )


    def expert_gradient(name, left, right):
        (out,) = call(
            weight_gradient,
            name,
            2,
            [((*grads_shape, width), BF)],
            [((D, width), F32)],
            place_at,
            left,
            right,
        )
        return blocks_to_send(out)

    out_terms = expert_gradient("grad_w_out", grad_expert, activation)
    in_terms = expert_gradient("grad_w_in", buffer, grad_pre)
    mine = scatter_t(kept, given).astype(BF)
    out_sums = add(swap_r(out_terms)).astype(BF)
    in_sums = add(swap_r(after(in_terms, out_sums, mine))).astype(BF)
    returned = deliver_z(after(mine, out_sums).reshape(E, SUB, 2 * D))
    returned = jnp.concatenate(returned, axis=0).astype(F32)
    combined, grad_normed_two = returned[:, :D], returned[:, D:]

    experts = jnp.arange(E, dtype=jnp.int32)[None, :]
    route = jax.nn.softmax(mm(normed_two, router_rows, 1, 1), axis=-1)
    chosen = experts == chosen_own[:, None]
    gate = jnp.sum(jnp.where(chosen, route, 0.0), axis=-1)
    layer_rows = (middle + gate[:, None] * combined).astype(BF)
    grad_gate = jnp.sum(grad_output * combined, axis=-1)
    grad_logits = gate[:, None] * (chosen.astype(F32) - route) * grad_gate[:, None]
    grad_router = lax.dot_general(
        grad_logits,
        normed_two.astype(F32),
        (((0,), (0,)), ((), ())),
        precision=HIGHEST_PRECISION,
    )
    grad_normed_two = grad_normed_two + jnp.dot(
        grad_logits, router_rows.astype(F32), precision=HIGHEST_PRECISION
    )
    grad_gain_two = jnp.sum(grad_normed_two * middle * scale_two, axis=0, keepdims=True)
    grad_middle = (grad_output + norm_back(grad_normed_two, middle, scale_two, gain_two)).astype(BF)
    grad_parts = gather_t(grad_middle, in_sums)
    layer_parts = gather_t(after(layer_rows, grad_parts))

    late_terms, kept, given, grad_gain_one, grad_rel = call(
        attention_backward,
        "attention_backward",
        12,
        [
            ((*grads_shape, 4 * LW), BF),
            ((2, ROWS, D), BF),
            ((2, ROWS, D), BF),
            ((1, D), F32),
            ((LH, SPAN), F32),
        ],
        [
            ((SEQ, D), BF),
            ((SEQ, LW), BF),
            ((SEQ, 3 * LW), BF),
            ((SEQ, D), F32),
            ((D, 4 * LW), F32),
        ],
        place_at,
        *grad_parts,
        to_slots,
        attention_weight,
        tokens_all,
        normed_all,
        qkv,
        probs,
        heads_all,
    )
    expert_sums = jnp.stack([in_sums, out_sums], axis=1)
    expert_sums = after(expert_sums, grad_middle)
    delivered = deliver_z(expert_sums)
    late_terms, kept, given, grad_gain_one, grad_rel = after(
        (late_terms, kept, given, grad_gain_one, grad_rel), layer_parts[1]
    )
    late_terms = blocks_to_send(late_terms)
    far_terms = swap_r(late_terms[:, 2:])
    delivered = after(delivered, far_terms)
    far_sums = add(far_terms).astype(BF)
    near_terms = swap_r(after(late_terms[:, :2], far_sums))
    given = over_t(given, 1)
    grad_normed_one = finish_scatter(kept, given)
    own_inputs = tokens.astype(F32)
    grad_slots = jnp.concatenate(in_order(grad_parts), axis=0)
    grad_tokens = mm(from_slots_own, grad_slots, 1, 0) + norm_back(
        grad_normed_one, own_inputs, norm_scale(own_inputs), gain_one
    )
    layer_slots = jnp.concatenate(in_order(layer_parts), axis=0)
    layer_out = mm(from_slots_own, layer_slots, 1, 0).astype(BF)
    grad_table_rows = lax.dot_general(
        grad_rel[:, : 2 * SEQ - 1],
        bucket_table,
        (((1,), (1,)), ((), ())),
        precision=HIGHEST_PRECISION,
    )
    grad_table = lax.dynamic_update_slice_in_dim(
        jnp.zeros((H, NB), F32), grad_table_rows, t * LH, 0
    ).reshape(1, -1)
    small = sum_but_z(
        jnp.concatenate(
            [
                grad_router,
                grad_gain_two,
                grad_gain_one,
                jnp.pad(grad_table, ((0, 0), (0, D - H * NB))),
                jnp.zeros((1, D), F32),
            ],
            axis=0,
        ),
        far_terms,
        given,
        layer_parts[2],
    )
    low = after(small, delivered).astype(BF)
    far = [over_z(jnp.concatenate([far_sums[d - 2], low], axis=0), d) for d in (2, 3)]
    near_terms, delivered = after((near_terms, delivered), far)
    near_sums = add(near_terms)
    near = over_z(jnp.concatenate([near_sums[1].astype(BF), low], axis=0), 1)
    late = jnp.concatenate([near_sums[0], small], axis=0)
    late = late + far[0].astype(F32) + far[1].astype(F32) + near.astype(F32)
    late, small = late[:local], late[local:]
    small_own = lax.dynamic_slice_in_dim(small[: E + 2], at_dp * local, local, 1)
    table_own = lax.dynamic_slice_in_dim(small[E + 2], at_dp * (H * NB // n), H * NB // n, 0)
    return (
        layer_out,
        grad_tokens,
        late[:, : 3 * LW].reshape(local, 3, LW),
        late[:, 3 * LW :],
        small_own[:E].T,
        jnp.stack(natural([part[0] for part in delivered], z), axis=1).astype(F32),
        jnp.stack(natural([part[1] for part in delivered], z), axis=1).astype(F32),
        small_own[E + 1],
        small_own[E],
        table_own,
    )


def solution(mesh):
    in_specs = (
        P(("dp", "tensor"), None),
        P(("dp", "tensor"), None),
        P("dp", None, "tensor"),
        P("dp", "tensor"),
        P("dp", None),
        P("dp", None, "tensor"),
        P("dp", None, "tensor"),
        P("dp"),
        P("dp"),
        P("dp"),
        P("dp"),
        P("dp"),
        P("dp"),
        P(),
    )
    out_specs = (
        P(("dp", "tensor"), None),
        P(("dp", "tensor"), None),
        P("dp", None, "tensor"),
        P("dp", "tensor"),
        P("dp", None),
        P("dp", None, "tensor"),
        P("dp", None, "tensor"),
        P("dp"),
        P("dp"),
        P("dp"),
    )
    return jax.shard_map(body, mesh=mesh, in_specs=in_specs, out_specs=out_specs, check_vma=False)
```

```python
import functools

import jax
import jax.numpy as jnp
from jax import lax
from jax.experimental import pallas as pl
from jax.experimental.pallas import tpu as pltpu
from jax.sharding import PartitionSpec as P

D = 768
H = 12
HD = 64
NB = 32
E = 4
SEQ = 512
CAP = 128
T = 4
LH = H // T
LW = LH * HD
ROWS = SEQ // T
SUB = CAP // T
SPAN = 2 * SEQ
TILE = 128
TILES = SEQ // TILE

EPSILON = 1e-06
HIGHEST_PRECISION = lax.Precision.HIGHEST
BF = jnp.bfloat16
F32 = jnp.float32


def mm(a, b, ca, cb):
    return lax.dot_general(a, b, (((ca,), (cb,)), ((), ())), preferred_element_type=F32)


def over_t(x, k):
    return lax.ppermute(x, "tensor", [(i, i ^ k) for i in range(T)])


def over_z(x, d):
    n = lax.axis_size("dp")
    r = n // E
    return lax.ppermute(x, "dp", [(i, ((i // r) ^ d) * r + i % r) for i in range(n)])


def over_r(x, c):
    n = lax.axis_size("dp")
    r = n // E
    return lax.ppermute(x, "dp", [(i, (i // r) * r + ((i % r) ^ c)) for i in range(n)])


def natural(parts, index):
    bit = 1
    while bit < len(parts):
        flip = (index & bit) != 0
        parts = [jnp.where(flip, parts[j ^ bit], parts[j]) for j in range(len(parts))]
        bit *= 2
    return parts


def gather_t(x, *earlier):
    far = over_t(x, 2)
    return x, far, over_t(after(jnp.stack([x, far]), *earlier), 1)


def in_order(gathered):
    own, far, near = gathered
    return [own, near[0], far, near[1]]


def scatter_t(kept, sent):
    return finish_scatter(kept, over_t(sent, 1))


def finish_scatter(kept, first):
    first = first.astype(F32)
    away = (kept[1].astype(F32) + first[1]).astype(BF)
    return kept[0].astype(F32) + first[0] + over_t(away, 2).astype(F32)


def pick(x, index, axis):
    return lax.dynamic_index_in_dim(x, index, axis, keepdims=False)


def after(x, *others):
    return lax.optimization_barrier((x, others))[0]


def swap_r(x):
    return [x[0]] + [over_r(x[c], c) for c in range(1, x.shape[0])]


def add(terms):
    return sum(term.astype(F32) for term in terms)


def deliver_z(x):
    return [x[0]] + [over_z(x[d], d) for d in range(1, E)]


def sum_but_z(x, *earlier):
    R = lax.axis_size("dp") // E
    c = 1
    while c < R:
        x = x + over_r(x, c)
        c *= 2
    x = after(x, *earlier)
    x = x + over_t(x, 1)
    return x + over_t(x, 2)


VMEM = pl.BlockSpec(memory_space=pltpu.VMEM)
SMEM = pl.BlockSpec(memory_space=pltpu.SMEM)
PARAMS = pltpu.CompilerParams(vmem_limit_bytes=48 * 2**20)


def call(kernel, name, micros, outs, scratch, at, *operands):
    moved = sum(a.size * a.dtype.itemsize for a in operands)
    return pl.pallas_call(
        kernel,
        out_shape=[jax.ShapeDtypeStruct(shape, kind) for shape, kind in outs],
        in_specs=[SMEM] + [VMEM] * len(operands),
        out_specs=[VMEM] * len(outs),
        scratch_shapes=[pltpu.VMEM(shape, kind) for shape, kind in scratch],
        compiler_params=PARAMS,
        cost_estimate=pl.CostEstimate(
            flops=micros * 10**9, bytes_accessed=moved, transcendentals=0
        ),
        name=name,
    )(at, *operands)


def block(index, length):
    return pl.ds(pl.multiple_of(index * length, length), length)


def place_rows(target, own_ref, far_ref, near_ref, t):
    for k, rows in ((0, own_ref[...]), (1, near_ref[0]), (2, far_ref[...]), (3, near_ref[1])):
        at = k if t is None else t ^ k
        target[block(at, ROWS), :] = rows


def place_weight(target, refs, at_ref):
    pieces = []
    for ref in refs:
        pieces += [ref] if len(ref.shape) == 2 else [ref.at[i] for i in range(ref.shape[0])]
    z, r, R = at_ref[0], at_ref[1], len(pieces) // E
    local = D // len(pieces)
    for c in range(R):
        for d in range(E):
            at = block((z ^ d) * R + (r ^ c), local)
            target[at, :] = pieces[c * E + d][:local, :]


def load_weight(target, refs, at_ref):
    if refs[0].shape == target.shape:
        target[...] = refs[0][...]
    else:
        place_weight(target, refs, at_ref)


def send_rows(source, out_ref, at_ref):
    R, _, local, _ = out_ref.shape
    for c in range(R):
        for d in range(E):
            at = block((at_ref[0] ^ d) * R + (at_ref[1] ^ c), local)
            out_ref[c, d] = source[at, :].astype(BF)


def attention_forward(
    at_ref,
    own_ref,
    far_ref,
    near_ref,
    gain_ref,
    rel_ref,
    slots_ref,
    *rest,
    pieces,
):
    refs, rest = rest[:pieces], rest[pieces:]
    normed_ref, qkv_ref, probs_ref, heads_ref, kept_ref, sent_ref, tokens_ref, weight_ref = rest
    t, length = at_ref[2], at_ref[3]
    load_weight(weight_ref, refs, at_ref)
    place_rows(tokens_ref, own_ref, far_ref, near_ref, t)
    inputs = tokens_ref[...].astype(F32)
    normed_ref[...] = (inputs * norm_scale(inputs) * gain_ref[...]).astype(BF)
    qkv_ref[...] = mm(normed_ref[...], weight_ref[:, : 3 * LW], 1, 0).astype(BF)
    live = lax.broadcasted_iota(jnp.int32, (TILE, SEQ), 1) < length
    for h in range(LH):
        key = qkv_ref[:, LW + h * HD : LW + (h + 1) * HD]
        value = qkv_ref[:, 2 * LW + h * HD : 2 * LW + (h + 1) * HD]
        bias = jnp.broadcast_to(rel_ref[h : h + 1, :], (TILE, SPAN))
        for i in range(TILES):
            rows = slice(i * TILE, (i + 1) * TILE)
            query = qkv_ref[rows, h * HD : (h + 1) * HD]
            rolled = pltpu.roll(bias, SEQ + 1 + i * TILE, 1, stride=1, stride_axis=0)[:, :SEQ]
            scores = mm(query, key, 1, 1) * 0.125 + rolled
            scores = jnp.where(live, scores, -1e30)
            exponent = jnp.exp(scores - jnp.max(scores, axis=1, keepdims=True))
            probs = exponent / jnp.sum(exponent, axis=1, keepdims=True)
            probs_ref[h, rows, :] = probs
            heads_ref[rows, h * HD : (h + 1) * HD] = mm(probs.astype(BF), value, 1, 0).astype(BF)
    in_slots = mm(slots_ref[...], heads_ref[...], 1, 0).astype(BF)
    part = mm(in_slots, weight_ref[:, 3 * LW :], 1, 1).astype(BF)
    for k, out in ((0, kept_ref.at[0]), (1, sent_ref.at[0]), (2, kept_ref.at[1]), (3, sent_ref.at[1])):
        out[...] = part[k * ROWS : (k + 1) * ROWS]


def attention_backward(
    at_ref,
    own_ref,
    far_ref,
    near_ref,
    slots_ref,
    weight_ref,
    tokens_ref,
    normed_ref,
    qkv_ref,
    probs_ref,
    heads_ref,
    grads_ref,
    kept_ref,
    sent_ref,
    gain_ref,
    rel_ref,
    slot_scratch,
    heads_scratch,
    qkv_scratch,
    wide_scratch,
    weight_scratch,
):
    t = at_ref[2]
    place_rows(slot_scratch, own_ref, far_ref, near_ref, None)
    attended = mm(slots_ref[...], slot_scratch[...], 0, 0).astype(BF)
    heads_scratch[...] = mm(attended, weight_ref[:, 3 * LW :], 1, 0).astype(BF)
    weight_scratch[:, 3 * LW :] = mm(attended, heads_ref[...], 0, 0)
    flip = (
        lax.broadcasted_iota(jnp.int32, (TILE, TILE), 0)
        + lax.broadcasted_iota(jnp.int32, (TILE, TILE), 1)
        == TILE - 1
    ).astype(BF)
    rel_ref[...] = jnp.zeros_like(rel_ref)
    for h in range(LH):
        key = qkv_ref[:, LW + h * HD : LW + (h + 1) * HD]
        value = qkv_ref[:, 2 * LW + h * HD : 2 * LW + (h + 1) * HD]
        grad_key = jnp.zeros((SEQ, HD), F32)
        grad_value = jnp.zeros((SEQ, HD), F32)
        diagonal = [None] * (2 * TILES - 1)
        for i in range(TILES):
            rows = slice(i * TILE, (i + 1) * TILE)
            query = qkv_ref[rows, h * HD : (h + 1) * HD]
            grad = heads_scratch[rows, h * HD : (h + 1) * HD]
            probs = probs_ref[h, rows, :]
            grad_probs = mm(grad, value, 1, 1)
            inner = jnp.sum(probs * grad_probs, axis=1, keepdims=True)
            low = (probs * (grad_probs - inner)).astype(BF)
            qkv_scratch[rows, h * HD : (h + 1) * HD] = (mm(low, key, 1, 0) * 0.125).astype(BF)
            grad_key = grad_key + mm(low, query, 0, 0)
            grad_value = grad_value + mm(probs.astype(BF), grad, 0, 0)
            for j in range(TILES):
                turned = mm(low[:, j * TILE : (j + 1) * TILE], flip, 1, 0)
                at = i - j + TILES - 1
                diagonal[at] = turned if diagonal[at] is None else diagonal[at] + turned
        qkv_scratch[:, LW + h * HD : LW + (h + 1) * HD] = (grad_key * 0.125).astype(BF)
        qkv_scratch[:, 2 * LW + h * HD : 2 * LW + (h + 1) * HD] = grad_value.astype(BF)
        for at, part in enumerate(diagonal):
            wide = jnp.concatenate([part, jnp.zeros((TILE, TILE), F32)], axis=1)
            line = jnp.sum(pltpu.roll(wide, 0, 1, stride=1, stride_axis=0), axis=0, keepdims=True)
            rel_ref[h : h + 1, at * TILE : (at + 2) * TILE] += line
    weight_scratch[:, : 3 * LW] = mm(normed_ref[...], qkv_scratch[...], 0, 0)
    if len(grads_ref.shape) == 4:
        send_rows(weight_scratch, grads_ref, at_ref)
    else:
        grads_ref[...] = weight_scratch[...].astype(BF)
    wide_scratch[...] = mm(qkv_scratch[...], weight_ref[:, : 3 * LW], 1, 1)
    inputs = tokens_ref[...].astype(F32)
    gain_ref[...] = jnp.sum(
        wide_scratch[...] * inputs * norm_scale(inputs), axis=0, keepdims=True
    )
    for k, out in ((0, kept_ref.at[0]), (1, sent_ref.at[0]), (2, kept_ref.at[1]), (3, sent_ref.at[1])):
        out[...] = wide_scratch[block(t ^ k, ROWS), :].astype(BF)


def expert_layer(
    at_ref,
    own_ref,
    far_ref,
    near_ref,
    own_grad_ref,
    far_grad_ref,
    near_grad_ref,
    router_ref,
    *rest,
    pieces,
):
    in_refs, out_refs, rest = rest[:pieces], rest[pieces : 2 * pieces], rest[2 * pieces :]
    buffer_ref, grad_ref, activation_ref, grad_pre_ref, kept_ref, sent_ref, in_ref, out_ref = rest
    load_weight(in_ref, in_refs, at_ref)
    load_weight(out_ref, out_refs, at_ref)
    place_rows(buffer_ref, own_ref, far_ref, near_ref, None)
    place_rows(grad_ref, own_grad_ref, far_grad_ref, near_grad_ref, None)
    logits = mm(buffer_ref[...], router_ref[...], 1, 0)
    lane = lax.broadcasted_iota(jnp.int32, logits.shape, 1)
    logits = jnp.where(lane < E, logits, -1e30)
    exponent = jnp.exp(logits - jnp.max(logits, axis=1, keepdims=True))
    mine = jnp.sum(jnp.where(lane == at_ref[0], exponent, 0.0), axis=1, keepdims=True)
    gate = mine / jnp.sum(exponent, axis=1, keepdims=True)
    grad_ref[...] = (gate * grad_ref[...].astype(F32)).astype(BF)
    pre = mm(buffer_ref[...], in_ref[...], 1, 0)
    square = pre * pre
    tanh = jnp.tanh(0.7978845608028654 * (pre + 0.044715 * pre * square))
    half = 0.5 * (1.0 + tanh)
    activation_ref[...] = (pre * half).astype(BF)
    slope = half + 0.5 * pre * (1.0 - tanh * tanh) * (
        0.7978845608028654 * (1.0 + 3.0 * 0.044715 * square)
    )
    grad_act = mm(grad_ref[...], out_ref[...], 1, 0)
    grad_pre_ref[...] = (grad_act * slope).astype(BF)
    for k, out in ((0, kept_ref.at[0]), (1, sent_ref.at[0]), (2, kept_ref.at[1]), (3, sent_ref.at[1])):
        rows = slice(k * ROWS, (k + 1) * ROWS)
        out[:, :D] = mm(activation_ref[rows, :], out_ref[...], 1, 1).astype(BF)
        out[:, D:] = mm(grad_pre_ref[rows, :], in_ref[...], 1, 1).astype(BF)


def weight_gradient(at_ref, left_ref, right_ref, out_ref, scratch):
    scratch[...] = mm(left_ref[...], right_ref[...], 0, 0)
    if len(out_ref.shape) == 4:
        send_rows(scratch, out_ref, at_ref)
    else:
        out_ref[...] = scratch[...].astype(BF)


def norm_scale(values):
    return lax.rsqrt(jnp.mean(values * values, axis=-1, keepdims=True) + EPSILON)


def norm_back(grad, values, scale, gain):
    u = grad * gain
    inner = jnp.mean(u * values, axis=-1, keepdims=True)
    return scale * u - scale * scale * scale * values * inner


def body(
    tokens,
    cotangent,
    w_qkv,
    w_out_attn,
    w_router,
    w_in,
    w_out,
    norm1_gain,
    norm2_gain,
    bias_table,
    seq_length,
    expert_ids,
    expert_slots,
    buckets,
):
    n = lax.axis_size("dp")
    R = n // E
    at_dp = lax.axis_index("dp")
    z, r = at_dp // R, at_dp % R
    t = lax.axis_index("tensor")
    local = D // n
    width = w_in.shape[2]
    aligned = local % 16 == 0
    place_at = jnp.stack([z, r, t, seq_length[0]]).astype(jnp.int32)

    def whole(parts):
        if aligned:
            return parts
        pieces = []
        for part in parts:
            pieces += [part] if part.ndim == 2 else list(part)
        pieces = [piece[:local] for piece in pieces]
        rows = [jnp.stack(natural(pieces[c * E : (c + 1) * E], z)) for c in range(R)]
        return [jnp.stack(natural(rows, r), axis=1).reshape(D, -1)]

    def blocks_to_send(grad):
        if aligned:
            return grad
        x = grad.reshape(E, R, local, -1)
        x = jnp.stack([pick(x, r ^ c, 1) for c in range(R)])
        return jnp.stack([pick(x, z ^ d, 1) for d in range(E)], axis=1)

    grads_shape = (R, E, local) if aligned else (D,)

    line = jnp.concatenate([w_router.T.reshape(-1), norm1_gain, norm2_gain, bias_table])
    line = jnp.pad(line, (0, 4 * LW - line.shape[0]))[None]
    packed = jnp.concatenate(
        [jnp.concatenate([w_qkv.reshape(local, 3 * LW), w_out_attn], axis=1), line], axis=0
    )
    packed_z = [packed] + [over_z(packed, d) for d in range(1, E)]
    packed_own = [over_r(packed, c) for c in range(1, R)]
    packed_rest = after(jnp.stack([part[:local] for part in packed_z[1:]]), packed_own)
    packed_all = list(packed_z)
    for c in range(1, R):
        packed_all += [packed_own[c - 1], over_r(packed_rest, c)]
    lines = jnp.stack(natural([part[local] for part in packed_z], z))
    lines = [lines] + [over_r(lines, c) for c in range(1, R)]
    lines = jnp.stack(natural(lines, r), axis=1).reshape(n, -1)
    router_rows = lines[:, : local * E].reshape(n, E, local).transpose(1, 0, 2).reshape(E, D)
    gain_one = lines[:, local * E : local * (E + 1)].reshape(1, D).astype(F32)
    gain_two = lines[:, local * (E + 1) : local * (E + 2)].reshape(1, D).astype(F32)
    table_flat = lines[:, local * (E + 2) : local * (E + 2) + H * NB // n].reshape(-1)

    both_parts = gather_t(jnp.concatenate([tokens, cotangent], axis=1))
    token_parts = [part[..., :D] for part in both_parts]
    cotangent_all = jnp.concatenate(natural([p[:, D:] for p in in_order(both_parts)], t), axis=0)

    sent = expert_slots >= 0
    absolute = jnp.where(sent, expert_ids * CAP + expert_slots, -1)
    position = jnp.arange(SEQ, dtype=jnp.int32)
    empty = ~jnp.any(absolute[None, :] == position[:, None], axis=1)
    before = position[None, :] <= position[:, None]
    empty_rank = jnp.sum((before & empty[None, :]).astype(jnp.int32), axis=1)
    unsent_rank = jnp.sum((before & ~sent[None, :]).astype(jnp.int32), axis=1)
    match = empty[None, :] & (empty_rank[None, :] == unsent_rank[:, None])
    spare = jnp.sum(jnp.where(match, position[None, :], 0), axis=1)
    slot = jnp.where(sent, absolute, spare)
    in_expert = slot % CAP
    place = ((in_expert // SUB) ^ t) * ROWS + ((slot // CAP) ^ z) * SUB + in_expert % SUB
    to_slots_mask = place[None, :] == position[:, None]
    to_slots = to_slots_mask.astype(BF)
    own_mask = to_slots_mask[:ROWS]
    sent_own = jnp.any(own_mask & sent[None, :], axis=1)
    chosen_own = jnp.sum(jnp.where(own_mask, expert_ids[None, :], 0), axis=1)
    own_tokens = lax.dynamic_slice_in_dim(place, t * ROWS, ROWS, 0)
    from_slots_own = (own_tokens[:, None] == position[None, :]).astype(BF)

    def dispatch_z(rows):
        rows = jnp.where(sent_own[:, None], rows, 0).astype(BF)
        return jnp.concatenate(deliver_z(rows.reshape(E, SUB, D)), axis=0)

    grad_output = mm(to_slots[:ROWS], cotangent_all, 1, 0)
    masked = jnp.where(sent_own[:, None], grad_output, 0).astype(BF).reshape(E, SUB, D)
    in_rows = after(w_in, packed_z, packed_own, both_parts[1])
    in_columns = jnp.stack(deliver_z(jnp.stack([pick(in_rows, z ^ d, 1) for d in range(E)])))
    out_rows = after(w_out, in_columns)
    out_rows = jnp.stack([pick(out_rows, z ^ d, 1) for d in range(E)])
    out_z = jnp.stack(deliver_z(jnp.concatenate([out_rows, masked], axis=1)))
    out_columns, cotangent_z = out_z[:, :local], out_z[:, local:].reshape(E * SUB, D)
    in_weight = whole([in_columns] + [over_r(in_columns, c) for c in range(1, R)])
    out_weight = whole([out_columns] + [over_r(out_columns, c) for c in range(1, R)])
    cotangent_parts = gather_t(cotangent_z)

    table_rows = lax.dynamic_slice_in_dim(table_flat.astype(F32).reshape(H, NB), t * LH, LH, 0)
    bucket_table = (buckets[None, :] == jnp.arange(NB, dtype=jnp.int32)[:, None]).astype(F32)
    reversed_rel = jnp.dot(
        table_rows,
        jnp.pad(bucket_table[:, ::-1], ((0, 0), (0, 1))),
        precision=HIGHEST_PRECISION,
    )
    packed_refs = whole(packed_all)
    forward = call(
        functools.partial(attention_forward, pieces=len(packed_refs)),
        "attention_forward",
        12,
        [
            ((SEQ, D), BF),
            ((SEQ, 3 * LW), BF),
            ((LH, SEQ, SEQ), F32),
            ((SEQ, LW), BF),
            ((2, ROWS, D), BF),
            ((2, ROWS, D), BF),
            ((SEQ, D), BF),
            ((D, 4 * LW), BF),
        ],
        [],
        place_at,
        *token_parts,
        gain_one,
        reversed_rel,
        after(to_slots, in_columns),
        *packed_refs,
    )
    normed_all, qkv, probs, heads_all, kept, given, tokens_all, attention_weight = forward
    attended = scatter_t(kept, given)
    inputs = mm(to_slots[:ROWS], tokens_all, 1, 0)
    middle = inputs + attended
    scale_two = norm_scale(middle)
    normed_two = (middle * scale_two * gain_two).astype(BF)

    buffer_parts = gather_t(dispatch_z(after(normed_two, out_z, in_weight)), out_weight)
    router = jnp.pad(router_rows.T, ((0, 0), (0, 128 - E)))
    buffer, grad_expert, activation, grad_pre, kept, given = call(
        functools.partial(expert_layer, pieces=len(in_weight)),
        "expert_layer",
        8,
        [
            ((SEQ, D), BF),
            ((SEQ, D), BF),
            ((SEQ, width), BF),
            ((SEQ, width), BF),
            ((2, ROWS, 2 * D), BF),
            ((2, ROWS, 2 * D), BF),
        ],
        [((D, width), BF), ((D, width), BF)],
        place_at,
        *buffer_parts,
        *cotangent_parts,
        router,
        *in_weight,
        *out_weight,
    )


    def expert_gradient(name, left, right):
        (out,) = call(
            weight_gradient,
            name,
            2,
            [((*grads_shape, width), BF)],
            [((D, width), F32)],
            place_at,
            left,
            right,
        )
        return blocks_to_send(out)

    out_terms = expert_gradient("grad_w_out", grad_expert, activation)
    in_terms = expert_gradient("grad_w_in", buffer, grad_pre)
    mine = scatter_t(kept, given).astype(BF)
    out_sums = add(swap_r(out_terms)).astype(BF)
    in_sums = add(swap_r(after(in_terms, out_sums, mine))).astype(BF)
    returned = deliver_z(after(mine, out_sums).reshape(E, SUB, 2 * D))
    returned = jnp.concatenate(returned, axis=0).astype(F32)
    combined, grad_normed_two = returned[:, :D], returned[:, D:]

    experts = jnp.arange(E, dtype=jnp.int32)[None, :]
    route = jax.nn.softmax(mm(normed_two, router_rows, 1, 1), axis=-1)
    chosen = experts == chosen_own[:, None]
    gate = jnp.sum(jnp.where(chosen, route, 0.0), axis=-1)
    layer_rows = (middle + gate[:, None] * combined).astype(BF)
    grad_gate = jnp.sum(grad_output * combined, axis=-1)
    grad_logits = gate[:, None] * (chosen.astype(F32) - route) * grad_gate[:, None]
    grad_router = lax.dot_general(
        grad_logits,
        normed_two.astype(F32),
        (((0,), (0,)), ((), ())),
        precision=HIGHEST_PRECISION,
    )
    grad_normed_two = grad_normed_two + jnp.dot(
        grad_logits, router_rows.astype(F32), precision=HIGHEST_PRECISION
    )
    grad_gain_two = jnp.sum(grad_normed_two * middle * scale_two, axis=0, keepdims=True)
    grad_middle = (grad_output + norm_back(grad_normed_two, middle, scale_two, gain_two)).astype(BF)
    grad_parts = gather_t(grad_middle, in_sums)

    late_terms, kept, given, grad_gain_one, grad_rel = call(
        attention_backward,
        "attention_backward",
        12,
        [
            ((*grads_shape, 4 * LW), BF),
            ((2, ROWS, D), BF),
            ((2, ROWS, D), BF),
            ((1, D), F32),
            ((LH, SPAN), F32),
        ],
        [
            ((SEQ, D), BF),
            ((SEQ, LW), BF),
            ((SEQ, 3 * LW), BF),
            ((SEQ, D), F32),
            ((D, 4 * LW), F32),
        ],
        place_at,
        *grad_parts,
        to_slots,
        attention_weight,
        tokens_all,
        normed_all,
        qkv,
        probs,
        heads_all,
    )
    expert_sums = jnp.stack([in_sums, out_sums], axis=1)
    delivered = deliver_z(after(expert_sums, grad_middle))
    late_terms = swap_r(blocks_to_send(late_terms))
    delivered = after(delivered, late_terms)
    late_sums = add(late_terms)
    given = over_t(after(given, late_terms), 1)
    layer_parts = gather_t(after(layer_rows, given))
    grad_normed_one = finish_scatter(kept, given)
    own_inputs = tokens.astype(F32)
    grad_slots = jnp.concatenate(in_order(grad_parts), axis=0)
    grad_tokens = mm(from_slots_own, grad_slots, 1, 0) + norm_back(
        grad_normed_one, own_inputs, norm_scale(own_inputs), gain_one
    )
    layer_slots = jnp.concatenate(in_order(layer_parts), axis=0)
    layer_out = mm(from_slots_own, layer_slots, 1, 0).astype(BF)
    grad_table_rows = lax.dot_general(
        grad_rel[:, : 2 * SEQ - 1],
        bucket_table,
        (((1,), (1,)), ((), ())),
        precision=HIGHEST_PRECISION,
    )
    grad_table = lax.dynamic_update_slice_in_dim(
        jnp.zeros((H, NB), F32), grad_table_rows, t * LH, 0
    ).reshape(1, -1)
    small = sum_but_z(
        jnp.concatenate(
            [
                grad_router,
                grad_gain_two,
                grad_gain_one,
                jnp.pad(grad_table, ((0, 0), (0, D - H * NB))),
                jnp.zeros((1, D), F32),
            ],
            axis=0,
        ),
        late_terms,
    )
    low = after(small, given, layer_parts[1]).astype(BF)
    late = [over_z(jnp.concatenate([late_sums[d].astype(BF), low], axis=0), d) for d in (3, 2, 1)]
    late, grad_tokens = after((late, grad_tokens), layer_out)
    late = jnp.concatenate([late_sums[0], small], axis=0) + add(late)
    late, small = late[:local], late[local:]
    small_own = lax.dynamic_slice_in_dim(small[: E + 2], at_dp * local, local, 1)
    table_own = lax.dynamic_slice_in_dim(small[E + 2], at_dp * (H * NB // n), H * NB // n, 0)
    return (
        layer_out,
        grad_tokens,
        late[:, : 3 * LW].reshape(local, 3, LW),
        late[:, 3 * LW :],
        small_own[:E].T,
        jnp.stack(natural([part[0] for part in delivered], z), axis=1).astype(F32),
        jnp.stack(natural([part[1] for part in delivered], z), axis=1).astype(F32),
        small_own[E + 1],
        small_own[E],
        table_own,
    )


def solution(mesh):
    in_specs = (
        P(("dp", "tensor"), None),
        P(("dp", "tensor"), None),
        P("dp", None, "tensor"),
        P("dp", "tensor"),
        P("dp", None),
        P("dp", None, "tensor"),
        P("dp", None, "tensor"),
        P("dp"),
        P("dp"),
        P("dp"),
        P("dp"),
        P("dp"),
        P("dp"),
        P(),
    )
    out_specs = (
        P(("dp", "tensor"), None),
        P(("dp", "tensor"), None),
        P("dp", None, "tensor"),
        P("dp", "tensor"),
        P("dp", None),
        P("dp", None, "tensor"),
        P("dp", None, "tensor"),
        P("dp"),
        P("dp"),
        P("dp"),
    )
    return jax.shard_map(body, mesh=mesh, in_specs=in_specs, out_specs=out_specs, check_vma=False)
```

```python
import functools

import jax
import jax.numpy as jnp
from jax import lax
from jax.experimental import pallas as pl
from jax.experimental.pallas import tpu as pltpu
from jax.sharding import PartitionSpec as P

D = 768
H = 12
HD = 64
NB = 32
E = 4
SEQ = 512
CAP = 128
T = 4
LH = H // T
LW = LH * HD
ROWS = SEQ // T
SUB = CAP // T
SPAN = 2 * SEQ
TILE = 128
TILES = SEQ // TILE

EPSILON = 1e-06
HIGHEST_PRECISION = lax.Precision.HIGHEST
BF = jnp.bfloat16
F32 = jnp.float32


def mm(a, b, ca, cb):
    return lax.dot_general(a, b, (((ca,), (cb,)), ((), ())), preferred_element_type=F32)


def over_t(x, k):
    return lax.ppermute(x, "tensor", [(i, i ^ k) for i in range(T)])


def over_z(x, d):
    n = lax.axis_size("dp")
    r = n // E
    return lax.ppermute(x, "dp", [(i, ((i // r) ^ d) * r + i % r) for i in range(n)])


def over_r(x, c):
    n = lax.axis_size("dp")
    r = n // E
    return lax.ppermute(x, "dp", [(i, (i // r) * r + ((i % r) ^ c)) for i in range(n)])


def natural(parts, index):
    bit = 1
    while bit < len(parts):
        flip = (index & bit) != 0
        parts = [jnp.where(flip, parts[j ^ bit], parts[j]) for j in range(len(parts))]
        bit *= 2
    return parts


def gather_t(x, *earlier):
    far = over_t(x, 2)
    return x, far, over_t(after(jnp.stack([x, far]), *earlier), 1)


def in_order(gathered):
    own, far, near = gathered
    return [own, near[0], far, near[1]]


def scatter_t(kept, sent):
    return finish_scatter(kept, over_t(sent, 1))


def finish_scatter(kept, first):
    first = first.astype(F32)
    away = (kept[1].astype(F32) + first[1]).astype(BF)
    return kept[0].astype(F32) + first[0] + over_t(away, 2).astype(F32)


def pick(x, index, axis):
    return lax.dynamic_index_in_dim(x, index, axis, keepdims=False)


def after(x, *others):
    return lax.optimization_barrier((x, others))[0]


def swap_r(x):
    return [x[0]] + [over_r(x[c], c) for c in range(1, x.shape[0])]


def add(terms):
    return sum(term.astype(F32) for term in terms)


def deliver_z(x):
    return [x[0]] + [over_z(x[d], d) for d in range(1, E)]


def sum_but_z(x, *earlier):
    R = lax.axis_size("dp") // E
    c = 1
    while c < R:
        x = x + over_r(x, c)
        c *= 2
    x = x + over_t(x, 2)
    x = after(x, *earlier)
    return x + over_t(x, 1)


VMEM = pl.BlockSpec(memory_space=pltpu.VMEM)
SMEM = pl.BlockSpec(memory_space=pltpu.SMEM)
PARAMS = pltpu.CompilerParams(vmem_limit_bytes=48 * 2**20)


def call(kernel, name, micros, outs, scratch, at, *operands):
    moved = sum(a.size * a.dtype.itemsize for a in operands)
    return pl.pallas_call(
        kernel,
        out_shape=[jax.ShapeDtypeStruct(shape, kind) for shape, kind in outs],
        in_specs=[SMEM] + [VMEM] * len(operands),
        out_specs=[VMEM] * len(outs),
        scratch_shapes=[pltpu.VMEM(shape, kind) for shape, kind in scratch],
        compiler_params=PARAMS,
        cost_estimate=pl.CostEstimate(
            flops=micros * 10**9, bytes_accessed=moved, transcendentals=0
        ),
        name=name,
    )(at, *operands)


def block(index, length):
    return pl.ds(pl.multiple_of(index * length, length), length)


def place_rows(target, own_ref, far_ref, near_ref, t):
    for k, rows in ((0, own_ref[...]), (1, near_ref[0]), (2, far_ref[...]), (3, near_ref[1])):
        at = k if t is None else t ^ k
        target[block(at, ROWS), :] = rows


def place_weight(target, refs, at_ref, local):
    z, r, R = at_ref[0], at_ref[1], len(refs)
    for c in range(R):
        for d in range(E):
            target[block((z ^ d) * R + (r ^ c), local), :] = refs[c][d, :local, :]


def send_rows(source, out_ref, at_ref):
    R, _, local, _ = out_ref.shape
    for c in range(R):
        for d in range(E):
            at = block((at_ref[0] ^ d) * R + (at_ref[1] ^ c), local)
            out_ref[c, d] = source[at, :].astype(BF)


def attention_forward(
    at_ref,
    own_ref,
    far_ref,
    near_ref,
    gain_ref,
    rel_ref,
    slots_ref,
    *rest,
    pieces,
):
    refs, rest = rest[:pieces], rest[pieces:]
    normed_ref, qkv_ref, probs_ref, heads_ref, kept_ref, sent_ref, tokens_ref, weight_ref = rest
    t, length = at_ref[2], at_ref[3]
    if pieces == 1:
        weight_ref[...] = refs[0][...]
    else:
        place_weight(weight_ref, refs, at_ref, D // (pieces * E))
    place_rows(tokens_ref, own_ref, far_ref, near_ref, t)
    inputs = tokens_ref[...].astype(F32)
    normed_ref[...] = (inputs * norm_scale(inputs) * gain_ref[...]).astype(BF)
    qkv_ref[...] = mm(normed_ref[...], weight_ref[:, : 3 * LW], 1, 0).astype(BF)
    live = lax.broadcasted_iota(jnp.int32, (TILE, SEQ), 1) < length
    for h in range(LH):
        key = qkv_ref[:, LW + h * HD : LW + (h + 1) * HD]
        value = qkv_ref[:, 2 * LW + h * HD : 2 * LW + (h + 1) * HD]
        bias = jnp.broadcast_to(rel_ref[h : h + 1, :], (TILE, SPAN))
        for i in range(TILES):
            rows = slice(i * TILE, (i + 1) * TILE)
            query = qkv_ref[rows, h * HD : (h + 1) * HD]
            rolled = pltpu.roll(bias, SEQ + 1 + i * TILE, 1, stride=1, stride_axis=0)[:, :SEQ]
            scores = mm(query, key, 1, 1) * 0.125 + rolled
            scores = jnp.where(live, scores, -1e30)
            exponent = jnp.exp(scores - jnp.max(scores, axis=1, keepdims=True))
            probs = exponent / jnp.sum(exponent, axis=1, keepdims=True)
            probs_ref[h, rows, :] = probs
            heads_ref[rows, h * HD : (h + 1) * HD] = mm(probs.astype(BF), value, 1, 0).astype(BF)
    in_slots = mm(slots_ref[...], heads_ref[...], 1, 0).astype(BF)
    part = mm(in_slots, weight_ref[:, 3 * LW :], 1, 1).astype(BF)
    for k, out in ((0, kept_ref.at[0]), (1, sent_ref.at[0]), (2, kept_ref.at[1]), (3, sent_ref.at[1])):
        out[...] = part[k * ROWS : (k + 1) * ROWS]


def attention_backward(
    at_ref,
    own_ref,
    far_ref,
    near_ref,
    slots_ref,
    weight_ref,
    tokens_ref,
    normed_ref,
    qkv_ref,
    probs_ref,
    heads_ref,
    grads_ref,
    kept_ref,
    sent_ref,
    gain_ref,
    rel_ref,
    slot_scratch,
    heads_scratch,
    qkv_scratch,
    wide_scratch,
    weight_scratch,
):
    t = at_ref[2]
    place_rows(slot_scratch, own_ref, far_ref, near_ref, None)
    attended = mm(slots_ref[...], slot_scratch[...], 0, 0).astype(BF)
    heads_scratch[...] = mm(attended, weight_ref[:, 3 * LW :], 1, 0).astype(BF)
    weight_scratch[:, 3 * LW :] = mm(attended, heads_ref[...], 0, 0)
    flip = (
        lax.broadcasted_iota(jnp.int32, (TILE, TILE), 0)
        + lax.broadcasted_iota(jnp.int32, (TILE, TILE), 1)
        == TILE - 1
    ).astype(BF)
    rel_ref[...] = jnp.zeros_like(rel_ref)
    for h in range(LH):
        key = qkv_ref[:, LW + h * HD : LW + (h + 1) * HD]
        value = qkv_ref[:, 2 * LW + h * HD : 2 * LW + (h + 1) * HD]
        grad_key = jnp.zeros((SEQ, HD), F32)
        grad_value = jnp.zeros((SEQ, HD), F32)
        diagonal = [None] * (2 * TILES - 1)
        for i in range(TILES):
            rows = slice(i * TILE, (i + 1) * TILE)
            query = qkv_ref[rows, h * HD : (h + 1) * HD]
            grad = heads_scratch[rows, h * HD : (h + 1) * HD]
            probs = probs_ref[h, rows, :]
            grad_probs = mm(grad, value, 1, 1)
            inner = jnp.sum(probs * grad_probs, axis=1, keepdims=True)
            low = (probs * (grad_probs - inner)).astype(BF)
            qkv_scratch[rows, h * HD : (h + 1) * HD] = (mm(low, key, 1, 0) * 0.125).astype(BF)
            grad_key = grad_key + mm(low, query, 0, 0)
            grad_value = grad_value + mm(probs.astype(BF), grad, 0, 0)
            for j in range(TILES):
                turned = mm(low[:, j * TILE : (j + 1) * TILE], flip, 1, 0)
                at = i - j + TILES - 1
                diagonal[at] = turned if diagonal[at] is None else diagonal[at] + turned
        qkv_scratch[:, LW + h * HD : LW + (h + 1) * HD] = (grad_key * 0.125).astype(BF)
        qkv_scratch[:, 2 * LW + h * HD : 2 * LW + (h + 1) * HD] = grad_value.astype(BF)
        for at, part in enumerate(diagonal):
            wide = jnp.concatenate([part, jnp.zeros((TILE, TILE), F32)], axis=1)
            line = jnp.sum(pltpu.roll(wide, 0, 1, stride=1, stride_axis=0), axis=0, keepdims=True)
            rel_ref[h : h + 1, at * TILE : (at + 2) * TILE] += line
    weight_scratch[:, : 3 * LW] = mm(normed_ref[...], qkv_scratch[...], 0, 0)
    if len(grads_ref.shape) == 4:
        send_rows(weight_scratch, grads_ref, at_ref)
    else:
        grads_ref[...] = weight_scratch[...].astype(BF)
    wide_scratch[...] = mm(qkv_scratch[...], weight_ref[:, : 3 * LW], 1, 1)
    inputs = tokens_ref[...].astype(F32)
    gain_ref[...] = jnp.sum(
        wide_scratch[...] * inputs * norm_scale(inputs), axis=0, keepdims=True
    )
    for k, out in ((0, kept_ref.at[0]), (1, sent_ref.at[0]), (2, kept_ref.at[1]), (3, sent_ref.at[1])):
        out[...] = wide_scratch[block(t ^ k, ROWS), :].astype(BF)


def expert_layer(
    at_ref,
    own_ref,
    far_ref,
    near_ref,
    own_grad_ref,
    far_grad_ref,
    near_grad_ref,
    router_ref,
    *rest,
    pieces,
):
    in_refs, out_refs, rest = rest[:pieces], rest[pieces : 2 * pieces], rest[2 * pieces :]
    buffer_ref, grad_ref, activation_ref, grad_pre_ref, kept_ref, sent_ref, in_ref, out_ref = rest
    if pieces == 1:
        in_ref[...] = in_refs[0][...]
        out_ref[...] = out_refs[0][...]
    else:
        place_weight(in_ref, in_refs, at_ref, D // (pieces * E))
        place_weight(out_ref, out_refs, at_ref, D // (pieces * E))
    place_rows(buffer_ref, own_ref, far_ref, near_ref, None)
    place_rows(grad_ref, own_grad_ref, far_grad_ref, near_grad_ref, None)
    logits = mm(buffer_ref[...], router_ref[...], 1, 0)
    lane = lax.broadcasted_iota(jnp.int32, logits.shape, 1)
    logits = jnp.where(lane < E, logits, -1e30)
    exponent = jnp.exp(logits - jnp.max(logits, axis=1, keepdims=True))
    mine = jnp.sum(jnp.where(lane == at_ref[0], exponent, 0.0), axis=1, keepdims=True)
    gate = mine / jnp.sum(exponent, axis=1, keepdims=True)
    grad_ref[...] = (gate * grad_ref[...].astype(F32)).astype(BF)
    pre = mm(buffer_ref[...], in_ref[...], 1, 0)
    square = pre * pre
    tanh = jnp.tanh(0.7978845608028654 * (pre + 0.044715 * pre * square))
    half = 0.5 * (1.0 + tanh)
    activation_ref[...] = (pre * half).astype(BF)
    slope = half + 0.5 * pre * (1.0 - tanh * tanh) * (
        0.7978845608028654 * (1.0 + 3.0 * 0.044715 * square)
    )
    grad_act = mm(grad_ref[...], out_ref[...], 1, 0)
    grad_pre_ref[...] = (grad_act * slope).astype(BF)
    for k, out in ((0, kept_ref.at[0]), (1, sent_ref.at[0]), (2, kept_ref.at[1]), (3, sent_ref.at[1])):
        rows = slice(k * ROWS, (k + 1) * ROWS)
        out[:, :D] = mm(activation_ref[rows, :], out_ref[...], 1, 1).astype(BF)
        out[:, D:] = mm(grad_pre_ref[rows, :], in_ref[...], 1, 1).astype(BF)


def weight_gradient(at_ref, left_ref, right_ref, out_ref, scratch):
    scratch[...] = mm(left_ref[...], right_ref[...], 0, 0)
    if len(out_ref.shape) == 4:
        send_rows(scratch, out_ref, at_ref)
    else:
        out_ref[...] = scratch[...].astype(BF)


def norm_scale(values):
    return lax.rsqrt(jnp.mean(values * values, axis=-1, keepdims=True) + EPSILON)


def norm_back(grad, values, scale, gain):
    u = grad * gain
    inner = jnp.mean(u * values, axis=-1, keepdims=True)
    return scale * u - scale * scale * scale * values * inner


def body(
    tokens,
    cotangent,
    w_qkv,
    w_out_attn,
    w_router,
    w_in,
    w_out,
    norm1_gain,
    norm2_gain,
    bias_table,
    seq_length,
    expert_ids,
    expert_slots,
    buckets,
):
    n = lax.axis_size("dp")
    R = n // E
    at_dp = lax.axis_index("dp")
    z, r = at_dp // R, at_dp % R
    t = lax.axis_index("tensor")
    local = D // n
    width = w_in.shape[2]
    aligned = local % 16 == 0
    place_at = jnp.stack([z, r, t, seq_length[0]]).astype(jnp.int32)

    def whole(parts):
        if aligned:
            return [jnp.stack(part) if isinstance(part, list) else part for part in parts]
        rows = [jnp.stack(natural(list(part), z)) for part in parts]
        return [jnp.stack(natural(rows, r), axis=1).reshape(D, -1)]

    def blocks_to_send(grad):
        if aligned:
            return grad
        x = grad.reshape(E, R, local, -1)
        x = jnp.stack([pick(x, r ^ c, 1) for c in range(R)])
        return jnp.stack([pick(x, z ^ d, 1) for d in range(E)], axis=1)

    grads_shape = (R, E, local) if aligned else (D,)

    line = jnp.concatenate([w_router.T.reshape(-1), norm1_gain, norm2_gain, bias_table])
    line = jnp.pad(line, (0, 4 * LW - line.shape[0]))[None]
    packed = jnp.concatenate(
        [jnp.concatenate([w_qkv.reshape(local, 3 * LW), w_out_attn], axis=1), line], axis=0
    )
    packed_z = [packed] + [over_z(packed, d) for d in range(1, E)]
    packed_r = [
        [over_r(packed, c), *over_r(jnp.stack([part[:local] for part in packed_z[1:]]), c)]
        for c in range(1, R)
    ]
    packed_all = [[part[:local] for part in parts] for parts in [packed_z] + packed_r]
    lines = jnp.stack(natural([part[local] for part in packed_z], z))
    lines = [lines] + [over_r(lines, c) for c in range(1, R)]
    lines = jnp.stack(natural(lines, r), axis=1).reshape(n, -1)
    router_rows = lines[:, : local * E].reshape(n, E, local).transpose(1, 0, 2).reshape(E, D)
    gain_one = lines[:, local * E : local * (E + 1)].reshape(1, D).astype(F32)
    gain_two = lines[:, local * (E + 1) : local * (E + 2)].reshape(1, D).astype(F32)
    table_flat = lines[:, local * (E + 2) : local * (E + 2) + H * NB // n].reshape(-1)

    both_parts = gather_t(jnp.concatenate([tokens, cotangent], axis=1))
    token_parts = [part[..., :D] for part in both_parts]
    cotangent_all = jnp.concatenate(natural([p[:, D:] for p in in_order(both_parts)], t), axis=0)

    sent = expert_slots >= 0
    absolute = jnp.where(sent, expert_ids * CAP + expert_slots, -1)
    position = jnp.arange(SEQ, dtype=jnp.int32)
    empty = ~jnp.any(absolute[None, :] == position[:, None], axis=1)
    before = position[None, :] <= position[:, None]
    empty_rank = jnp.sum((before & empty[None, :]).astype(jnp.int32), axis=1)
    unsent_rank = jnp.sum((before & ~sent[None, :]).astype(jnp.int32), axis=1)
    match = empty[None, :] & (empty_rank[None, :] == unsent_rank[:, None])
    spare = jnp.sum(jnp.where(match, position[None, :], 0), axis=1)
    slot = jnp.where(sent, absolute, spare)
    in_expert = slot % CAP
    place = ((in_expert // SUB) ^ t) * ROWS + ((slot // CAP) ^ z) * SUB + in_expert % SUB
    to_slots_mask = place[None, :] == position[:, None]
    to_slots = to_slots_mask.astype(BF)
    own_mask = to_slots_mask[:ROWS]
    sent_own = jnp.any(own_mask & sent[None, :], axis=1)
    chosen_own = jnp.sum(jnp.where(own_mask, expert_ids[None, :], 0), axis=1)
    own_tokens = lax.dynamic_slice_in_dim(place, t * ROWS, ROWS, 0)
    from_slots_own = (own_tokens[:, None] == position[None, :]).astype(BF)

    def dispatch_z(rows):
        rows = jnp.where(sent_own[:, None], rows, 0).astype(BF)
        return jnp.concatenate(deliver_z(rows.reshape(E, SUB, D)), axis=0)

    grad_output = mm(to_slots[:ROWS], cotangent_all, 1, 0)
    masked = jnp.where(sent_own[:, None], grad_output, 0).astype(BF).reshape(E, SUB, D)
    in_rows = after(w_in, packed_z)
    in_columns = jnp.stack(deliver_z(jnp.stack([pick(in_rows, z ^ d, 1) for d in range(E)])))
    out_rows = after(w_out, in_columns)
    out_rows = jnp.stack([pick(out_rows, z ^ d, 1) for d in range(E)])
    out_z = jnp.stack(deliver_z(jnp.concatenate([out_rows, masked], axis=1)))
    out_columns, cotangent_z = out_z[:, :local], out_z[:, local:].reshape(E * SUB, D)
    in_weight = whole([in_columns] + [over_r(in_columns, c) for c in range(1, R)])
    out_weight = whole([out_columns] + [over_r(out_columns, c) for c in range(1, R)])
    cotangent_parts = gather_t(cotangent_z)

    table_rows = lax.dynamic_slice_in_dim(table_flat.astype(F32).reshape(H, NB), t * LH, LH, 0)
    bucket_table = (buckets[None, :] == jnp.arange(NB, dtype=jnp.int32)[:, None]).astype(F32)
    reversed_rel = jnp.dot(
        table_rows,
        jnp.pad(bucket_table[:, ::-1], ((0, 0), (0, 1))),
        precision=HIGHEST_PRECISION,
    )
    packed_refs = whole(packed_all)
    forward = call(
        functools.partial(attention_forward, pieces=len(packed_refs)),
        "attention_forward",
        12,
        [
            ((SEQ, D), BF),
            ((SEQ, 3 * LW), BF),
            ((LH, SEQ, SEQ), F32),
            ((SEQ, LW), BF),
            ((2, ROWS, D), BF),
            ((2, ROWS, D), BF),
            ((SEQ, D), BF),
            ((D, 4 * LW), BF),
        ],
        [],
        place_at,
        *token_parts,
        gain_one,
        reversed_rel,
        after(to_slots, in_columns),
        *packed_refs,
    )
    normed_all, qkv, probs, heads_all, kept, given, tokens_all, attention_weight = forward
    attended = scatter_t(kept, given)
    inputs = mm(to_slots[:ROWS], tokens_all, 1, 0)
    middle = inputs + attended
    scale_two = norm_scale(middle)
    normed_two = (middle * scale_two * gain_two).astype(BF)

    buffer_parts = gather_t(dispatch_z(after(normed_two, out_z, in_weight)), out_weight)
    router = jnp.pad(router_rows.T, ((0, 0), (0, 128 - E)))
    buffer, grad_expert, activation, grad_pre, kept, given = call(
        functools.partial(expert_layer, pieces=len(in_weight)),
        "expert_layer",
        8,
        [
            ((SEQ, D), BF),
            ((SEQ, D), BF),
            ((SEQ, width), BF),
            ((SEQ, width), BF),
            ((2, ROWS, 2 * D), BF),
            ((2, ROWS, 2 * D), BF),
        ],
        [((D, width), BF), ((D, width), BF)],
        place_at,
        *buffer_parts,
        *cotangent_parts,
        router,
        *in_weight,
        *out_weight,
    )


    def expert_gradient(name, left, right):
        (out,) = call(
            weight_gradient,
            name,
            2,
            [((*grads_shape, width), BF)],
            [((D, width), F32)],
            place_at,
            left,
            right,
        )
        return blocks_to_send(out)

    out_terms = expert_gradient("grad_w_out", grad_expert, activation)
    in_terms = expert_gradient("grad_w_in", buffer, grad_pre)
    mine = scatter_t(kept, given).astype(BF)
    out_sums = add(swap_r(out_terms)).astype(BF)
    in_sums = add(swap_r(after(in_terms, out_sums, mine))).astype(BF)
    returned = deliver_z(after(mine, out_sums).reshape(E, SUB, 2 * D))
    returned = jnp.concatenate(returned, axis=0).astype(F32)
    combined, grad_normed_two = returned[:, :D], returned[:, D:]

    experts = jnp.arange(E, dtype=jnp.int32)[None, :]
    route = jax.nn.softmax(mm(normed_two, router_rows, 1, 1), axis=-1)
    chosen = experts == chosen_own[:, None]
    gate = jnp.sum(jnp.where(chosen, route, 0.0), axis=-1)
    layer_rows = (middle + gate[:, None] * combined).astype(BF)
    grad_gate = jnp.sum(grad_output * combined, axis=-1)
    grad_logits = gate[:, None] * (chosen.astype(F32) - route) * grad_gate[:, None]
    grad_router = lax.dot_general(
        grad_logits,
        normed_two.astype(F32),
        (((0,), (0,)), ((), ())),
        precision=HIGHEST_PRECISION,
    )
    grad_normed_two = grad_normed_two + jnp.dot(
        grad_logits, router_rows.astype(F32), precision=HIGHEST_PRECISION
    )
    grad_gain_two = jnp.sum(grad_normed_two * middle * scale_two, axis=0, keepdims=True)
    grad_middle = (grad_output + norm_back(grad_normed_two, middle, scale_two, gain_two)).astype(BF)
    grad_parts = gather_t(grad_middle, in_sums)
    layer_parts = gather_t(after(layer_rows, grad_parts))

    late_terms, kept, given, grad_gain_one, grad_rel = call(
        attention_backward,
        "attention_backward",
        12,
        [
            ((*grads_shape, 4 * LW), BF),
            ((2, ROWS, D), BF),
            ((2, ROWS, D), BF),
            ((1, D), F32),
            ((LH, SPAN), F32),
        ],
        [
            ((SEQ, D), BF),
            ((SEQ, LW), BF),
            ((SEQ, 3 * LW), BF),
            ((SEQ, D), F32),
            ((D, 4 * LW), F32),
        ],
        place_at,
        *grad_parts,
        to_slots,
        attention_weight,
        tokens_all,
        normed_all,
        qkv,
        probs,
        heads_all,
    )
    expert_sums = jnp.stack([in_sums, out_sums], axis=1)
    delivered = deliver_z(after(expert_sums, grad_middle))
    late_terms, kept, given, grad_gain_one, grad_rel = after(
        (late_terms, kept, given, grad_gain_one, grad_rel), layer_parts[1]
    )
    late_terms = blocks_to_send(late_terms)
    far_terms = swap_r(late_terms[:, 2:])
    delivered = after(delivered, far_terms)
    far_sums = add(far_terms).astype(BF)
    near_terms = swap_r(after(late_terms[:, :2], far_sums))
    given = over_t(given, 1)
    grad_normed_one = finish_scatter(kept, given)
    own_inputs = tokens.astype(F32)
    grad_slots = jnp.concatenate(in_order(grad_parts), axis=0)
    grad_tokens = mm(from_slots_own, grad_slots, 1, 0) + norm_back(
        grad_normed_one, own_inputs, norm_scale(own_inputs), gain_one
    )
    layer_slots = jnp.concatenate(in_order(layer_parts), axis=0)
    layer_out = mm(from_slots_own, layer_slots, 1, 0).astype(BF)
    grad_table_rows = lax.dot_general(
        grad_rel[:, : 2 * SEQ - 1],
        bucket_table,
        (((1,), (1,)), ((), ())),
        precision=HIGHEST_PRECISION,
    )
    grad_table = lax.dynamic_update_slice_in_dim(
        jnp.zeros((H, NB), F32), grad_table_rows, t * LH, 0
    ).reshape(1, -1)
    small = sum_but_z(
        jnp.concatenate(
            [
                grad_router,
                grad_gain_two,
                grad_gain_one,
                jnp.pad(grad_table, ((0, 0), (0, D - H * NB))),
                jnp.zeros((1, D), F32),
            ],
            axis=0,
        ),
        far_terms,
        given,
        layer_parts[2],
    )
    low = after(small, delivered).astype(BF)
    far = [over_z(jnp.concatenate([far_sums[d - 2], low], axis=0), d) for d in (2, 3)]
    near_sums = add(after(near_terms, far))
    near = jnp.concatenate([near_sums[1].astype(BF), low], axis=0)
    delivered = after(delivered, near)
    near = over_z(near, 1)
    late = jnp.concatenate([near_sums[0], small], axis=0)
    late = late + far[0].astype(F32) + far[1].astype(F32) + near.astype(F32)
    late, small = late[:local], late[local:]
    small_own = lax.dynamic_slice_in_dim(small[: E + 2], at_dp * local, local, 1)
    table_own = lax.dynamic_slice_in_dim(small[E + 2], at_dp * (H * NB // n), H * NB // n, 0)
    return (
        layer_out,
        grad_tokens,
        late[:, : 3 * LW].reshape(local, 3, LW),
        late[:, 3 * LW :],
        small_own[:E].T,
        jnp.stack(natural([part[0] for part in delivered], z), axis=1).astype(F32),
        jnp.stack(natural([part[1] for part in delivered], z), axis=1).astype(F32),
        small_own[E + 1],
        small_own[E],
        table_own,
    )


def solution(mesh):
    in_specs = (
        P(("dp", "tensor"), None),
        P(("dp", "tensor"), None),
        P("dp", None, "tensor"),
        P("dp", "tensor"),
        P("dp", None),
        P("dp", None, "tensor"),
        P("dp", None, "tensor"),
        P("dp"),
        P("dp"),
        P("dp"),
        P("dp"),
        P("dp"),
        P("dp"),
        P(),
    )
    out_specs = (
        P(("dp", "tensor"), None),
        P(("dp", "tensor"), None),
        P("dp", None, "tensor"),
        P("dp", "tensor"),
        P("dp", None),
        P("dp", None, "tensor"),
        P("dp", None, "tensor"),
        P("dp"),
        P("dp"),
        P("dp"),
    )
    return jax.shard_map(body, mesh=mesh, in_specs=in_specs, out_specs=out_specs, check_vma=False)
```

```python
import functools

import jax
import jax.numpy as jnp
from jax import lax
from jax.experimental import pallas as pl
from jax.experimental.pallas import tpu as pltpu
from jax.sharding import PartitionSpec as P

D = 768
H = 12
HD = 64
NB = 32
E = 4
SEQ = 512
CAP = 128
T = 4
LH = H // T
LW = LH * HD
ROWS = SEQ // T
SUB = CAP // T
SPAN = 2 * SEQ
TILE = 128
TILES = SEQ // TILE

EPSILON = 1e-06
HIGHEST_PRECISION = lax.Precision.HIGHEST
BF = jnp.bfloat16
F32 = jnp.float32


def mm(a, b, ca, cb):
    return lax.dot_general(a, b, (((ca,), (cb,)), ((), ())), preferred_element_type=F32)


def over_t(x, k):
    return lax.ppermute(x, "tensor", [(i, i ^ k) for i in range(T)])


def over_z(x, d):
    n = lax.axis_size("dp")
    r = n // E
    return lax.ppermute(x, "dp", [(i, ((i // r) ^ d) * r + i % r) for i in range(n)])


def over_r(x, c):
    n = lax.axis_size("dp")
    r = n // E
    return lax.ppermute(x, "dp", [(i, (i // r) * r + ((i % r) ^ c)) for i in range(n)])


def natural(parts, index):
    bit = 1
    while bit < len(parts):
        flip = (index & bit) != 0
        parts = [jnp.where(flip, parts[j ^ bit], parts[j]) for j in range(len(parts))]
        bit *= 2
    return parts


def gather_t(x, *earlier):
    far = over_t(x, 2)
    return x, far, over_t(after(jnp.stack([x, far]), *earlier), 1)


def in_order(gathered):
    own, far, near = gathered
    return [own, near[0], far, near[1]]


def scatter_t(kept, sent):
    return finish_scatter(kept, over_t(sent, 1))


def finish_scatter(kept, first):
    first = first.astype(F32)
    away = (kept[1].astype(F32) + first[1]).astype(BF)
    return kept[0].astype(F32) + first[0] + over_t(away, 2).astype(F32)


def pick(x, index, axis):
    return lax.dynamic_index_in_dim(x, index, axis, keepdims=False)


def after(x, *others):
    return lax.optimization_barrier((x, others))[0]


def swap_r(x):
    return [x[0]] + [over_r(x[c], c) for c in range(1, x.shape[0])]


def add(terms):
    return sum(term.astype(F32) for term in terms)


def deliver_z(x):
    return [x[0]] + [over_z(x[d], d) for d in range(1, E)]


def sum_but_z(x, *earlier):
    R = lax.axis_size("dp") // E
    c = 1
    while c < R:
        x = x + over_r(x, c)
        c *= 2
    x = x + over_t(x, 2)
    x = after(x, *earlier)
    return x + over_t(x, 1)


VMEM = pl.BlockSpec(memory_space=pltpu.VMEM)
SMEM = pl.BlockSpec(memory_space=pltpu.SMEM)
ANY = pl.BlockSpec(memory_space=pl.ANY)
PARAMS = pltpu.CompilerParams(vmem_limit_bytes=48 * 2**20)


def call(kernel, name, micros, outs, scratch, at, *operands, unplaced=0):
    moved = sum(a.size * a.dtype.itemsize for a in operands)
    return pl.pallas_call(
        kernel,
        out_shape=[jax.ShapeDtypeStruct(shape, kind) for shape, kind in outs],
        in_specs=[SMEM] + [VMEM] * (len(operands) - unplaced) + [ANY] * unplaced,
        out_specs=[VMEM] * len(outs),
        scratch_shapes=[
            pltpu.SemaphoreType.DMA(shape) if kind is None else pltpu.VMEM(shape, kind)
            for shape, kind in scratch
        ],
        compiler_params=PARAMS,
        cost_estimate=pl.CostEstimate(
            flops=micros * 10**9, bytes_accessed=moved, transcendentals=0
        ),
        name=name,
    )(at, *operands)


def block(index, length):
    return pl.ds(pl.multiple_of(index * length, length), length)


def place_rows(target, own_ref, far_ref, near_ref, t):
    for k, rows in ((0, own_ref[...]), (1, near_ref[0]), (2, far_ref[...]), (3, near_ref[1])):
        at = k if t is None else t ^ k
        target[block(at, ROWS), :] = rows


def place_weight(target, refs, at_ref, local):
    z, r, R = at_ref[0], at_ref[1], len(refs)
    for c in range(R):
        for d in range(E):
            target[block((z ^ d) * R + (r ^ c), local), :] = refs[c][d, :local, :]


def fetch_weight(target, refs, at_ref, sems):
    if len(refs) == 1:
        return [pltpu.make_async_copy(refs[0], target, sems.at[0])]
    z, r, R = at_ref[0], at_ref[1], len(refs)
    local = D // (R * E)
    return [
        pltpu.make_async_copy(
            refs[c].at[d],
            target.at[block((z ^ d) * R + (r ^ c), local), :],
            sems.at[c * E + d],
        )
        for c in range(R)
        for d in range(E)
    ]


def send_rows(source, out_ref, at_ref):
    R, _, local, _ = out_ref.shape
    for c in range(R):
        for d in range(E):
            at = block((at_ref[0] ^ d) * R + (at_ref[1] ^ c), local)
            out_ref[c, d] = source[at, :].astype(BF)


def attention_forward(
    at_ref,
    own_ref,
    far_ref,
    near_ref,
    gain_ref,
    rel_ref,
    slots_ref,
    *rest,
    pieces,
):
    refs, rest = rest[:pieces], rest[pieces:]
    normed_ref, qkv_ref, probs_ref, heads_ref, kept_ref, sent_ref, tokens_ref, weight_ref = rest
    t, length = at_ref[2], at_ref[3]
    if pieces == 1:
        weight_ref[...] = refs[0][...]
    else:
        place_weight(weight_ref, refs, at_ref, D // (pieces * E))
    place_rows(tokens_ref, own_ref, far_ref, near_ref, t)
    inputs = tokens_ref[...].astype(F32)
    normed_ref[...] = (inputs * norm_scale(inputs) * gain_ref[...]).astype(BF)
    qkv_ref[...] = mm(normed_ref[...], weight_ref[:, : 3 * LW], 1, 0).astype(BF)
    live = lax.broadcasted_iota(jnp.int32, (TILE, SEQ), 1) < length
    for h in range(LH):
        key = qkv_ref[:, LW + h * HD : LW + (h + 1) * HD]
        value = qkv_ref[:, 2 * LW + h * HD : 2 * LW + (h + 1) * HD]
        bias = jnp.broadcast_to(rel_ref[h : h + 1, :], (TILE, SPAN))
        for i in range(TILES):
            rows = slice(i * TILE, (i + 1) * TILE)
            query = qkv_ref[rows, h * HD : (h + 1) * HD]
            rolled = pltpu.roll(bias, SEQ + 1 + i * TILE, 1, stride=1, stride_axis=0)[:, :SEQ]
            scores = mm(query, key, 1, 1) * 0.125 + rolled
            scores = jnp.where(live, scores, -1e30)
            exponent = jnp.exp(scores - jnp.max(scores, axis=1, keepdims=True))
            probs = exponent / jnp.sum(exponent, axis=1, keepdims=True)
            probs_ref[h, rows, :] = probs
            heads_ref[rows, h * HD : (h + 1) * HD] = mm(probs.astype(BF), value, 1, 0).astype(BF)
    in_slots = mm(slots_ref[...], heads_ref[...], 1, 0).astype(BF)
    part = mm(in_slots, weight_ref[:, 3 * LW :], 1, 1).astype(BF)
    for k, out in ((0, kept_ref.at[0]), (1, sent_ref.at[0]), (2, kept_ref.at[1]), (3, sent_ref.at[1])):
        out[...] = part[k * ROWS : (k + 1) * ROWS]


def attention_backward(
    at_ref,
    own_ref,
    far_ref,
    near_ref,
    slots_ref,
    weight_ref,
    tokens_ref,
    normed_ref,
    qkv_ref,
    probs_ref,
    heads_ref,
    grads_ref,
    kept_ref,
    sent_ref,
    gain_ref,
    rel_ref,
    slot_scratch,
    heads_scratch,
    qkv_scratch,
    wide_scratch,
    weight_scratch,
):
    t = at_ref[2]
    place_rows(slot_scratch, own_ref, far_ref, near_ref, None)
    attended = mm(slots_ref[...], slot_scratch[...], 0, 0).astype(BF)
    heads_scratch[...] = mm(attended, weight_ref[:, 3 * LW :], 1, 0).astype(BF)
    weight_scratch[:, 3 * LW :] = mm(attended, heads_ref[...], 0, 0)
    flip = (
        lax.broadcasted_iota(jnp.int32, (TILE, TILE), 0)
        + lax.broadcasted_iota(jnp.int32, (TILE, TILE), 1)
        == TILE - 1
    ).astype(BF)
    rel_ref[...] = jnp.zeros_like(rel_ref)
    for h in range(LH):
        key = qkv_ref[:, LW + h * HD : LW + (h + 1) * HD]
        value = qkv_ref[:, 2 * LW + h * HD : 2 * LW + (h + 1) * HD]
        grad_key = jnp.zeros((SEQ, HD), F32)
        grad_value = jnp.zeros((SEQ, HD), F32)
        diagonal = [None] * (2 * TILES - 1)
        for i in range(TILES):
            rows = slice(i * TILE, (i + 1) * TILE)
            query = qkv_ref[rows, h * HD : (h + 1) * HD]
            grad = heads_scratch[rows, h * HD : (h + 1) * HD]
            probs = probs_ref[h, rows, :]
            grad_probs = mm(grad, value, 1, 1)
            inner = jnp.sum(probs * grad_probs, axis=1, keepdims=True)
            low = (probs * (grad_probs - inner)).astype(BF)
            qkv_scratch[rows, h * HD : (h + 1) * HD] = (mm(low, key, 1, 0) * 0.125).astype(BF)
            grad_key = grad_key + mm(low, query, 0, 0)
            grad_value = grad_value + mm(probs.astype(BF), grad, 0, 0)
            for j in range(TILES):
                turned = mm(low[:, j * TILE : (j + 1) * TILE], flip, 1, 0)
                at = i - j + TILES - 1
                diagonal[at] = turned if diagonal[at] is None else diagonal[at] + turned
        qkv_scratch[:, LW + h * HD : LW + (h + 1) * HD] = (grad_key * 0.125).astype(BF)
        qkv_scratch[:, 2 * LW + h * HD : 2 * LW + (h + 1) * HD] = grad_value.astype(BF)
        for at, part in enumerate(diagonal):
            wide = jnp.concatenate([part, jnp.zeros((TILE, TILE), F32)], axis=1)
            line = jnp.sum(pltpu.roll(wide, 0, 1, stride=1, stride_axis=0), axis=0, keepdims=True)
            rel_ref[h : h + 1, at * TILE : (at + 2) * TILE] += line
    weight_scratch[:, : 3 * LW] = mm(normed_ref[...], qkv_scratch[...], 0, 0)
    if len(grads_ref.shape) == 4:
        send_rows(weight_scratch, grads_ref, at_ref)
    else:
        grads_ref[...] = weight_scratch[...].astype(BF)
    wide_scratch[...] = mm(qkv_scratch[...], weight_ref[:, : 3 * LW], 1, 1)
    inputs = tokens_ref[...].astype(F32)
    gain_ref[...] = jnp.sum(
        wide_scratch[...] * inputs * norm_scale(inputs), axis=0, keepdims=True
    )
    for k, out in ((0, kept_ref.at[0]), (1, sent_ref.at[0]), (2, kept_ref.at[1]), (3, sent_ref.at[1])):
        out[...] = wide_scratch[block(t ^ k, ROWS), :].astype(BF)


def expert_layer(
    at_ref,
    own_ref,
    far_ref,
    near_ref,
    own_grad_ref,
    far_grad_ref,
    near_grad_ref,
    router_ref,
    *rest,
    pieces,
):
    in_refs, out_refs, rest = rest[:pieces], rest[pieces : 2 * pieces], rest[2 * pieces :]
    buffer_ref, grad_ref, activation_ref, grad_pre_ref, kept_ref, sent_ref, *rest = rest
    in_ref, out_ref, in_sems, out_sems = rest
    in_copies = fetch_weight(in_ref, in_refs, at_ref, in_sems)
    out_copies = fetch_weight(out_ref, out_refs, at_ref, out_sems)
    for copy in in_copies + out_copies:
        copy.start()
    place_rows(buffer_ref, own_ref, far_ref, near_ref, None)
    place_rows(grad_ref, own_grad_ref, far_grad_ref, near_grad_ref, None)
    logits = mm(buffer_ref[...], router_ref[...], 1, 0)
    lane = lax.broadcasted_iota(jnp.int32, logits.shape, 1)
    logits = jnp.where(lane < E, logits, -1e30)
    exponent = jnp.exp(logits - jnp.max(logits, axis=1, keepdims=True))
    mine = jnp.sum(jnp.where(lane == at_ref[0], exponent, 0.0), axis=1, keepdims=True)
    gate = mine / jnp.sum(exponent, axis=1, keepdims=True)
    grad_ref[...] = (gate * grad_ref[...].astype(F32)).astype(BF)
    for copy in in_copies:
        copy.wait()
    pre = mm(buffer_ref[...], in_ref[...], 1, 0)
    square = pre * pre
    tanh = jnp.tanh(0.7978845608028654 * (pre + 0.044715 * pre * square))
    half = 0.5 * (1.0 + tanh)
    activation_ref[...] = (pre * half).astype(BF)
    slope = half + 0.5 * pre * (1.0 - tanh * tanh) * (
        0.7978845608028654 * (1.0 + 3.0 * 0.044715 * square)
    )
    for copy in out_copies:
        copy.wait()
    grad_act = mm(grad_ref[...], out_ref[...], 1, 0)
    grad_pre_ref[...] = (grad_act * slope).astype(BF)
    for k, out in ((0, kept_ref.at[0]), (1, sent_ref.at[0]), (2, kept_ref.at[1]), (3, sent_ref.at[1])):
        rows = slice(k * ROWS, (k + 1) * ROWS)
        out[:, :D] = mm(activation_ref[rows, :], out_ref[...], 1, 1).astype(BF)
        out[:, D:] = mm(grad_pre_ref[rows, :], in_ref[...], 1, 1).astype(BF)


def weight_gradient(at_ref, left_ref, right_ref, out_ref, scratch):
    scratch[...] = mm(left_ref[...], right_ref[...], 0, 0)
    if len(out_ref.shape) == 4:
        send_rows(scratch, out_ref, at_ref)
    else:
        out_ref[...] = scratch[...].astype(BF)


def norm_scale(values):
    return lax.rsqrt(jnp.mean(values * values, axis=-1, keepdims=True) + EPSILON)


def norm_back(grad, values, scale, gain):
    u = grad * gain
    inner = jnp.mean(u * values, axis=-1, keepdims=True)
    return scale * u - scale * scale * scale * values * inner


def body(
    tokens,
    cotangent,
    w_qkv,
    w_out_attn,
    w_router,
    w_in,
    w_out,
    norm1_gain,
    norm2_gain,
    bias_table,
    seq_length,
    expert_ids,
    expert_slots,
    buckets,
):
    n = lax.axis_size("dp")
    R = n // E
    at_dp = lax.axis_index("dp")
    z, r = at_dp // R, at_dp % R
    t = lax.axis_index("tensor")
    local = D // n
    width = w_in.shape[2]
    aligned = local % 16 == 0
    place_at = jnp.stack([z, r, t, seq_length[0]]).astype(jnp.int32)

    def whole(parts):
        if aligned:
            return [jnp.stack(part) if isinstance(part, list) else part for part in parts]
        rows = [jnp.stack(natural(list(part), z)) for part in parts]
        return [jnp.stack(natural(rows, r), axis=1).reshape(D, -1)]

    def blocks_to_send(grad):
        if aligned:
            return grad
        x = grad.reshape(E, R, local, -1)
        x = jnp.stack([pick(x, r ^ c, 1) for c in range(R)])
        return jnp.stack([pick(x, z ^ d, 1) for d in range(E)], axis=1)

    grads_shape = (R, E, local) if aligned else (D,)

    line = jnp.concatenate([w_router.T.reshape(-1), norm1_gain, norm2_gain, bias_table])
    line = jnp.pad(line, (0, 4 * LW - line.shape[0]))[None]
    packed = jnp.concatenate(
        [jnp.concatenate([w_qkv.reshape(local, 3 * LW), w_out_attn], axis=1), line], axis=0
    )
    packed_z = [packed] + [over_z(packed, d) for d in range(1, E)]
    packed_r = [
        [over_r(packed, c), *over_r(jnp.stack([part[:local] for part in packed_z[1:]]), c)]
        for c in range(1, R)
    ]
    packed_all = [[part[:local] for part in parts] for parts in [packed_z] + packed_r]
    lines = jnp.stack(natural([part[local] for part in packed_z], z))
    lines = [lines] + [over_r(lines, c) for c in range(1, R)]
    lines = jnp.stack(natural(lines, r), axis=1).reshape(n, -1)
    router_rows = lines[:, : local * E].reshape(n, E, local).transpose(1, 0, 2).reshape(E, D)
    gain_one = lines[:, local * E : local * (E + 1)].reshape(1, D).astype(F32)
    gain_two = lines[:, local * (E + 1) : local * (E + 2)].reshape(1, D).astype(F32)
    table_flat = lines[:, local * (E + 2) : local * (E + 2) + H * NB // n].reshape(-1)

    both_parts = gather_t(jnp.concatenate([tokens, cotangent], axis=1))
    token_parts = [part[..., :D] for part in both_parts]
    cotangent_all = jnp.concatenate(natural([p[:, D:] for p in in_order(both_parts)], t), axis=0)

    sent = expert_slots >= 0
    absolute = jnp.where(sent, expert_ids * CAP + expert_slots, -1)
    position = jnp.arange(SEQ, dtype=jnp.int32)
    empty = ~jnp.any(absolute[None, :] == position[:, None], axis=1)
    before = position[None, :] <= position[:, None]
    empty_rank = jnp.sum((before & empty[None, :]).astype(jnp.int32), axis=1)
    unsent_rank = jnp.sum((before & ~sent[None, :]).astype(jnp.int32), axis=1)
    match = empty[None, :] & (empty_rank[None, :] == unsent_rank[:, None])
    spare = jnp.sum(jnp.where(match, position[None, :], 0), axis=1)
    slot = jnp.where(sent, absolute, spare)
    in_expert = slot % CAP
    place = ((in_expert // SUB) ^ t) * ROWS + ((slot // CAP) ^ z) * SUB + in_expert % SUB
    to_slots_mask = place[None, :] == position[:, None]
    to_slots = to_slots_mask.astype(BF)
    own_mask = to_slots_mask[:ROWS]
    sent_own = jnp.any(own_mask & sent[None, :], axis=1)
    chosen_own = jnp.sum(jnp.where(own_mask, expert_ids[None, :], 0), axis=1)
    own_tokens = lax.dynamic_slice_in_dim(place, t * ROWS, ROWS, 0)
    from_slots_own = (own_tokens[:, None] == position[None, :]).astype(BF)

    def dispatch_z(rows):
        rows = jnp.where(sent_own[:, None], rows, 0).astype(BF)
        return jnp.concatenate(deliver_z(rows.reshape(E, SUB, D)), axis=0)

    grad_output = mm(to_slots[:ROWS], cotangent_all, 1, 0)
    masked = jnp.where(sent_own[:, None], grad_output, 0).astype(BF).reshape(E, SUB, D)
    in_rows = after(w_in, packed_z)
    in_columns = jnp.stack(deliver_z(jnp.stack([pick(in_rows, z ^ d, 1) for d in range(E)])))
    out_rows = after(w_out, in_columns)
    out_rows = jnp.stack([pick(out_rows, z ^ d, 1) for d in range(E)])
    out_z = jnp.stack(deliver_z(jnp.concatenate([out_rows, masked], axis=1)))
    out_columns, cotangent_z = out_z[:, :local], out_z[:, local:].reshape(E * SUB, D)
    in_weight = whole([in_columns] + [over_r(in_columns, c) for c in range(1, R)])
    out_weight = whole([out_columns] + [over_r(out_columns, c) for c in range(1, R)])
    cotangent_parts = gather_t(cotangent_z)

    table_rows = lax.dynamic_slice_in_dim(table_flat.astype(F32).reshape(H, NB), t * LH, LH, 0)
    bucket_table = (buckets[None, :] == jnp.arange(NB, dtype=jnp.int32)[:, None]).astype(F32)
    reversed_rel = jnp.dot(
        table_rows,
        jnp.pad(bucket_table[:, ::-1], ((0, 0), (0, 1))),
        precision=HIGHEST_PRECISION,
    )
    packed_refs = whole(packed_all)
    forward = call(
        functools.partial(attention_forward, pieces=len(packed_refs)),
        "attention_forward",
        12,
        [
            ((SEQ, D), BF),
            ((SEQ, 3 * LW), BF),
            ((LH, SEQ, SEQ), F32),
            ((SEQ, LW), BF),
            ((2, ROWS, D), BF),
            ((2, ROWS, D), BF),
            ((SEQ, D), BF),
            ((D, 4 * LW), BF),
        ],
        [],
        place_at,
        *token_parts,
        gain_one,
        reversed_rel,
        after(to_slots, in_columns),
        *packed_refs,
    )
    normed_all, qkv, probs, heads_all, kept, given, tokens_all, attention_weight = forward
    attended = scatter_t(kept, given)
    inputs = mm(to_slots[:ROWS], tokens_all, 1, 0)
    middle = inputs + attended
    scale_two = norm_scale(middle)
    normed_two = (middle * scale_two * gain_two).astype(BF)

    buffer_parts = gather_t(dispatch_z(after(normed_two, out_z, in_weight)), out_weight)
    router = jnp.pad(router_rows.T, ((0, 0), (0, 128 - E)))
    buffer, grad_expert, activation, grad_pre, kept, given = call(
        functools.partial(expert_layer, pieces=len(in_weight)),
        "expert_layer",
        8,
        [
            ((SEQ, D), BF),
            ((SEQ, D), BF),
            ((SEQ, width), BF),
            ((SEQ, width), BF),
            ((2, ROWS, 2 * D), BF),
            ((2, ROWS, 2 * D), BF),
        ],
        [
            ((D, width), BF),
            ((D, width), BF),
            ((E * len(in_weight),), None),
            ((E * len(in_weight),), None),
        ],
        place_at,
        *buffer_parts,
        *cotangent_parts,
        router,
        *in_weight,
        *out_weight,
        unplaced=2 * len(in_weight),
    )


    def expert_gradient(name, left, right):
        (out,) = call(
            weight_gradient,
            name,
            2,
            [((*grads_shape, width), BF)],
            [((D, width), F32)],
            place_at,
            left,
            right,
        )
        return blocks_to_send(out)

    out_terms = expert_gradient("grad_w_out", grad_expert, activation)
    in_terms = expert_gradient("grad_w_in", buffer, grad_pre)
    mine = scatter_t(kept, given).astype(BF)
    out_sums = add(swap_r(out_terms)).astype(BF)
    in_sums = add(swap_r(after(in_terms, out_sums, mine))).astype(BF)
    returned = deliver_z(after(mine, out_sums).reshape(E, SUB, 2 * D))
    returned = jnp.concatenate(returned, axis=0).astype(F32)
    combined, grad_normed_two = returned[:, :D], returned[:, D:]

    experts = jnp.arange(E, dtype=jnp.int32)[None, :]
    route = jax.nn.softmax(mm(normed_two, router_rows, 1, 1), axis=-1)
    chosen = experts == chosen_own[:, None]
    gate = jnp.sum(jnp.where(chosen, route, 0.0), axis=-1)
    layer_rows = (middle + gate[:, None] * combined).astype(BF)
    grad_gate = jnp.sum(grad_output * combined, axis=-1)
    grad_logits = gate[:, None] * (chosen.astype(F32) - route) * grad_gate[:, None]
    grad_router = lax.dot_general(
        grad_logits,
        normed_two.astype(F32),
        (((0,), (0,)), ((), ())),
        precision=HIGHEST_PRECISION,
    )
    grad_normed_two = grad_normed_two + jnp.dot(
        grad_logits, router_rows.astype(F32), precision=HIGHEST_PRECISION
    )
    grad_gain_two = jnp.sum(grad_normed_two * middle * scale_two, axis=0, keepdims=True)
    grad_middle = (grad_output + norm_back(grad_normed_two, middle, scale_two, gain_two)).astype(BF)
    grad_parts = gather_t(grad_middle, in_sums)
    layer_parts = gather_t(after(layer_rows, grad_parts))

    late_terms, kept, given, grad_gain_one, grad_rel = call(
        attention_backward,
        "attention_backward",
        12,
        [
            ((*grads_shape, 4 * LW), BF),
            ((2, ROWS, D), BF),
            ((2, ROWS, D), BF),
            ((1, D), F32),
            ((LH, SPAN), F32),
        ],
        [
            ((SEQ, D), BF),
            ((SEQ, LW), BF),
            ((SEQ, 3 * LW), BF),
            ((SEQ, D), F32),
            ((D, 4 * LW), F32),
        ],
        place_at,
        *grad_parts,
        to_slots,
        attention_weight,
        tokens_all,
        normed_all,
        qkv,
        probs,
        heads_all,
    )
    expert_sums = jnp.stack([in_sums, out_sums], axis=1)
    delivered = deliver_z(after(expert_sums, grad_middle))
    late_terms, kept, given, grad_gain_one, grad_rel = after(
        (late_terms, kept, given, grad_gain_one, grad_rel), layer_parts[1]
    )
    late_terms = blocks_to_send(late_terms)
    far_terms = swap_r(late_terms[:, 2:])
    delivered = after(delivered, far_terms)
    far_sums = add(far_terms).astype(BF)
    near_terms = swap_r(after(late_terms[:, :2], far_sums))
    given = over_t(given, 1)
    grad_normed_one = finish_scatter(kept, given)
    own_inputs = tokens.astype(F32)
    grad_slots = jnp.concatenate(in_order(grad_parts), axis=0)
    grad_tokens = mm(from_slots_own, grad_slots, 1, 0) + norm_back(
        grad_normed_one, own_inputs, norm_scale(own_inputs), gain_one
    )
    layer_slots = jnp.concatenate(in_order(layer_parts), axis=0)
    layer_out = mm(from_slots_own, layer_slots, 1, 0).astype(BF)
    grad_table_rows = lax.dot_general(
        grad_rel[:, : 2 * SEQ - 1],
        bucket_table,
        (((1,), (1,)), ((), ())),
        precision=HIGHEST_PRECISION,
    )
    grad_table = lax.dynamic_update_slice_in_dim(
        jnp.zeros((H, NB), F32), grad_table_rows, t * LH, 0
    ).reshape(1, -1)
    small = sum_but_z(
        jnp.concatenate(
            [
                grad_router,
                grad_gain_two,
                grad_gain_one,
                jnp.pad(grad_table, ((0, 0), (0, D - H * NB))),
                jnp.zeros((1, D), F32),
            ],
            axis=0,
        ),
        far_terms,
        given,
        layer_parts[2],
    )
    low = after(small, delivered).astype(BF)
    far = [over_z(jnp.concatenate([far_sums[d - 2], low], axis=0), d) for d in (2, 3)]
    near_sums = add(after(near_terms, far))
    near = jnp.concatenate([near_sums[1].astype(BF), low], axis=0)
    delivered = after(delivered, near)
    near = over_z(near, 1)
    late = jnp.concatenate([near_sums[0], small], axis=0)
    late = late + far[0].astype(F32) + far[1].astype(F32) + near.astype(F32)
    late, small = late[:local], late[local:]
    small_own = lax.dynamic_slice_in_dim(small[: E + 2], at_dp * local, local, 1)
    table_own = lax.dynamic_slice_in_dim(small[E + 2], at_dp * (H * NB // n), H * NB // n, 0)
    return (
        layer_out,
        grad_tokens,
        late[:, : 3 * LW].reshape(local, 3, LW),
        late[:, 3 * LW :],
        small_own[:E].T,
        jnp.stack(natural([part[0] for part in delivered], z), axis=1).astype(F32),
        jnp.stack(natural([part[1] for part in delivered], z), axis=1).astype(F32),
        small_own[E + 1],
        small_own[E],
        table_own,
    )


def solution(mesh):
    in_specs = (
        P(("dp", "tensor"), None),
        P(("dp", "tensor"), None),
        P("dp", None, "tensor"),
        P("dp", "tensor"),
        P("dp", None),
        P("dp", None, "tensor"),
        P("dp", None, "tensor"),
        P("dp"),
        P("dp"),
        P("dp"),
        P("dp"),
        P("dp"),
        P("dp"),
        P(),
    )
    out_specs = (
        P(("dp", "tensor"), None),
        P(("dp", "tensor"), None),
        P("dp", None, "tensor"),
        P("dp", "tensor"),
        P("dp", None),
        P("dp", None, "tensor"),
        P("dp", None, "tensor"),
        P("dp"),
        P("dp"),
        P("dp"),
    )
    return jax.shard_map(body, mesh=mesh, in_specs=in_specs, out_specs=out_specs, check_vma=False)
```
